512 devices in a mesh: tm: 64 (over z, x), sta: 8 (over y, core).
Axes of the slice: x: 4, y: 4, z: 16, core: 2. Of those that a mesh axis runs over, the one named last changes fastest.
Arguments:
- record: bfloat16 [3, 32, 65536], P(None, 'sta', 'tm'), may hold values from -36 to 36
- templates: bfloat16 [512, 3, 4, 1536], P(('tm', 'sta')), may hold values from -18 to 18
- template_groups: int32 [512, 3], replicated, may hold values from 0 to 7, all different within a row; in each aligned block of 8 rows (0 to 7, 8 to 15, ...) at most 4 rows name the same one
Outputs:
- detection: float32 [512, 65536], P('sta', 'tm')
The draws below stay inside these ranges and needn't reach their ends.
Inputs may be any that keep to these rules, and one draw needn't show every extreme that they name: `template_groups`: each row names 3 different station groups. Among the 8 templates of one index of tm (rows m * 8 to m * 8 + 7) no group is named by more than 4 rows, a bound that some block reaches.
All inputs are finite; a program needn't handle non-finite values.
Results may differ from the reference program's by a relative error of at most 0.0003.
Values may be sent and summed in bfloat16 or wider, within the bound.
No kernel may reach another device: no remote copies, remote signals or barrier semaphores. Data moves between devices by JAX's collectives and lax.ppermute only.
A program may use at most 64 MiB of HBM per device.

```python
import math
import jax
import jax.numpy as jnp
import numpy as np
from jax import lax

L = 512
STA_DEV = 4
TOPG = 3
MOST = 4
K = 512
STATIONS = 32
TIME = 65536
N_TM = 64
N_STA = 8


def log_spread(key, shape, lowest, highest):
    return jnp.exp(jax.random.uniform(key, shape, jnp.float32, math.log(lowest), math.log(highest)))


def draw_record(key, part):
    key = jax.random.fold_in(key, 11)
    base_key, station_key, time_key = jax.random.split(key, 3)
    shape = (3, STATIONS, TIME)
    base = jnp.clip(jax.random.normal(base_key, shape, jnp.float32), -6.0, 6.0)
    station_gain = log_spread(station_key, (1, STATIONS, 1), 0.5, 2.0)
    envelope = log_spread(time_key, (1, STATIONS, TIME // 32), 0.3, 3.0)
    envelope = jnp.repeat(envelope, 32, axis=2)
    return (base * station_gain * envelope).astype(jnp.bfloat16)


def draw_templates(key, part):
    key = jax.random.fold_in(key, 23)
    base_key, gain_key = jax.random.split(key)
    shape = (K, TOPG, STA_DEV, 3 * L)
    base = jnp.clip(jax.random.normal(base_key, shape, jnp.float32), -6.0, 6.0)
    slot_gain = log_spread(gain_key, (K, TOPG, STA_DEV, 1), 0.3, 3.0)
    return (base * slot_gain).astype(jnp.bfloat16)


def assign_block(key, own, number, rows, amount, top, most, skew):
    sequence = jax.random.permutation(key, amount)
    packed, usual = portions_of(amount, rows * top, most, skew, True), portions_of(amount, rows * top, most, skew, False)
    places = jnp.arange(amount)

    def named(lengths, rotation):
        used = int((lengths > 0).sum())
        fixed = max(1, used // 4)
        passed = fixed + (places - fixed + rotation * (used - fixed)) % max(1, amount - fixed)
        return jnp.zeros((amount,), jnp.int32).at[sequence[jnp.where(places < fixed, places, passed)]].set(jnp.asarray(lengths, jnp.int32))

    lengths = jnp.where(number % 4 == 0, named(packed, number // 4), named(usual, number - number // 4 - 1))
    mixed = jax.random.permutation(jax.random.fold_in(own, 3), amount)
    giver, receiver = mixed[0:amount // 2 * 2:2], mixed[1:amount // 2 * 2:2]
    slack = jnp.minimum(lengths[giver] - 1, most - lengths[receiver]) // 2
    slack = jnp.where((giver == sequence[0]) | (receiver == sequence[0]) | (lengths[receiver] == 0), 0, jnp.maximum(slack, 0))
    passed = jax.random.randint(jax.random.fold_in(own, 4), (amount // 2,), 0, 1 << 20) % (slack + 1)
    lengths = lengths.at[giver].add(-passed).at[receiver].add(passed)
    items = jnp.searchsorted(jnp.cumsum(lengths), jnp.arange(rows * top), side="right").astype(jnp.int32)
    grid = items.reshape(top, rows).T
    grid = grid[jax.random.permutation(jax.random.fold_in(own, 1), rows)]
    rotation = jax.random.randint(jax.random.fold_in(own, 2), (rows, 1), 0, top)
    return jnp.take_along_axis(grid, (jnp.arange(top)[None, :] + rotation) % top, axis=1)


def portions_of(amount, total, reach, slope, full):
    loads = [(1 << 20) // math.isqrt(rank ** slope) + 1 for rank in range(1, amount + 1)]
    largest = reach if full else min(reach, max(-(-total // amount), total * loads[0] // sum(loads)))
    least = 1 if total - largest >= amount - 1 else 0
    counts, surplus = [largest] + [least] * (amount - 1), total - largest - least * (amount - 1)
    while surplus > 0:
        free = [i for i in range(1, amount) if counts[i] < largest] or [i for i in range(1, amount) if counts[i] < reach]
        mass, remaining = sum([loads[i] for i in free]), surplus
        for i in free:
            addition = min(reach - counts[i], max(1, remaining * loads[i] // mass), surplus)
            counts[i] = counts[i] + addition
            surplus = surplus - addition
    return np.array(counts)


def setup_inputs(seed: int = 0) -> dict:
    key_of = jax.random.split(jax.random.key(seed), 4)
    record = draw_record(jax.random.fold_in(key_of[3], 71), 0)
    templates = draw_templates(jax.random.fold_in(key_of[3], 71), 0)
    template_groups_keys = jax.random.split(jax.random.fold_in(key_of[2], 1), K // N_STA)
    template_groups_turns = jax.random.permutation(jax.random.fold_in(key_of[2], 3), K // N_STA)
    template_groups = jax.vmap(lambda own, number: assign_block(jax.random.fold_in(key_of[2], 2), own, number, N_STA, N_STA, TOPG, MOST, 2))(template_groups_keys, template_groups_turns).reshape((K, TOPG))
    return dict(record=record, templates=templates, template_groups=template_groups)


epsilon = 1e-06

def hankel_rows(series, columns):
    length = series.shape[-1]
    leading = series.shape[:-1]
    tiled = jnp.broadcast_to(series[..., None, :], leading + (L + 1, length))
    tiled = tiled.reshape(leading + ((L + 1) * length,))
    tiled = tiled[..., :L * (length + 1)].reshape(leading + (L, length + 1))
    return tiled[..., :columns]

def reference(record, templates, template_groups):
    channels = record.shape[0]
    extended = jnp.pad(record.astype(jnp.float32), ((0, 0), (0, 0), (0, L - 1)))
    weights = templates.astype(jnp.float32)
    capacity = N_TM * MOST

    def group_term(summed, group_index):
        hits = template_groups == group_index
        member = jnp.any(hits, axis=1)
        chosen = jnp.nonzero(member, size=capacity, fill_value=0)[0].astype(jnp.int32)
        used = (jnp.arange(capacity) < jnp.sum(member.astype(jnp.int32))).astype(jnp.float32)
        blocks = jnp.einsum('ki,kisd->ksd', hits.astype(jnp.float32), weights)
        picked = blocks[chosen] * used[:, None, None]

        def station_term(station, correlation):
            series = lax.dynamic_index_in_dim(extended, group_index * STA_DEV + station, 1, keepdims=False)
            windows = hankel_rows(series, TIME).reshape(channels * L, TIME)
            data_norm = jnp.sqrt(lax.optimization_barrier(jnp.sum(windows * windows, axis=0)) + epsilon)
            slot_rows = lax.dynamic_index_in_dim(picked, station, 1, keepdims=False)
            template_norm = jnp.sqrt(lax.optimization_barrier(jnp.sum(slot_rows * slot_rows, axis=1)) + epsilon)
            numerator = jnp.dot(slot_rows, windows, precision=lax.Precision.HIGHEST)
            return correlation + numerator / template_norm[:, None] / data_norm[None, :]
        correlation = lax.fori_loop(0, STA_DEV, station_term, jnp.zeros((capacity, TIME), jnp.float32))
        return (summed.at[chosen].add(correlation * used[:, None]), None)
    network_sum, _ = lax.scan(group_term, jnp.zeros((K, TIME), jnp.float32), jnp.arange(N_STA))
    return network_sum * math.sqrt(channels * L / (TOPG * STA_DEV))
```

```python
import math

import jax
import jax.numpy as jnp
from jax import lax
from jax.experimental import pallas as pl
from jax.experimental.pallas import tpu as pltpu
from jax.sharding import PartitionSpec as P

L = 512
LANES = 128
HALF = 64
SPAN = L + LANES
SLOTS = 4
epsilon = 1e-06


def detect_kernel(
    factor,
    groups_ref,
    templates_ref,
    series_ref,
    out_ref,
    source,
    home,
    count,
    waves,
    norms,
    band,
    shifts,
    energy,
    windows,
    toeplitz,
    share,
    total,
    turned,
):
    group = pl.program_id(0)
    block, spread = groups_ref.shape
    stations = series_ref.shape[1] // 3
    padded = series_ref.shape[2]
    rows = total.shape[1]
    slots = templates_ref.shape[0]
    lane = lax.broadcasted_iota(jnp.int32, (1, LANES), 1)
    low = lane < HALF

    @pl.when(group == 0)
    def _():
        def clear(n, carry):
            source[n] = block * spread
            home[n] = block
            return carry

        lax.fori_loop(0, source.shape[0], clear, 0)
        for n in range(count.shape[0]):
            count[n] = 0
        for r in range(block):
            for i in range(spread):
                named = groups_ref[r, i]
                place = named * SLOTS + count[named]
                source[place] = r * spread + i
                home[place] = r
                count[named] = count[named] + 1
        waves[...] = jnp.zeros_like(waves)
        norms[...] = jnp.zeros_like(norms)
        squares = jnp.zeros((slots, 1), jnp.float32)
        for c in range(3):
            part = templates_ref[:, c * L : (c + 1) * L].astype(jnp.float32)
            waves[0:slots, c * SPAN : c * SPAN + L] = part
            squares = squares + jnp.sum(part * part, axis=1, keepdims=True)
        norms[0:slots, :] = jnp.broadcast_to(lax.rsqrt(squares + epsilon), (slots, LANES))
        r = lax.broadcasted_iota(jnp.int32, (LANES, LANES), 0)
        l = lax.broadcasted_iota(jnp.int32, (LANES, LANES), 1)
        band[0:LANES, :] = jnp.where(r >= l, 1.0, 0.0).astype(jnp.bfloat16)
        band[LANES : 2 * LANES, :] = jnp.ones((LANES, LANES), jnp.bfloat16)
        band[2 * LANES :, :] = jnp.where(r < l, 1.0, 0.0).astype(jnp.bfloat16)
        shifts[...] = jnp.zeros_like(shifts)
        total[...] = jnp.zeros_like(total)

    share[...] = jnp.zeros_like(share)

    def station_term(station, carry):
        squares = jnp.zeros((padded, LANES), jnp.float32)
        for c in range(3):
            plain = series_ref[0, c * stations + station].astype(jnp.float32)
            squares = squares + plain * plain
            shifts[c, 0, 0:padded, :] = plain
            after = shifts[c, 0, 1 : padded + 1, :]
            shifts[c, 1, 0:padded, :] = pltpu.roll(jnp.where(low, after, plain), HALF, 1)
        energy[...] = squares
        middle = energy[1 : rows + 1, :] + energy[2 : rows + 2, :] + energy[3 : rows + 3, :]
        pieces = jnp.concatenate([energy[0:rows, :], middle, energy[4 : rows + 4, :]], axis=1)
        coarse = pieces.astype(jnp.bfloat16)
        fine = (pieces - coarse.astype(jnp.float32)).astype(jnp.bfloat16)
        window_energy = jnp.dot(coarse, band[...], preferred_element_type=jnp.float32)
        window_energy += jnp.dot(fine, band[...], preferred_element_type=jnp.float32)
        scale = lax.rsqrt(window_energy + epsilon)
        scale_other = pltpu.roll(scale, HALF, 1)
        scale_first = jnp.where(low, scale, scale_other)
        scale_second = jnp.where(low, scale_other, scale)

        weight = []
        for j in range(SLOTS):
            row = source[group * SLOTS + j] * stations + station
            weight.append(norms[pl.ds(row, 1), :])
            for c in range(3):
                wave = waves[pl.ds(row, 1), c * SPAN : (c + 1) * SPAN]
                moved = pltpu.roll(
                    jnp.broadcast_to(wave, (HALF, SPAN)), 0, 1, stride=1, stride_axis=0
                )
                toeplitz[j * HALF : (j + 1) * HALF, c * SPAN : (c + 1) * SPAN] = moved.astype(
                    jnp.bfloat16
                )
        for c in range(3):
            for e in range(2):
                for v in range(SPAN // LANES):
                    at = c * SPAN + v * LANES
                    windows[e * rows : (e + 1) * rows, at : at + LANES] = shifts[
                        c, e, v : v + rows, :
                    ].astype(jnp.bfloat16)
        product = lax.dot_general(
            windows[...],
            toeplitz[...],
            (((1,), (1,)), ((), ())),
            preferred_element_type=jnp.float32,
        )
        for p in range(SLOTS // 2):
            both = jnp.where(low, weight[2 * p], weight[2 * p + 1])
            at = p * LANES
            share[0, :, at : at + LANES] += product[0:rows, at : at + LANES] * (scale_first * both)
            share[1, :, at : at + LANES] += product[rows:, at : at + LANES] * (scale_second * both)
        return carry

    lax.fori_loop(0, stations, station_term, 0)
    for j in range(SLOTS):
        at = (j // 2) * LANES
        first = share[0, :, at : at + LANES]
        second = share[1, :, at : at + LANES]
        if j % 2 == 0:
            whole = jnp.where(low, first, pltpu.roll(second, HALF, 1))
        else:
            whole = jnp.where(low, pltpu.roll(first, HALF, 1), second)
        r = home[group * SLOTS + j]
        total[r] = total[r] + whole

    @pl.when(group == pl.num_programs(0) - 1)
    def _():
        for r in range(block):
            turned[:, r, :] = total[r] * factor
        parts, _, samples = out_ref.shape
        for w in range(parts):
            for i in range(samples // LANES):
                out_ref[w, :, i * LANES : (i + 1) * LANES] = turned[w * (samples // LANES) + i]


def detect(groups, templates, series, parts, factor):
    n_group, channels, padded, _ = series.shape
    block, spread = groups.shape
    slots = templates.shape[0]
    rows = padded - 8
    samples = rows * LANES // parts
    spare = -(-(slots + 4) // 8) * 8
    body = lambda *refs: detect_kernel(factor, *refs)
    return pl.pallas_call(
        body,
        grid=(n_group,),
        out_shape=jax.ShapeDtypeStruct((parts, block, samples), jnp.float32),
        in_specs=[
            pl.BlockSpec(memory_space=pltpu.SMEM),
            pl.BlockSpec((slots, 3 * L), lambda g: (0, 0)),
            pl.BlockSpec((1, channels, padded, LANES), lambda g: (g, 0, 0, 0)),
        ],
        out_specs=pl.BlockSpec((parts, block, samples), lambda g: (0, 0, 0)),
        scratch_shapes=[
            pltpu.SMEM((n_group * SLOTS,), jnp.int32),
            pltpu.SMEM((n_group * SLOTS,), jnp.int32),
            pltpu.SMEM((n_group,), jnp.int32),
            pltpu.VMEM((spare, 3 * SPAN), jnp.float32),
            pltpu.VMEM((spare, LANES), jnp.float32),
            pltpu.VMEM((3 * LANES, LANES), jnp.bfloat16),
            pltpu.VMEM((3, 2, padded + 8, LANES), jnp.float32),
            pltpu.VMEM((padded, LANES), jnp.float32),
            pltpu.VMEM((2 * rows, 3 * SPAN), jnp.bfloat16),
            pltpu.VMEM((SLOTS * HALF, 3 * SPAN), jnp.bfloat16),
            pltpu.VMEM((2, rows, SLOTS * HALF), jnp.float32),
            pltpu.VMEM((block + 1, rows, LANES), jnp.float32),
            pltpu.VMEM((rows, block, LANES), jnp.float32),
        ],
        compiler_params=pltpu.CompilerParams(vmem_limit_bytes=32 * 1024 * 1024),
        cost_estimate=pl.CostEstimate(
            flops=2 * n_group * 4 * 2 * rows * 3 * SPAN * SLOTS * HALF,
            bytes_accessed=series.size * 2 + templates.size * 2 + 4 * block * rows * LANES,
            transcendentals=0,
        ),
    )(groups, templates, series)


def copies_to(value, axis, groups=None):
    count = len(groups[0]) if groups else lax.axis_size(axis)
    spread = jnp.broadcast_to(value[None], (count,) + value.shape)
    return lax.all_to_all(spread, axis, 0, 0, axis_index_groups=groups, tiled=True)


def on_device(record, templates, template_groups):
    channels, stations, samples = record.shape
    n_tm, n_sta = lax.axis_size("tm"), lax.axis_size("sta")
    m, s = lax.axis_index("tm"), lax.axis_index("sta")
    n_a = n_sta
    n_b = n_tm // n_a
    near = [[a * n_b + b for b in range(n_b)] for a in range(n_a)]
    far = [[a * n_b + b for a in range(n_a)] for b in range(n_b)]
    spread = template_groups.shape[1]

    turn = [
        ((a * n_b + b) * n_sta + t, (t * n_b + b) * n_sta + a)
        for a in range(n_a)
        for b in range(n_b)
        for t in range(n_sta)
    ]
    lines = templates.reshape(spread * stations, -1)
    own = lax.ppermute(lines, ("tm", "sta"), turn)
    block = copies_to(own, "tm", far)
    block = block.reshape(n_a * spread * stations, -1)
    first = (s * n_b + lax.rem(m, n_b)) * n_a
    groups = lax.dynamic_slice_in_dim(template_groups, first, n_a, 0)

    halo = lax.ppermute(record[:, :, :L], "tm", [(i + 1, i) for i in range(n_tm - 1)])
    lines = channels * stations
    steps = samples // LANES
    piece = jnp.concatenate(
        [record.reshape(lines * steps, LANES), halo.reshape(lines * (L // LANES), LANES)]
    )
    around = copies_to(piece, "tm", near)
    main = around[:, : lines * steps].reshape(n_b, lines, steps, LANES)
    main = main.transpose(1, 0, 2, 3).reshape(lines, n_b * steps, LANES)
    tail = around[-1, lines * steps :].reshape(lines, L // LANES, LANES)
    rest = jnp.zeros((lines, 8 - L // LANES, LANES), record.dtype)
    series = copies_to(jnp.concatenate([main, tail, rest], axis=1), "sta")

    factor = math.sqrt(channels * L / (spread * stations))
    found = detect(groups, block, series, n_b, factor)
    found = lax.all_to_all(found, "tm", 0, 0, axis_index_groups=near, tiled=True)
    return found.reshape(n_b * n_a, samples)


def solution(mesh):
    return jax.shard_map(
        on_device,
        mesh=mesh,
        in_specs=(P(None, "sta", "tm"), P(("tm", "sta"), None, None, None), P()),
        out_specs=P("sta", "tm"),
        check_vma=False,
    )
```

```python
import math

import jax
import jax.numpy as jnp
from jax import lax
from jax.experimental import pallas as pl
from jax.experimental.pallas import tpu as pltpu
from jax.sharding import PartitionSpec as P

L = 512
LANES = 128
HALF = 64
SPAN = L + LANES
SLOTS = 4
epsilon = 1e-06


def detect_kernel(
    first_station,
    factor,
    place_ref,
    groups_ref,
    templates_ref,
    series_ref,
    before_ref,
    out_ref,
    source,
    home,
    count,
    waves,
    norms,
    band,
    shifts,
    energy,
    scales,
    windows,
    toeplitz,
    share,
    total,
    turned,
):
    block, spread = groups_ref.shape
    n_group = series_ref.shape[0]
    here = series_ref.shape[1] // 3
    padded = series_ref.shape[2]
    rows = total.shape[1]
    stations = templates_ref.shape[2]
    slots = block * spread * stations
    lane = lax.broadcasted_iota(jnp.int32, (1, LANES), 1)
    low = lane < HALF

    def clear(n, carry):
        source[n] = block * spread
        home[n] = block
        return carry

    lax.fori_loop(0, source.shape[0], clear, 0)
    for n in range(n_group):
        count[n] = 0
    for r in range(block):
        k = r ^ place_ref[0]
        held = (k & 1) * 4 + (k & 2) + k // 4
        for i in range(spread):
            named = groups_ref[r, i]
            slot = named * SLOTS + count[named]
            source[slot] = held * spread + i
            home[slot] = r
            count[named] = count[named] + 1
    spare = waves.shape[0] - slots
    for c in range(3):
        for n in range(block * spread):
            part = templates_ref[n // spread, n % spread, :, c * L : (c + 1) * L]
            at = n * stations
            waves[at : at + stations, c * SPAN : c * SPAN + L] = part.astype(jnp.float32)
        waves[0:slots, c * SPAN + L : (c + 1) * SPAN] = jnp.zeros((slots, LANES), jnp.float32)
    waves[slots:, :] = jnp.zeros((spare, 3 * SPAN), jnp.float32)
    squares = jnp.sum(jnp.square(waves[0:slots, :]), axis=1, keepdims=True)
    norms[0:slots, :] = jnp.broadcast_to(lax.rsqrt(squares + epsilon), (slots, LANES))
    norms[slots:, :] = jnp.zeros((spare, LANES), jnp.float32)
    r = lax.broadcasted_iota(jnp.int32, (LANES, LANES), 0)
    l = lax.broadcasted_iota(jnp.int32, (LANES, LANES), 1)
    band[0:LANES, :] = jnp.where(r >= l, 1.0, 0.0).astype(jnp.bfloat16)
    band[LANES : 2 * LANES, :] = jnp.ones((LANES, LANES), jnp.bfloat16)
    band[2 * LANES :, :] = jnp.where(r < l, 1.0, 0.0).astype(jnp.bfloat16)
    shifts[:, :, padded:, :] = jnp.zeros((3, 2, 8, LANES), jnp.float32)
    if before_ref is None:
        total[...] = jnp.zeros_like(total)
    else:
        total[...] = before_ref[...]

    def prepare(group, station, buffer):
        squares = jnp.zeros((padded, LANES), jnp.float32)
        for c in range(3):
            plain = series_ref[group, c * here + station].astype(jnp.float32)
            squares = squares + plain * plain
            shifts[c, 0, 0:padded, :] = plain
            after = shifts[c, 0, 1 : padded + 1, :]
            shifts[c, 1, 0:padded, :] = pltpu.roll(jnp.where(low, after, plain), HALF, 1)
        energy[...] = squares
        middle = energy[1 : rows + 1, :] + energy[2 : rows + 2, :] + energy[3 : rows + 3, :]
        pieces = jnp.concatenate([energy[0:rows, :], middle, energy[4 : rows + 4, :]], axis=1)
        coarse = pieces.astype(jnp.bfloat16)
        fine = (pieces - coarse.astype(jnp.float32)).astype(jnp.bfloat16)
        window_energy = jnp.dot(coarse, band[...], preferred_element_type=jnp.float32)
        window_energy += jnp.dot(fine, band[...], preferred_element_type=jnp.float32)
        scale = lax.rsqrt(window_energy + epsilon)
        other = pltpu.roll(scale, HALF, 1)
        scales[buffer, 0] = jnp.where(low, scale, other)
        scales[buffer, 1] = jnp.where(low, other, scale)
        for j in range(SLOTS):
            row = source[group * SLOTS + j] * stations + first_station + station
            for c in range(3):
                wave = waves[pl.ds(row, 1), c * SPAN : (c + 1) * SPAN]
                moved = pltpu.roll(
                    jnp.broadcast_to(wave, (HALF, SPAN)), 0, 1, stride=1, stride_axis=0
                )
                toeplitz[buffer, j * HALF : (j + 1) * HALF, c * SPAN : (c + 1) * SPAN] = (
                    moved.astype(jnp.bfloat16)
                )
        for c in range(3):
            for e in range(2):
                for v in range(SPAN // LANES):
                    at = c * SPAN + v * LANES
                    windows[buffer, e * rows : (e + 1) * rows, at : at + LANES] = shifts[
                        c, e, v : v + rows, :
                    ].astype(jnp.bfloat16)

    def combine(group, station, buffer):
        product = lax.dot_general(
            windows[buffer],
            toeplitz[buffer],
            (((1,), (1,)), ((), ())),
            preferred_element_type=jnp.float32,
        )
        weight = []
        for j in range(SLOTS):
            row = source[group * SLOTS + j] * stations + first_station + station
            weight.append(norms[pl.ds(row, 1), :])
        for p in range(SLOTS // 2):
            both = jnp.where(low, weight[2 * p], weight[2 * p + 1])
            at = p * LANES
            for e in range(2):
                term = product[e * rows : (e + 1) * rows, at : at + LANES]
                term = term * (scales[buffer, e] * both)
                if station:
                    term = term + share[e, :, at : at + LANES]
                share[e, :, at : at + LANES] = term

    def group_term(group, carry):
        later = lax.min(group + 1, n_group - 1)
        for station in range(here):
            if station < here - 1:
                prepare(group, station + 1, (station + 1) % 2)
            else:
                prepare(later, 0, (station + 1) % 2)
            combine(group, station, station % 2)
        for j in range(SLOTS):
            at = (j // 2) * LANES
            first = share[0, :, at : at + LANES]
            second = share[1, :, at : at + LANES]
            if j % 2 == 0:
                whole = jnp.where(low, first, pltpu.roll(second, HALF, 1))
            else:
                whole = jnp.where(low, pltpu.roll(first, HALF, 1), second)
            r = home[group * SLOTS + j]
            total[r] = total[r] + whole
        return carry

    prepare(0, 0, 0)
    lax.fori_loop(0, n_group, group_term, 0)
    if factor is None:
        out_ref[...] = total[...]
        return
    for r in range(block):
        turned[:, r, :] = total[r] * factor
    parts, _, samples = out_ref.shape
    for w in range(parts):
        for i in range(samples // LANES):
            out_ref[w, :, i * LANES : (i + 1) * LANES] = turned[w * (samples // LANES) + i]


def detect(place, groups, templates, series, before, first_station, parts, factor):
    n_group, channels, padded, _ = series.shape
    block, spread = groups.shape
    stations = templates.shape[2]
    slots = block * spread * stations
    rows = padded - 8
    samples = rows * LANES // parts
    spare = -(-(slots + stations) // 8) * 8
    if factor is None:
        out_shape = jax.ShapeDtypeStruct((block + 1, rows, LANES), jnp.float32)
    else:
        out_shape = jax.ShapeDtypeStruct((parts, block, samples), jnp.float32)
    operands = [place, groups, templates, series]
    spaces = [pltpu.SMEM, pltpu.SMEM, pltpu.VMEM, pltpu.VMEM]
    if before is not None:
        operands.append(before)
        spaces.append(pltpu.VMEM)

    def body(*refs):
        refs = list(refs)
        if before is None:
            refs.insert(4, None)
        detect_kernel(first_station, factor, *refs)

    return pl.pallas_call(
        body,
        out_shape=out_shape,
        in_specs=[pl.BlockSpec(memory_space=space) for space in spaces],
        out_specs=pl.BlockSpec(memory_space=pltpu.VMEM),
        scratch_shapes=[
            pltpu.SMEM((n_group * SLOTS,), jnp.int32),
            pltpu.SMEM((n_group * SLOTS,), jnp.int32),
            pltpu.SMEM((n_group,), jnp.int32),
            pltpu.VMEM((spare, 3 * SPAN), jnp.float32),
            pltpu.VMEM((spare, LANES), jnp.float32),
            pltpu.VMEM((3 * LANES, LANES), jnp.bfloat16),
            pltpu.VMEM((3, 2, padded + 8, LANES), jnp.float32),
            pltpu.VMEM((padded, LANES), jnp.float32),
            pltpu.VMEM((2, 2, rows, LANES), jnp.float32),
            pltpu.VMEM((2, 2 * rows, 3 * SPAN), jnp.bfloat16),
            pltpu.VMEM((2, SLOTS * HALF, 3 * SPAN), jnp.bfloat16),
            pltpu.VMEM((2, rows, SLOTS * HALF), jnp.float32),
            pltpu.VMEM((block + 1, rows, LANES), jnp.float32),
            pltpu.VMEM((rows, block, LANES), jnp.float32),
        ],
        compiler_params=pltpu.CompilerParams(vmem_limit_bytes=32 * 1024 * 1024),
        cost_estimate=pl.CostEstimate(
            flops=8 * n_group * (channels // 3) * 2 * rows * 3 * SPAN * SLOTS * HALF,
            bytes_accessed=series.size * 2 + templates.size * 2 + 4 * block * rows * LANES,
            transcendentals=0,
        ),
    )(*operands)


def copies_to(value, axis, groups=None):
    count = len(groups[0]) if groups else lax.axis_size(axis)
    spread = jnp.broadcast_to(value[None], (count,) + value.shape)
    return lax.all_to_all(spread, axis, 0, 0, axis_index_groups=groups, tiled=True)


def on_device(record, templates, template_groups):
    channels, stations, samples = record.shape
    n_tm, n_sta = lax.axis_size("tm"), lax.axis_size("sta")
    m, s = lax.axis_index("tm"), lax.axis_index("sta")
    n_a = n_sta
    n_b = n_tm // n_a
    near = [[a * n_b + b for b in range(n_b)] for a in range(n_a)]
    far = [[a * n_b + b for a in range(n_a)] for b in range(n_b)]
    spread = template_groups.shape[1]

    def device(a, b, t):
        return (a * n_b + b) * n_sta + t

    def carried(value, target):
        pairs = [
            (device(a, b, t), device(*target(a, b, t)))
            for a in range(n_a)
            for b in range(n_b)
            for t in range(n_sta)
        ]
        return lax.ppermute(value, ("tm", "sta"), pairs)

    held = templates
    half = n_a // 2
    held = jnp.concatenate(
        [
            carried(held, lambda a, b, t: (t, b, a)),
            carried(held, lambda a, b, t: (t ^ half, b, a)),
        ]
    )
    step = half // 2
    while step:
        held = jnp.concatenate([held, carried(held, lambda a, b, t: (a ^ step, b, t))])
        step //= 2
    place = (m // n_b).reshape(1)
    first = (s * n_b + lax.rem(m, n_b)) * n_a
    groups = lax.dynamic_slice_in_dim(template_groups, first, n_a, 0)

    halo = lax.ppermute(record[:, :, :L], "tm", [(i + 1, i) for i in range(n_tm - 1)])
    lines = channels * stations
    steps = samples // LANES
    piece = jnp.concatenate(
        [record.reshape(lines * steps, LANES), halo.reshape(lines * (L // LANES), LANES)]
    )
    around = copies_to(piece, "tm", near)
    main = around[:, : lines * steps].reshape(n_b, channels, stations, steps, LANES)
    tail = around[-1, lines * steps :].reshape(channels, stations, L // LANES, LANES)
    some = stations // 2
    total = None
    for begin in range(0, stations, some):
        part = main[:, :, begin : begin + some].transpose(1, 2, 0, 3, 4)
        part = part.reshape(channels * some, n_b * steps, LANES)
        end = tail[:, begin : begin + some].reshape(channels * some, L // LANES, LANES)
        rest = jnp.zeros((channels * some, 8 - L // LANES, LANES), record.dtype)
        series = copies_to(jnp.concatenate([part, end, rest], axis=1), "sta")
        last = begin + some == stations
        factor = math.sqrt(channels * L / (spread * stations)) if last else None
        total = detect(place, groups, held, series, total, begin, n_b, factor)

    found = lax.all_to_all(total, "tm", 0, 0, axis_index_groups=near, tiled=True)
    return found.reshape(n_b * n_a, samples)


def solution(mesh):
    return jax.shard_map(
        on_device,
        mesh=mesh,
        in_specs=(P(None, "sta", "tm"), P(("tm", "sta"), None, None, None), P()),
        out_specs=P("sta", "tm"),
        check_vma=False,
    )
```

```python
import math

import jax
import jax.numpy as jnp
from jax import lax
from jax.experimental import pallas as pl
from jax.experimental.pallas import tpu as pltpu
from jax.sharding import PartitionSpec as P

L = 512
LANES = 128
HALF = 64
SPAN = L + LANES
SLOTS = 4
epsilon = 1e-06


def detect_kernel(
    first_station,
    factor,
    place_ref,
    groups_ref,
    templates_ref,
    series_ref,
    before_ref,
    out_ref,
    source,
    home,
    count,
    waves,
    norms,
    band,
    shifts,
    energy,
    scales,
    windows,
    toeplitz,
    share,
    total,
    turned,
):
    block, spread = groups_ref.shape
    n_group = series_ref.shape[0]
    here = series_ref.shape[1] // 3
    padded = series_ref.shape[2]
    rows = total.shape[1]
    stations = templates_ref.shape[2]
    slots = block * spread * stations
    lane = lax.broadcasted_iota(jnp.int32, (1, LANES), 1)
    low = lane < HALF

    def clear(n, carry):
        source[n] = block * spread
        home[n] = block
        return carry

    lax.fori_loop(0, source.shape[0], clear, 0)
    for n in range(n_group):
        count[n] = 0
    for r in range(block):
        k = r ^ place_ref[0]
        held = (k & 1) * 4 + (k & 2) + k // 4
        for i in range(spread):
            named = groups_ref[r, i]
            slot = named * SLOTS + count[named]
            source[slot] = held * spread + i
            home[slot] = r
            count[named] = count[named] + 1
    spare = waves.shape[0] - slots
    for c in range(3):
        for n in range(block * spread):
            part = templates_ref[n // spread, n % spread, :, c * L : (c + 1) * L]
            at = n * stations
            waves[at : at + stations, c * SPAN : c * SPAN + L] = part.astype(jnp.float32)
        waves[0:slots, c * SPAN + L : (c + 1) * SPAN] = jnp.zeros((slots, LANES), jnp.float32)
    waves[slots:, :] = jnp.zeros((spare, 3 * SPAN), jnp.float32)
    squares = jnp.sum(jnp.square(waves[0:slots, :]), axis=1, keepdims=True)
    norms[0:slots, :] = jnp.broadcast_to(lax.rsqrt(squares + epsilon), (slots, LANES))
    norms[slots:, :] = jnp.zeros((spare, LANES), jnp.float32)
    r = lax.broadcasted_iota(jnp.int32, (LANES, LANES), 0)
    l = lax.broadcasted_iota(jnp.int32, (LANES, LANES), 1)
    band[0:LANES, :] = jnp.where(r >= l, 1.0, 0.0).astype(jnp.bfloat16)
    band[LANES : 2 * LANES, :] = jnp.ones((LANES, LANES), jnp.bfloat16)
    band[2 * LANES :, :] = jnp.where(r < l, 1.0, 0.0).astype(jnp.bfloat16)
    shifts[:, :, padded:, :] = jnp.zeros((3, 2, 8, LANES), jnp.float32)
    if before_ref is None:
        total[...] = jnp.zeros_like(total)
    else:
        total[...] = before_ref[...]

    def prepare(group, station, buffer):
        squares = jnp.zeros((padded, LANES), jnp.float32)
        for c in range(3):
            plain = series_ref[group, c * here + station].astype(jnp.float32)
            squares = squares + plain * plain
            shifts[c, 0, 0:padded, :] = plain
            after = shifts[c, 0, 1 : padded + 1, :]
            shifts[c, 1, 0:padded, :] = pltpu.roll(jnp.where(low, after, plain), HALF, 1)
        energy[...] = squares
        middle = energy[1 : rows + 1, :] + energy[2 : rows + 2, :] + energy[3 : rows + 3, :]
        pieces = jnp.concatenate([energy[0:rows, :], middle, energy[4 : rows + 4, :]], axis=1)
        coarse = pieces.astype(jnp.bfloat16)
        fine = (pieces - coarse.astype(jnp.float32)).astype(jnp.bfloat16)
        window_energy = jnp.dot(coarse, band[...], preferred_element_type=jnp.float32)
        window_energy += jnp.dot(fine, band[...], preferred_element_type=jnp.float32)
        scale = lax.rsqrt(window_energy + epsilon)
        other = pltpu.roll(scale, HALF, 1)
        scales[buffer, 0] = jnp.where(low, scale, other)
        scales[buffer, 1] = jnp.where(low, other, scale)
        for j in range(SLOTS):
            row = source[group * SLOTS + j] * stations + first_station + station
            for c in range(3):
                wave = waves[pl.ds(row, 1), c * SPAN : (c + 1) * SPAN]
                moved = pltpu.roll(
                    jnp.broadcast_to(wave, (HALF, SPAN)), 0, 1, stride=1, stride_axis=0
                )
                toeplitz[buffer, j * HALF : (j + 1) * HALF, c * SPAN : (c + 1) * SPAN] = (
                    moved.astype(jnp.bfloat16)
                )
        for c in range(3):
            for e in range(2):
                for v in range(SPAN // LANES):
                    at = c * SPAN + v * LANES
                    windows[buffer, e * rows : (e + 1) * rows, at : at + LANES] = shifts[
                        c, e, v : v + rows, :
                    ].astype(jnp.bfloat16)

    def combine(group, station, buffer):
        product = lax.dot_general(
            windows[buffer],
            toeplitz[buffer],
            (((1,), (1,)), ((), ())),
            preferred_element_type=jnp.float32,
        )
        weight = []
        for j in range(SLOTS):
            row = source[group * SLOTS + j] * stations + first_station + station
            weight.append(norms[pl.ds(row, 1), :])
        for p in range(SLOTS // 2):
            both = jnp.where(low, weight[2 * p], weight[2 * p + 1])
            at = p * LANES
            for e in range(2):
                term = product[e * rows : (e + 1) * rows, at : at + LANES]
                term = term * (scales[buffer, e] * both)
                if station:
                    term = term + share[e, :, at : at + LANES]
                share[e, :, at : at + LANES] = term

    def group_term(group, carry):
        later = lax.min(group + 1, n_group - 1)
        for station in range(here):
            if station < here - 1:
                prepare(group, station + 1, (station + 1) % 2)
            else:
                prepare(later, 0, (station + 1) % 2)
            combine(group, station, station % 2)
        for j in range(SLOTS):
            at = (j // 2) * LANES
            first = share[0, :, at : at + LANES]
            second = share[1, :, at : at + LANES]
            if j % 2 == 0:
                whole = jnp.where(low, first, pltpu.roll(second, HALF, 1))
            else:
                whole = jnp.where(low, pltpu.roll(first, HALF, 1), second)
            r = home[group * SLOTS + j]
            total[r] = total[r] + whole
        return carry

    prepare(0, 0, 0)
    lax.fori_loop(0, n_group, group_term, 0)
    if factor is None:
        out_ref[...] = total[...]
        return
    for r in range(block):
        turned[:, r, :] = total[r] * factor
    parts, _, samples = out_ref.shape
    for w in range(parts):
        for i in range(samples // LANES):
            out_ref[w, :, i * LANES : (i + 1) * LANES] = turned[w * (samples // LANES) + i]


def detect(place, groups, templates, series, before, first_station, parts, factor):
    n_group, channels, padded, _ = series.shape
    block, spread = groups.shape
    stations = templates.shape[2]
    slots = block * spread * stations
    rows = padded - 8
    samples = rows * LANES // parts
    spare = -(-(slots + stations) // 8) * 8
    if factor is None:
        out_shape = jax.ShapeDtypeStruct((block + 1, rows, LANES), jnp.float32)
    else:
        out_shape = jax.ShapeDtypeStruct((parts, block, samples), jnp.float32)
    operands = [place, groups, templates, series]
    spaces = [pltpu.SMEM, pltpu.SMEM, pltpu.VMEM, pltpu.VMEM]
    if before is not None:
        operands.append(before)
        spaces.append(pltpu.VMEM)

    def body(*refs):
        refs = list(refs)
        if before is None:
            refs.insert(4, None)
        detect_kernel(first_station, factor, *refs)

    return pl.pallas_call(
        body,
        out_shape=out_shape,
        in_specs=[pl.BlockSpec(memory_space=space) for space in spaces],
        out_specs=pl.BlockSpec(memory_space=pltpu.VMEM),
        scratch_shapes=[
            pltpu.SMEM((n_group * SLOTS,), jnp.int32),
            pltpu.SMEM((n_group * SLOTS,), jnp.int32),
            pltpu.SMEM((n_group,), jnp.int32),
            pltpu.VMEM((spare, 3 * SPAN), jnp.float32),
            pltpu.VMEM((spare, LANES), jnp.float32),
            pltpu.VMEM((3 * LANES, LANES), jnp.bfloat16),
            pltpu.VMEM((3, 2, padded + 8, LANES), jnp.float32),
            pltpu.VMEM((padded, LANES), jnp.float32),
            pltpu.VMEM((2, 2, rows, LANES), jnp.float32),
            pltpu.VMEM((2, 2 * rows, 3 * SPAN), jnp.bfloat16),
            pltpu.VMEM((2, SLOTS * HALF, 3 * SPAN), jnp.bfloat16),
            pltpu.VMEM((2, rows, SLOTS * HALF), jnp.float32),
            pltpu.VMEM((block + 1, rows, LANES), jnp.float32),
            pltpu.VMEM((rows, block, LANES), jnp.float32),
        ],
        compiler_params=pltpu.CompilerParams(vmem_limit_bytes=32 * 1024 * 1024),
        cost_estimate=pl.CostEstimate(
            flops=8 * n_group * (channels // 3) * 2 * rows * 3 * SPAN * SLOTS * HALF,
            bytes_accessed=series.size * 2 + templates.size * 2 + 4 * block * rows * LANES,
            transcendentals=0,
        ),
    )(*operands)


def copies_to(value, axis, groups=None):
    count = len(groups[0]) if groups else lax.axis_size(axis)
    spread = jnp.broadcast_to(value[None], (count,) + value.shape)
    return lax.all_to_all(spread, axis, 0, 0, axis_index_groups=groups, tiled=True)


def on_device(record, templates, template_groups):
    channels, stations, samples = record.shape
    n_tm, n_sta = lax.axis_size("tm"), lax.axis_size("sta")
    m, s = lax.axis_index("tm"), lax.axis_index("sta")
    n_a = n_sta
    n_b = n_tm // n_a
    near = [[a * n_b + b for b in range(n_b)] for a in range(n_a)]
    far = [[a * n_b + b for a in range(n_a)] for b in range(n_b)]
    spread = template_groups.shape[1]

    def device(a, b, t):
        return (a * n_b + b) * n_sta + t

    def carried(value, target):
        pairs = [
            (device(a, b, t), device(*target(a, b, t)))
            for a in range(n_a)
            for b in range(n_b)
            for t in range(n_sta)
        ]
        return lax.ppermute(value, ("tm", "sta"), pairs)

    near_ones = [carried(templates, lambda a, b, t: (t ^ k, b, a)) for k in (0, 4, 2, 6)]
    held = jnp.concatenate(near_ones)
    held = jnp.concatenate([held, carried(held, lambda a, b, t: (a ^ 1, b, t))])
    place = (m // n_b).reshape(1)
    first = (s * n_b + lax.rem(m, n_b)) * n_a
    groups = lax.dynamic_slice_in_dim(template_groups, first, n_a, 0)

    halo = lax.ppermute(record[:, :, :L], "tm", [(i + 1, i) for i in range(n_tm - 1)])
    lines = channels * stations
    steps = samples // LANES
    piece = jnp.concatenate(
        [record.reshape(lines * steps, LANES), halo.reshape(lines * (L // LANES), LANES)]
    )
    around = copies_to(piece, "tm", near)
    main = around[:, : lines * steps].reshape(n_b, channels, stations, steps, LANES)
    tail = around[-1, lines * steps :].reshape(channels, stations, L // LANES, LANES)
    some = stations // 2
    total = None
    for begin in range(0, stations, some):
        part = main[:, :, begin : begin + some].transpose(1, 2, 0, 3, 4)
        part = part.reshape(channels * some, n_b * steps, LANES)
        end = tail[:, begin : begin + some].reshape(channels * some, L // LANES, LANES)
        rest = jnp.zeros((channels * some, 8 - L // LANES, LANES), record.dtype)
        series = copies_to(jnp.concatenate([part, end, rest], axis=1), "sta")
        last = begin + some == stations
        factor = math.sqrt(channels * L / (spread * stations)) if last else None
        total = detect(place, groups, held, series, total, begin, n_b, factor)

    found = lax.all_to_all(total, "tm", 0, 0, axis_index_groups=near, tiled=True)
    return found.reshape(n_b * n_a, samples)


def solution(mesh):
    return jax.shard_map(
        on_device,
        mesh=mesh,
        in_specs=(P(None, "sta", "tm"), P(("tm", "sta"), None, None, None), P()),
        out_specs=P("sta", "tm"),
        check_vma=False,
    )
```

```python
import math

import jax
import jax.numpy as jnp
from jax import lax
from jax.experimental import pallas as pl
from jax.experimental.pallas import tpu as pltpu
from jax.sharding import PartitionSpec as P

L = 512
LANES = 128
HALF = 64
SPAN = L + LANES
SLOTS = 4
epsilon = 1e-06


def detect_kernel(
    first_station,
    here,
    padded,
    factor,
    groups_ref,
    templates_ref,
    series_ref,
    before_ref,
    out_ref,
    source,
    home,
    count,
    wide,
    waves,
    norms,
    band,
    shifts,
    energy,
    scales,
    windows,
    toeplitz,
    share,
    total,
    turned,
):
    block, spread = groups_ref.shape
    n_group = series_ref.shape[0]
    rows = total.shape[1]
    parts = 3 * L // LANES
    slots = wide.shape[0] // parts
    stations = slots // (block * spread)
    lane = lax.broadcasted_iota(jnp.int32, (1, LANES), 1)
    low = lane < HALF

    def clear(n, carry):
        source[n] = block * spread
        home[n] = block
        return carry

    lax.fori_loop(0, source.shape[0], clear, 0)
    for n in range(n_group):
        count[n] = 0
    for r in range(block):
        for i in range(spread):
            named = groups_ref[r, i]
            slot = named * SLOTS + count[named]
            source[slot] = r * spread + i
            home[slot] = r
            count[named] = count[named] + 1
    spare = waves.shape[0] - slots
    for r in range(block):
        each = slots // block * parts
        wide[r * each : (r + 1) * each, :] = templates_ref[r, -each:, :].astype(jnp.float32)
    for c in range(3):
        for v in range(L // LANES):
            at = c * SPAN + v * LANES
            waves[0:slots, at : at + LANES] = wide[pl.ds(c * L // LANES + v, slots, parts), :]
        waves[0:slots, c * SPAN + L : (c + 1) * SPAN] = jnp.zeros((slots, LANES), jnp.float32)
    waves[slots:, :] = jnp.zeros((spare, 3 * SPAN), jnp.float32)
    squares = jnp.sum(jnp.square(waves[0:slots, :]), axis=1, keepdims=True)
    norms[0:slots, :] = jnp.broadcast_to(lax.rsqrt(squares + epsilon), (slots, LANES))
    norms[slots:, :] = jnp.zeros((spare, LANES), jnp.float32)
    r = lax.broadcasted_iota(jnp.int32, (LANES, LANES), 0)
    l = lax.broadcasted_iota(jnp.int32, (LANES, LANES), 1)
    band[0:LANES, :] = jnp.where(r >= l, 1.0, 0.0).astype(jnp.bfloat16)
    band[LANES : 2 * LANES, :] = jnp.ones((LANES, LANES), jnp.bfloat16)
    band[2 * LANES :, :] = jnp.where(r < l, 1.0, 0.0).astype(jnp.bfloat16)
    shifts[:, :, padded:, :] = jnp.zeros((3, 2, 8, LANES), jnp.float32)
    if before_ref is None:
        total[...] = jnp.zeros_like(total)
    else:
        total[...] = before_ref[...]

    def prepare(group, station, buffer):
        squares = jnp.zeros((padded, LANES), jnp.float32)
        for c in range(3):
            at = (c * here + station) * padded
            plain = series_ref[group, at : at + padded, :].astype(jnp.float32)
            squares = squares + plain * plain
            shifts[c, 0, 0:padded, :] = plain
            after = shifts[c, 0, 1 : padded + 1, :]
            shifts[c, 1, 0:padded, :] = pltpu.roll(jnp.where(low, after, plain), HALF, 1)
        energy[...] = squares
        middle = energy[1 : rows + 1, :] + energy[2 : rows + 2, :] + energy[3 : rows + 3, :]
        pieces = jnp.concatenate([energy[0:rows, :], middle, energy[4 : rows + 4, :]], axis=1)
        coarse = pieces.astype(jnp.bfloat16)
        fine = (pieces - coarse.astype(jnp.float32)).astype(jnp.bfloat16)
        window_energy = jnp.dot(coarse, band[...], preferred_element_type=jnp.float32)
        window_energy += jnp.dot(fine, band[...], preferred_element_type=jnp.float32)
        scale = lax.rsqrt(window_energy + epsilon)
        other = pltpu.roll(scale, HALF, 1)
        scales[buffer, 0] = jnp.where(low, scale, other)
        scales[buffer, 1] = jnp.where(low, other, scale)
        for j in range(SLOTS):
            row = source[group * SLOTS + j] * stations + first_station + station
            for c in range(3):
                wave = waves[pl.ds(row, 1), c * SPAN : (c + 1) * SPAN]
                moved = pltpu.roll(
                    jnp.broadcast_to(wave, (HALF, SPAN)), 0, 1, stride=1, stride_axis=0
                )
                toeplitz[buffer, j * HALF : (j + 1) * HALF, c * SPAN : (c + 1) * SPAN] = (
                    moved.astype(jnp.bfloat16)
                )
        for c in range(3):
            for e in range(2):
                for v in range(SPAN // LANES):
                    at = c * SPAN + v * LANES
                    windows[buffer, e * rows : (e + 1) * rows, at : at + LANES] = shifts[
                        c, e, v : v + rows, :
                    ].astype(jnp.bfloat16)

    def combine(group, station, buffer):
        product = lax.dot_general(
            windows[buffer],
            toeplitz[buffer],
            (((1,), (1,)), ((), ())),
            preferred_element_type=jnp.float32,
        )
        weight = []
        for j in range(SLOTS):
            row = source[group * SLOTS + j] * stations + first_station + station
            weight.append(norms[pl.ds(row, 1), :])
        for p in range(SLOTS // 2):
            both = jnp.where(low, weight[2 * p], weight[2 * p + 1])
            at = p * LANES
            for e in range(2):
                term = product[e * rows : (e + 1) * rows, at : at + LANES]
                term = term * (scales[buffer, e] * both)
                if station:
                    term = term + share[e, :, at : at + LANES]
                share[e, :, at : at + LANES] = term

    def group_term(group, carry):
        later = lax.min(group + 1, n_group - 1)
        for station in range(here):
            if station < here - 1:
                prepare(group, station + 1, (station + 1) % 2)
            else:
                prepare(later, 0, (station + 1) % 2)
            combine(group, station, station % 2)
        for j in range(SLOTS):
            at = (j // 2) * LANES
            first = share[0, :, at : at + LANES]
            second = share[1, :, at : at + LANES]
            if j % 2 == 0:
                whole = jnp.where(low, first, pltpu.roll(second, HALF, 1))
            else:
                whole = jnp.where(low, pltpu.roll(first, HALF, 1), second)
            r = home[group * SLOTS + j]
            total[r] = total[r] + whole
        return carry

    prepare(0, 0, 0)
    lax.fori_loop(0, n_group, group_term, 0)
    if factor is None:
        out_ref[...] = total[...]
        return
    for r in range(block):
        turned[:, r, :] = total[r] * factor
    n_out, _, samples = out_ref.shape
    for w in range(n_out):
        for i in range(samples // LANES):
            out_ref[w, :, i * LANES : (i + 1) * LANES] = turned[w * (samples // LANES) + i]


def detect(groups, templates, series, before, first_station, here, padded, parts, factor):
    n_group = templates.shape[0]
    block, spread = groups.shape
    stations = 4
    slots = block * spread * stations
    rows = padded - 8
    samples = rows * LANES // parts
    spare = -(-(slots + stations) // 8) * 8
    if factor is None:
        out_shape = jax.ShapeDtypeStruct((block + 1, rows, LANES), jnp.float32)
    else:
        out_shape = jax.ShapeDtypeStruct((parts, block, samples), jnp.float32)
    operands = [groups, templates]
    spaces = [pltpu.SMEM, pltpu.VMEM]
    for other in (series, before):
        if other is not None:
            operands.append(other)
            spaces.append(pltpu.VMEM)

    def body(*refs):
        refs = list(refs)
        if series is None:
            refs.insert(2, refs[1])
        if before is None:
            refs.insert(3, None)
        detect_kernel(first_station, here, padded, factor, *refs)

    return pl.pallas_call(
        body,
        out_shape=out_shape,
        in_specs=[pl.BlockSpec(memory_space=space) for space in spaces],
        out_specs=pl.BlockSpec(memory_space=pltpu.VMEM),
        scratch_shapes=[
            pltpu.SMEM((n_group * SLOTS,), jnp.int32),
            pltpu.SMEM((n_group * SLOTS,), jnp.int32),
            pltpu.SMEM((n_group,), jnp.int32),
            pltpu.VMEM((slots * 3 * L // LANES, LANES), jnp.float32),
            pltpu.VMEM((spare, 3 * SPAN), jnp.float32),
            pltpu.VMEM((spare, LANES), jnp.float32),
            pltpu.VMEM((3 * LANES, LANES), jnp.bfloat16),
            pltpu.VMEM((3, 2, padded + 8, LANES), jnp.float32),
            pltpu.VMEM((padded, LANES), jnp.float32),
            pltpu.VMEM((2, 2, rows, LANES), jnp.float32),
            pltpu.VMEM((2, 2 * rows, 3 * SPAN), jnp.bfloat16),
            pltpu.VMEM((2, SLOTS * HALF, 3 * SPAN), jnp.bfloat16),
            pltpu.VMEM((2, rows, SLOTS * HALF), jnp.float32),
            pltpu.VMEM((block + 1, rows, LANES), jnp.float32),
            pltpu.VMEM((rows, block, LANES), jnp.float32),
        ],
        compiler_params=pltpu.CompilerParams(vmem_limit_bytes=32 * 1024 * 1024),
        cost_estimate=pl.CostEstimate(
            flops=16 * n_group * here * 2 * rows * 3 * SPAN * SLOTS * HALF,
            bytes_accessed=templates.size * 2 + 4 * block * rows * LANES,
            transcendentals=0,
        ),
    )(*operands)


def copies_to(value, axis, groups=None):
    count = len(groups[0]) if groups else lax.axis_size(axis)
    spread = jnp.broadcast_to(value[None], (count,) + value.shape)
    return lax.all_to_all(spread, axis, 0, 0, axis_index_groups=groups, tiled=True)


def on_device(record, templates, template_groups):
    channels, stations, samples = record.shape
    n_tm, n_sta = lax.axis_size("tm"), lax.axis_size("sta")
    m, s = lax.axis_index("tm"), lax.axis_index("sta")
    n_a = n_sta
    n_b = n_tm // n_a
    near = [[a * n_b + b for b in range(n_b)] for a in range(n_a)]
    far = [[a * n_b + b for a in range(o, n_a, 2)] for b in range(n_b) for o in range(2)]
    spread = template_groups.shape[1]

    own = templates.reshape(-1, LANES)
    halo = lax.ppermute(record[:, :, :L], "tm", [(i + 1, i) for i in range(n_tm - 1)])
    same = copies_to(own, "tm", far)
    halo, same = lax.optimization_barrier((halo, same))
    swap = [(a * n_b + b, (a ^ 1) * n_b + b) for a in range(n_a) for b in range(n_b)]
    other = lax.ppermute(same, "tm", swap)
    odd = lax.rem(m // n_b, 2) == 1
    held = jnp.stack([jnp.where(odd, other, same), jnp.where(odd, same, other)], axis=1)
    held = held.reshape((n_a,) + own.shape)
    first = (s * n_b + lax.rem(m, n_b)) * n_a
    groups = lax.dynamic_slice_in_dim(template_groups, first, n_a, 0)

    lines = channels * stations
    steps = samples // LANES
    piece = jnp.concatenate(
        [record.reshape(lines * steps, LANES), halo.reshape(lines * (L // LANES), LANES)]
    )
    around = copies_to(piece, "tm", near)
    main = around[:, : lines * steps].reshape(n_b, channels, stations, steps, LANES)
    tail = around[-1, lines * steps :].reshape(channels, stations, L // LANES, LANES)
    some = stations // 2
    padded = n_b * steps + 8
    flat = []
    for begin in range(0, stations, some):
        part = main[:, :, begin : begin + some].transpose(1, 2, 0, 3, 4)
        part = part.reshape(channels * some, n_b * steps, LANES)
        end = tail[:, begin : begin + some].reshape(channels * some, L // LANES, LANES)
        rest = jnp.zeros((channels * some, 8 - L // LANES, LANES), record.dtype)
        part = jnp.concatenate([part, end, rest], axis=1).reshape(-1, LANES)
        flat.append(jnp.broadcast_to(part[None], (n_sta,) + part.shape))
    both = jnp.concatenate([flat[0], held], axis=1)
    both = lax.all_to_all(both, "sta", 0, 0, tiled=True)
    late, both = lax.optimization_barrier((flat[1], both))
    late = lax.all_to_all(late, "sta", 0, 0, tiled=True)
    factor = math.sqrt(channels * L / (spread * stations))
    total = detect(groups, both, None, None, 0, some, padded, n_b, None)
    total = detect(groups, both, late, total, some, some, padded, n_b, factor)

    found = lax.all_to_all(total, "tm", 0, 0, axis_index_groups=near, tiled=True)
    return found.reshape(n_b * n_a, samples)


def solution(mesh):
    return jax.shard_map(
        on_device,
        mesh=mesh,
        in_specs=(P(None, "sta", "tm"), P(("tm", "sta"), None, None, None), P()),
        out_specs=P("sta", "tm"),
        check_vma=False,
    )
```

```python
import math

import jax
import jax.numpy as jnp
from jax import lax
from jax.experimental import pallas as pl
from jax.experimental.pallas import tpu as pltpu
from jax.sharding import PartitionSpec as P

L = 512
LANES = 128
HALF = 64
SPAN = L + LANES
SLOTS = 4
epsilon = 1e-06


def detect_kernel(
    padded,
    factor,
    order_ref,
    groups_ref,
    templates_ref,
    pieces_refs,
    before_ref,
    out_ref,
    source,
    home,
    count,
    series,
    wide,
    waves,
    norms,
    band,
    shifts,
    energy,
    scales,
    windows,
    toeplitz,
    share,
    total,
    turned,
):
    block, spread = groups_ref.shape
    n_group = len(pieces_refs)
    rows = total.shape[1]
    parts = 3 * L // LANES
    slots = wide.shape[0] // parts
    stations = slots // (block * spread)
    lane = lax.broadcasted_iota(jnp.int32, (1, LANES), 1)
    low = lane < HALF

    def clear(n, carry):
        source[n] = block * spread
        home[n] = block
        return carry

    lax.fori_loop(0, source.shape[0], clear, 0)
    for n in range(count.shape[0]):
        count[n] = 0
    for n in range(n_group):
        series[n] = pieces_refs[n][...]
    for r in range(block):
        for i in range(spread):
            named = groups_ref[r, i]
            slot = named * SLOTS + count[named]
            source[slot] = r * spread + i
            home[slot] = r
            count[named] = count[named] + 1
    spare = waves.shape[0] - slots
    for r in range(block):
        each = slots // block * parts
        wide[r * each : (r + 1) * each, :] = templates_ref[r, -each:, :].astype(jnp.float32)
    for c in range(3):
        for v in range(L // LANES):
            at = c * SPAN + v * LANES
            waves[0:slots, at : at + LANES] = wide[pl.ds(c * L // LANES + v, slots, parts), :]
        waves[0:slots, c * SPAN + L : (c + 1) * SPAN] = jnp.zeros((slots, LANES), jnp.float32)
    waves[slots:, :] = jnp.zeros((spare, 3 * SPAN), jnp.float32)
    squares = jnp.sum(jnp.square(waves[0:slots, :]), axis=1, keepdims=True)
    norms[0:slots, :] = jnp.broadcast_to(lax.rsqrt(squares + epsilon), (slots, LANES))
    norms[slots:, :] = jnp.zeros((spare, LANES), jnp.float32)
    r = lax.broadcasted_iota(jnp.int32, (LANES, LANES), 0)
    l = lax.broadcasted_iota(jnp.int32, (LANES, LANES), 1)
    band[0:LANES, :] = jnp.where(r >= l, 1.0, 0.0).astype(jnp.bfloat16)
    band[LANES : 2 * LANES, :] = jnp.ones((LANES, LANES), jnp.bfloat16)
    band[2 * LANES :, :] = jnp.where(r < l, 1.0, 0.0).astype(jnp.bfloat16)
    shifts[:, :, padded:, :] = jnp.zeros((3, 2, 8, LANES), jnp.float32)
    if before_ref is None:
        total[...] = jnp.zeros_like(total)
    else:
        total[...] = before_ref[...]

    def prepare(group, station, buffer):
        squares = jnp.zeros((padded, LANES), jnp.float32)
        for c in range(3):
            at = (c * stations + station) * padded
            plain = series[group, at : at + padded, :].astype(jnp.float32)
            squares = squares + plain * plain
            shifts[c, 0, 0:padded, :] = plain
            after = shifts[c, 0, 1 : padded + 1, :]
            shifts[c, 1, 0:padded, :] = pltpu.roll(jnp.where(low, after, plain), HALF, 1)
        energy[...] = squares
        middle = energy[1 : rows + 1, :] + energy[2 : rows + 2, :] + energy[3 : rows + 3, :]
        pieces = jnp.concatenate([energy[0:rows, :], middle, energy[4 : rows + 4, :]], axis=1)
        coarse = pieces.astype(jnp.bfloat16)
        fine = (pieces - coarse.astype(jnp.float32)).astype(jnp.bfloat16)
        window_energy = jnp.dot(coarse, band[...], preferred_element_type=jnp.float32)
        window_energy += jnp.dot(fine, band[...], preferred_element_type=jnp.float32)
        scale = lax.rsqrt(window_energy + epsilon)
        other = pltpu.roll(scale, HALF, 1)
        scales[buffer, 0] = jnp.where(low, scale, other)
        scales[buffer, 1] = jnp.where(low, other, scale)
        for j in range(SLOTS):
            row = source[order_ref[group] * SLOTS + j] * stations + station
            for c in range(3):
                wave = waves[pl.ds(row, 1), c * SPAN : (c + 1) * SPAN]
                moved = pltpu.roll(
                    jnp.broadcast_to(wave, (HALF, SPAN)), 0, 1, stride=1, stride_axis=0
                )
                toeplitz[buffer, j * HALF : (j + 1) * HALF, c * SPAN : (c + 1) * SPAN] = (
                    moved.astype(jnp.bfloat16)
                )
        for c in range(3):
            for e in range(2):
                for v in range(SPAN // LANES):
                    at = c * SPAN + v * LANES
                    windows[buffer, e * rows : (e + 1) * rows, at : at + LANES] = shifts[
                        c, e, v : v + rows, :
                    ].astype(jnp.bfloat16)

    def combine(group, station, buffer):
        product = lax.dot_general(
            windows[buffer],
            toeplitz[buffer],
            (((1,), (1,)), ((), ())),
            preferred_element_type=jnp.float32,
        )
        weight = []
        for j in range(SLOTS):
            row = source[order_ref[group] * SLOTS + j] * stations + station
            weight.append(norms[pl.ds(row, 1), :])
        for p in range(SLOTS // 2):
            both = jnp.where(low, weight[2 * p], weight[2 * p + 1])
            at = p * LANES
            for e in range(2):
                term = product[e * rows : (e + 1) * rows, at : at + LANES]
                term = term * (scales[buffer, e] * both)
                if station:
                    term = term + share[e, :, at : at + LANES]
                share[e, :, at : at + LANES] = term

    def group_term(group, carry):
        later = lax.min(group + 1, n_group - 1)
        for station in range(stations):
            if station < stations - 1:
                prepare(group, station + 1, (station + 1) % 2)
            else:
                prepare(later, 0, (station + 1) % 2)
            combine(group, station, station % 2)
        for j in range(SLOTS):
            at = (j // 2) * LANES
            first = share[0, :, at : at + LANES]
            second = share[1, :, at : at + LANES]
            if j % 2 == 0:
                whole = jnp.where(low, first, pltpu.roll(second, HALF, 1))
            else:
                whole = jnp.where(low, pltpu.roll(first, HALF, 1), second)
            r = home[order_ref[group] * SLOTS + j]
            total[r] = total[r] + whole
        return carry

    prepare(0, 0, 0)
    lax.fori_loop(0, n_group, group_term, 0)
    if factor is None:
        out_ref[...] = total[...]
        return
    for r in range(block):
        turned[:, r, :] = total[r] * factor
    n_out, _, samples = out_ref.shape
    for w in range(n_out):
        for i in range(samples // LANES):
            out_ref[w, :, i * LANES : (i + 1) * LANES] = turned[w * (samples // LANES) + i]


def detect(order, groups, templates, pieces, before, n_all, padded, parts, factor):
    block, spread = groups.shape
    stations = 4
    slots = block * spread * stations
    rows = padded - 8
    samples = rows * LANES // parts
    spare = -(-(slots + stations) // 8) * 8
    if factor is None:
        out_shape = jax.ShapeDtypeStruct((block + 1, rows, LANES), jnp.float32)
    else:
        out_shape = jax.ShapeDtypeStruct((parts, block, samples), jnp.float32)
    operands = [order, groups, templates, *pieces]
    spaces = [pltpu.SMEM, pltpu.SMEM] + [pltpu.VMEM] * (1 + len(pieces))
    if before is not None:
        operands.append(before)
        spaces.append(pltpu.VMEM)

    def body(*refs):
        end = 3 + len(pieces)
        taken = refs[end] if before is not None else None
        rest = refs[end + (before is not None) :]
        detect_kernel(padded, factor, *refs[:3], refs[3:end], taken, *rest)

    return pl.pallas_call(
        body,
        out_shape=out_shape,
        in_specs=[pl.BlockSpec(memory_space=space) for space in spaces],
        out_specs=pl.BlockSpec(memory_space=pltpu.VMEM),
        scratch_shapes=[
            pltpu.SMEM((n_all * SLOTS,), jnp.int32),
            pltpu.SMEM((n_all * SLOTS,), jnp.int32),
            pltpu.SMEM((n_all,), jnp.int32),
            pltpu.VMEM((len(pieces),) + pieces[0].shape, jnp.bfloat16),
            pltpu.VMEM((slots * 3 * L // LANES, LANES), jnp.float32),
            pltpu.VMEM((spare, 3 * SPAN), jnp.float32),
            pltpu.VMEM((spare, LANES), jnp.float32),
            pltpu.VMEM((3 * LANES, LANES), jnp.bfloat16),
            pltpu.VMEM((3, 2, padded + 8, LANES), jnp.float32),
            pltpu.VMEM((padded, LANES), jnp.float32),
            pltpu.VMEM((2, 2, rows, LANES), jnp.float32),
            pltpu.VMEM((2, 2 * rows, 3 * SPAN), jnp.bfloat16),
            pltpu.VMEM((2, SLOTS * HALF, 3 * SPAN), jnp.bfloat16),
            pltpu.VMEM((2, rows, SLOTS * HALF), jnp.float32),
            pltpu.VMEM((block + 1, rows, LANES), jnp.float32),
            pltpu.VMEM((rows, block, LANES), jnp.float32),
        ],
        compiler_params=pltpu.CompilerParams(vmem_limit_bytes=32 * 1024 * 1024),
        cost_estimate=pl.CostEstimate(
            flops=16 * len(pieces) * stations * 2 * rows * 3 * SPAN * SLOTS * HALF,
            bytes_accessed=templates.size * 2 + 4 * block * rows * LANES,
            transcendentals=0,
        ),
    )(*operands)


def copies_to(value, axis, groups=None):
    count = len(groups[0]) if groups else lax.axis_size(axis)
    spread = jnp.broadcast_to(value[None], (count,) + value.shape)
    return lax.all_to_all(spread, axis, 0, 0, axis_index_groups=groups, tiled=True)


def on_device(record, templates, template_groups):
    channels, stations, samples = record.shape
    n_tm, n_sta = lax.axis_size("tm"), lax.axis_size("sta")
    m, s = lax.axis_index("tm"), lax.axis_index("sta")
    n_a = n_sta
    n_b = n_tm // n_a
    near = [[a * n_b + b for b in range(n_b)] for a in range(n_a)]
    far = [[a * n_b + b for a in range(n_a)] for b in range(n_b)]
    spread = template_groups.shape[1]

    turn = [
        ((a * n_b + b) * n_sta + t, (t * n_b + b) * n_sta + a)
        for a in range(n_a)
        for b in range(n_b)
        for t in range(n_sta)
    ]
    halo = lax.ppermute(record[:, :, :L], "tm", [(i + 1, i) for i in range(n_tm - 1)])
    own = lax.ppermute(templates.reshape(-1, LANES), ("tm", "sta"), turn)
    first = (s * n_b + lax.rem(m, n_b)) * n_a
    groups = lax.dynamic_slice_in_dim(template_groups, first, n_a, 0)

    lines = channels * stations
    steps = samples // LANES
    piece = jnp.concatenate(
        [record.reshape(lines * steps, LANES), halo.reshape(lines * (L // LANES), LANES)]
    )
    around = copies_to(piece, "tm", near)
    around, own = lax.optimization_barrier((around, own))
    block = copies_to(own, "tm", far)
    main = around[:, : lines * steps].reshape(n_b, lines, steps, LANES)
    main = main.transpose(1, 0, 2, 3).reshape(lines, n_b * steps, LANES)
    tail = around[-1, lines * steps :].reshape(lines, L // LANES, LANES)
    rest = jnp.zeros((lines, 8 - L // LANES, LANES), record.dtype)
    padded = n_b * steps + 8
    mine = jnp.concatenate([main, tail, rest], axis=1).reshape(-1, LANES)

    cores = 2
    n_y = n_sta // cores
    y, core = s // cores, lax.rem(s, cores)
    pieces = [mine]
    for k in range(1, n_y):
        pairs = [(t, (t + k * cores) % n_sta) for t in range(n_sta)]
        pieces.append(lax.ppermute(mine, "sta", pairs))
    swap = [(t, t ^ 1) for t in range(n_sta)]
    others = [lax.ppermute(value, "sta", swap) for value in pieces]
    rows_of_y = lax.rem(y - jnp.arange(n_y, dtype=jnp.int32) + n_y, n_y) * cores
    factor = math.sqrt(channels * L / (spread * stations))
    total = detect(rows_of_y + core, groups, block, pieces, None, n_sta, padded, n_b, None)
    total = detect(rows_of_y + 1 - core, groups, block, others, total, n_sta, padded, n_b, factor)

    found = lax.all_to_all(total, "tm", 0, 0, axis_index_groups=near, tiled=True)
    return found.reshape(n_b * n_a, samples)


def solution(mesh):
    return jax.shard_map(
        on_device,
        mesh=mesh,
        in_specs=(P(None, "sta", "tm"), P(("tm", "sta"), None, None, None), P()),
        out_specs=P("sta", "tm"),
        check_vma=False,
    )
```

```python
import math

import jax
import jax.numpy as jnp
from jax import lax
from jax.experimental import pallas as pl
from jax.experimental.pallas import tpu as pltpu
from jax.sharding import PartitionSpec as P

L = 512
LANES = 128
HALF = 64
SPAN = L + LANES
SLOTS = 4
epsilon = 1e-06


def detect_kernel(
    padded,
    factor,
    order_ref,
    groups_ref,
    templates_ref,
    pieces_refs,
    before_ref,
    out_ref,
    source,
    home,
    count,
    series,
    wide,
    waves,
    norms,
    band,
    shifts,
    energy,
    scales,
    windows,
    toeplitz,
    share,
    total,
    turned,
):
    block, spread = groups_ref.shape
    n_group = len(pieces_refs)
    rows = total.shape[1]
    parts = 3 * L // LANES
    slots = wide.shape[0] // parts
    stations = slots // (block * spread)
    lane = lax.broadcasted_iota(jnp.int32, (1, LANES), 1)
    low = lane < HALF

    def clear(n, carry):
        source[n] = block * spread
        home[n] = block
        return carry

    lax.fori_loop(0, source.shape[0], clear, 0)
    for n in range(count.shape[0]):
        count[n] = 0
    for n in range(n_group):
        series[n] = pieces_refs[n][...]
    for r in range(block):
        for i in range(spread):
            named = groups_ref[r, i]
            slot = named * SLOTS + count[named]
            source[slot] = r * spread + i
            home[slot] = r
            count[named] = count[named] + 1
    spare = waves.shape[0] - slots
    for r in range(block):
        each = slots // block * parts
        wide[r * each : (r + 1) * each, :] = templates_ref[r, -each:, :].astype(jnp.float32)
    for c in range(3):
        for v in range(L // LANES):
            at = c * SPAN + v * LANES
            waves[0:slots, at : at + LANES] = wide[pl.ds(c * L // LANES + v, slots, parts), :]
        waves[0:slots, c * SPAN + L : (c + 1) * SPAN] = jnp.zeros((slots, LANES), jnp.float32)
    waves[slots:, :] = jnp.zeros((spare, 3 * SPAN), jnp.float32)
    squares = jnp.sum(jnp.square(waves[0:slots, :]), axis=1, keepdims=True)
    norms[0:slots, :] = jnp.broadcast_to(lax.rsqrt(squares + epsilon), (slots, LANES))
    norms[slots:, :] = jnp.zeros((spare, LANES), jnp.float32)
    r = lax.broadcasted_iota(jnp.int32, (LANES, LANES), 0)
    l = lax.broadcasted_iota(jnp.int32, (LANES, LANES), 1)
    band[0:LANES, :] = jnp.where(r >= l, 1.0, 0.0).astype(jnp.bfloat16)
    band[LANES : 2 * LANES, :] = jnp.ones((LANES, LANES), jnp.bfloat16)
    band[2 * LANES :, :] = jnp.where(r < l, 1.0, 0.0).astype(jnp.bfloat16)
    shifts[:, :, padded:, :] = jnp.zeros((3, 2, 8, LANES), jnp.float32)
    if before_ref is None:
        total[...] = jnp.zeros_like(total)
    else:
        total[...] = before_ref[...]

    def prepare(group, station, buffer):
        squares = jnp.zeros((padded, LANES), jnp.float32)
        for c in range(3):
            at = (c * stations + station) * padded
            plain = series[group, at : at + padded, :].astype(jnp.float32)
            squares = squares + plain * plain
            shifts[c, 0, 0:padded, :] = plain
            after = shifts[c, 0, 1 : padded + 1, :]
            shifts[c, 1, 0:padded, :] = pltpu.roll(jnp.where(low, after, plain), HALF, 1)
        energy[...] = squares
        middle = energy[1 : rows + 1, :] + energy[2 : rows + 2, :] + energy[3 : rows + 3, :]
        pieces = jnp.concatenate([energy[0:rows, :], middle, energy[4 : rows + 4, :]], axis=1)
        coarse = pieces.astype(jnp.bfloat16)
        fine = (pieces - coarse.astype(jnp.float32)).astype(jnp.bfloat16)
        window_energy = jnp.dot(coarse, band[...], preferred_element_type=jnp.float32)
        window_energy += jnp.dot(fine, band[...], preferred_element_type=jnp.float32)
        scale = lax.rsqrt(window_energy + epsilon)
        other = pltpu.roll(scale, HALF, 1)
        scales[buffer, 0] = jnp.where(low, scale, other)
        scales[buffer, 1] = jnp.where(low, other, scale)
        for j in range(SLOTS):
            row = source[order_ref[group] * SLOTS + j] * stations + station
            for c in range(3):
                wave = waves[pl.ds(row, 1), c * SPAN : (c + 1) * SPAN]
                moved = pltpu.roll(
                    jnp.broadcast_to(wave, (HALF, SPAN)), 0, 1, stride=1, stride_axis=0
                )
                toeplitz[buffer, j * HALF : (j + 1) * HALF, c * SPAN : (c + 1) * SPAN] = (
                    moved.astype(jnp.bfloat16)
                )
        for c in range(3):
            for e in range(2):
                for v in range(SPAN // LANES):
                    at = c * SPAN + v * LANES
                    windows[buffer, e * rows : (e + 1) * rows, at : at + LANES] = shifts[
                        c, e, v : v + rows, :
                    ].astype(jnp.bfloat16)

    def combine(group, station, buffer):
        product = lax.dot_general(
            windows[buffer],
            toeplitz[buffer],
            (((1,), (1,)), ((), ())),
            preferred_element_type=jnp.float32,
        )
        weight = []
        for j in range(SLOTS):
            row = source[order_ref[group] * SLOTS + j] * stations + station
            weight.append(norms[pl.ds(row, 1), :])
        for p in range(SLOTS // 2):
            both = jnp.where(low, weight[2 * p], weight[2 * p + 1])
            at = p * LANES
            for e in range(2):
                term = product[e * rows : (e + 1) * rows, at : at + LANES]
                term = term * (scales[buffer, e] * both)
                if station:
                    term = term + share[e, :, at : at + LANES]
                share[e, :, at : at + LANES] = term

    def group_term(group, carry):
        later = lax.min(group + 1, n_group - 1)
        for station in range(stations):
            if station < stations - 1:
                prepare(group, station + 1, (station + 1) % 2)
            else:
                prepare(later, 0, (station + 1) % 2)
            combine(group, station, station % 2)
        for j in range(SLOTS):
            at = (j // 2) * LANES
            first = share[0, :, at : at + LANES]
            second = share[1, :, at : at + LANES]
            if j % 2 == 0:
                whole = jnp.where(low, first, pltpu.roll(second, HALF, 1))
            else:
                whole = jnp.where(low, pltpu.roll(first, HALF, 1), second)
            r = home[order_ref[group] * SLOTS + j]
            total[r] = total[r] + whole
        return carry

    prepare(0, 0, 0)
    lax.fori_loop(0, n_group, group_term, 0)
    if factor is None:
        out_ref[...] = total[...]
        return
    for r in range(block):
        turned[:, r, :] = total[r] * factor
    n_out, _, samples = out_ref.shape
    for w in range(n_out):
        for i in range(samples // LANES):
            out_ref[w, :, i * LANES : (i + 1) * LANES] = turned[w * (samples // LANES) + i]


def detect(order, groups, templates, pieces, before, n_all, padded, parts, factor):
    block, spread = groups.shape
    stations = 4
    slots = block * spread * stations
    rows = padded - 8
    samples = rows * LANES // parts
    spare = -(-(slots + stations) // 8) * 8
    if factor is None:
        out_shape = jax.ShapeDtypeStruct((block + 1, rows, LANES), jnp.float32)
    else:
        out_shape = jax.ShapeDtypeStruct((parts, block, samples), jnp.float32)
    operands = [order, groups, templates, *pieces]
    spaces = [pltpu.SMEM, pltpu.SMEM] + [pltpu.VMEM] * (1 + len(pieces))
    if before is not None:
        operands.append(before)
        spaces.append(pltpu.VMEM)

    def body(*refs):
        end = 3 + len(pieces)
        taken = refs[end] if before is not None else None
        rest = refs[end + (before is not None) :]
        detect_kernel(padded, factor, *refs[:3], refs[3:end], taken, *rest)

    return pl.pallas_call(
        body,
        out_shape=out_shape,
        in_specs=[pl.BlockSpec(memory_space=space) for space in spaces],
        out_specs=pl.BlockSpec(memory_space=pltpu.VMEM),
        scratch_shapes=[
            pltpu.SMEM((n_all * SLOTS,), jnp.int32),
            pltpu.SMEM((n_all * SLOTS,), jnp.int32),
            pltpu.SMEM((n_all,), jnp.int32),
            pltpu.VMEM((len(pieces),) + pieces[0].shape, jnp.bfloat16),
            pltpu.VMEM((slots * 3 * L // LANES, LANES), jnp.float32),
            pltpu.VMEM((spare, 3 * SPAN), jnp.float32),
            pltpu.VMEM((spare, LANES), jnp.float32),
            pltpu.VMEM((3 * LANES, LANES), jnp.bfloat16),
            pltpu.VMEM((3, 2, padded + 8, LANES), jnp.float32),
            pltpu.VMEM((padded, LANES), jnp.float32),
            pltpu.VMEM((2, 2, rows, LANES), jnp.float32),
            pltpu.VMEM((2, 2 * rows, 3 * SPAN), jnp.bfloat16),
            pltpu.VMEM((2, SLOTS * HALF, 3 * SPAN), jnp.bfloat16),
            pltpu.VMEM((2, rows, SLOTS * HALF), jnp.float32),
            pltpu.VMEM((block + 1, rows, LANES), jnp.float32),
            pltpu.VMEM((rows, block, LANES), jnp.float32),
        ],
        compiler_params=pltpu.CompilerParams(vmem_limit_bytes=32 * 1024 * 1024),
        cost_estimate=pl.CostEstimate(
            flops=16 * len(pieces) * stations * 2 * rows * 3 * SPAN * SLOTS * HALF,
            bytes_accessed=templates.size * 2 + 4 * block * rows * LANES,
            transcendentals=0,
        ),
    )(*operands)


def copies_to(value, axis, groups=None):
    count = len(groups[0]) if groups else lax.axis_size(axis)
    spread = jnp.broadcast_to(value[None], (count,) + value.shape)
    return lax.all_to_all(spread, axis, 0, 0, axis_index_groups=groups, tiled=True)


def on_device(record, templates, template_groups):
    channels, stations, samples = record.shape
    n_tm, n_sta = lax.axis_size("tm"), lax.axis_size("sta")
    m, s = lax.axis_index("tm"), lax.axis_index("sta")
    n_a = n_sta
    n_b = n_tm // n_a
    near = [[a * n_b + b for b in range(n_b)] for a in range(n_a)]
    far = [[a * n_b + b for a in range(n_a)] for b in range(n_b)]
    spread = template_groups.shape[1]

    turn = [
        ((a * n_b + b) * n_sta + t, (t * n_b + b) * n_sta + a)
        for a in range(n_a)
        for b in range(n_b)
        for t in range(n_sta)
    ]
    own = lax.ppermute(templates.reshape(-1, LANES), ("tm", "sta"), turn)
    first = (s * n_b + lax.rem(m, n_b)) * n_a
    groups = lax.dynamic_slice_in_dim(template_groups, first, n_a, 0)

    lines = channels * stations
    steps = samples // LANES
    around = copies_to(record.reshape(lines * steps, LANES), "tm", near)
    front = around[0].reshape(lines, steps, LANES)[:, : L // LANES]
    tail = lax.ppermute(front, "tm", [(i + n_b, i) for i in range(n_tm - n_b)])
    tail, own = lax.optimization_barrier((tail, own))
    block = copies_to(own, "tm", far)
    main = around.reshape(n_b, lines, steps, LANES)
    main = main.transpose(1, 0, 2, 3).reshape(lines, n_b * steps, LANES)
    rest = jnp.zeros((lines, 8 - L // LANES, LANES), record.dtype)
    padded = n_b * steps + 8
    mine = jnp.concatenate([main, tail, rest], axis=1).reshape(-1, LANES)

    cores = 2
    n_y = n_sta // cores
    y, core = s // cores, lax.rem(s, cores)
    pieces = [mine]
    for k in range(1, n_y):
        pairs = [(t, (t + k * cores) % n_sta) for t in range(n_sta)]
        pieces.append(lax.ppermute(mine, "sta", pairs))
    swap = [(t, t ^ 1) for t in range(n_sta)]
    others = [lax.ppermute(value, "sta", swap) for value in pieces]
    rows_of_y = lax.rem(y - jnp.arange(n_y, dtype=jnp.int32) + n_y, n_y) * cores
    factor = math.sqrt(channels * L / (spread * stations))
    total = detect(rows_of_y + core, groups, block, pieces, None, n_sta, padded, n_b, None)
    total = detect(rows_of_y + 1 - core, groups, block, others, total, n_sta, padded, n_b, factor)

    found = lax.all_to_all(total, "tm", 0, 0, axis_index_groups=near, tiled=True)
    return found.reshape(n_b * n_a, samples)


def solution(mesh):
    return jax.shard_map(
        on_device,
        mesh=mesh,
        in_specs=(P(None, "sta", "tm"), P(("tm", "sta"), None, None, None), P()),
        out_specs=P("sta", "tm"),
        check_vma=False,
    )
```

```python
import math

import jax
import jax.numpy as jnp
from jax import lax
from jax.experimental import pallas as pl
from jax.experimental.pallas import tpu as pltpu
from jax.sharding import PartitionSpec as P

L = 512
LANES = 128
HALF = 64
SPAN = L + LANES
SLOTS = 4
epsilon = 1e-06


def detect_kernel(
    padded,
    factor,
    order_ref,
    groups_ref,
    templates_ref,
    series_ref,
    before_ref,
    out_ref,
    source,
    home,
    count,
    wide,
    waves,
    norms,
    band,
    shifts,
    energy,
    scales,
    windows,
    toeplitz,
    share,
    total,
    turned,
):
    block, spread = groups_ref.shape
    n_group = series_ref.shape[0]
    rows = total.shape[1]
    parts = 3 * L // LANES
    slots = wide.shape[0] // parts
    stations = slots // (block * spread)
    lane = lax.broadcasted_iota(jnp.int32, (1, LANES), 1)
    low = lane < HALF

    def clear(n, carry):
        source[n] = block * spread
        home[n] = block
        return carry

    lax.fori_loop(0, source.shape[0], clear, 0)
    for n in range(count.shape[0]):
        count[n] = 0
    for r in range(block):
        for i in range(spread):
            named = groups_ref[r, i]
            slot = named * SLOTS + count[named]
            source[slot] = r * spread + i
            home[slot] = r
            count[named] = count[named] + 1
    spare = waves.shape[0] - slots
    for r in range(block):
        each = slots // block * parts
        wide[r * each : (r + 1) * each, :] = templates_ref[r, -each:, :].astype(jnp.float32)
    for c in range(3):
        for v in range(L // LANES):
            at = c * SPAN + v * LANES
            waves[0:slots, at : at + LANES] = wide[pl.ds(c * L // LANES + v, slots, parts), :]
        waves[0:slots, c * SPAN + L : (c + 1) * SPAN] = jnp.zeros((slots, LANES), jnp.float32)
    waves[slots:, :] = jnp.zeros((spare, 3 * SPAN), jnp.float32)
    squares = jnp.sum(jnp.square(waves[0:slots, :]), axis=1, keepdims=True)
    norms[0:slots, :] = jnp.broadcast_to(lax.rsqrt(squares + epsilon), (slots, LANES))
    norms[slots:, :] = jnp.zeros((spare, LANES), jnp.float32)
    r = lax.broadcasted_iota(jnp.int32, (LANES, LANES), 0)
    l = lax.broadcasted_iota(jnp.int32, (LANES, LANES), 1)
    band[0:LANES, :] = jnp.where(r >= l, 1.0, 0.0).astype(jnp.bfloat16)
    band[LANES : 2 * LANES, :] = jnp.ones((LANES, LANES), jnp.bfloat16)
    band[2 * LANES :, :] = jnp.where(r < l, 1.0, 0.0).astype(jnp.bfloat16)
    shifts[:, :, padded:, :] = jnp.zeros((3, 2, 8, LANES), jnp.float32)
    if before_ref is None:
        total[...] = jnp.zeros_like(total)
    else:
        total[...] = before_ref[...]

    def prepare(group, station, buffer):
        squares = jnp.zeros((padded, LANES), jnp.float32)
        for c in range(3):
            at = (c * stations + station) * padded
            plain = series_ref[group, at : at + padded, :].astype(jnp.float32)
            squares = squares + plain * plain
            shifts[c, 0, 0:padded, :] = plain
            after = shifts[c, 0, 1 : padded + 1, :]
            shifts[c, 1, 0:padded, :] = pltpu.roll(jnp.where(low, after, plain), HALF, 1)
        energy[...] = squares
        middle = energy[1 : rows + 1, :] + energy[2 : rows + 2, :] + energy[3 : rows + 3, :]
        pieces = jnp.concatenate([energy[0:rows, :], middle, energy[4 : rows + 4, :]], axis=1)
        coarse = pieces.astype(jnp.bfloat16)
        fine = (pieces - coarse.astype(jnp.float32)).astype(jnp.bfloat16)
        window_energy = jnp.dot(coarse, band[...], preferred_element_type=jnp.float32)
        window_energy += jnp.dot(fine, band[...], preferred_element_type=jnp.float32)
        scale = lax.rsqrt(window_energy + epsilon)
        other = pltpu.roll(scale, HALF, 1)
        scales[buffer, 0] = jnp.where(low, scale, other)
        scales[buffer, 1] = jnp.where(low, other, scale)
        for j in range(SLOTS):
            row = source[order_ref[group] * SLOTS + j] * stations + station
            for c in range(3):
                wave = waves[pl.ds(row, 1), c * SPAN : (c + 1) * SPAN]
                moved = pltpu.roll(
                    jnp.broadcast_to(wave, (HALF, SPAN)), 0, 1, stride=1, stride_axis=0
                )
                toeplitz[buffer, j * HALF : (j + 1) * HALF, c * SPAN : (c + 1) * SPAN] = (
                    moved.astype(jnp.bfloat16)
                )
        for c in range(3):
            for e in range(2):
                for v in range(SPAN // LANES):
                    at = c * SPAN + v * LANES
                    windows[buffer, e * rows : (e + 1) * rows, at : at + LANES] = shifts[
                        c, e, v : v + rows, :
                    ].astype(jnp.bfloat16)

    def combine(group, station, buffer):
        product = lax.dot_general(
            windows[buffer],
            toeplitz[buffer],
            (((1,), (1,)), ((), ())),
            preferred_element_type=jnp.float32,
        )
        weight = []
        for j in range(SLOTS):
            row = source[order_ref[group] * SLOTS + j] * stations + station
            weight.append(norms[pl.ds(row, 1), :])
        for p in range(SLOTS // 2):
            both = jnp.where(low, weight[2 * p], weight[2 * p + 1])
            at = p * LANES
            for e in range(2):
                term = product[e * rows : (e + 1) * rows, at : at + LANES]
                term = term * (scales[buffer, e] * both)
                if station:
                    term = term + share[e, :, at : at + LANES]
                share[e, :, at : at + LANES] = term

    def group_term(group, carry):
        later = lax.min(group + 1, n_group - 1)
        for station in range(stations):
            if station < stations - 1:
                prepare(group, station + 1, (station + 1) % 2)
            else:
                prepare(later, 0, (station + 1) % 2)
            combine(group, station, station % 2)
        for j in range(SLOTS):
            at = (j // 2) * LANES
            first = share[0, :, at : at + LANES]
            second = share[1, :, at : at + LANES]
            if j % 2 == 0:
                whole = jnp.where(low, first, pltpu.roll(second, HALF, 1))
            else:
                whole = jnp.where(low, pltpu.roll(first, HALF, 1), second)
            r = home[order_ref[group] * SLOTS + j]
            total[r] = total[r] + whole
        return carry

    prepare(0, 0, 0)
    lax.fori_loop(0, n_group, group_term, 0)
    if factor is None:
        out_ref[...] = total[...]
        return
    for r in range(block):
        turned[:, r, :] = total[r] * factor
    n_out, _, samples = out_ref.shape
    for w in range(n_out):
        for i in range(samples // LANES):
            out_ref[w, :, i * LANES : (i + 1) * LANES] = turned[w * (samples // LANES) + i]


def detect(order, groups, templates, series, before, n_all, padded, parts, factor):
    block, spread = groups.shape
    stations = 4
    slots = block * spread * stations
    rows = padded - 8
    samples = rows * LANES // parts
    spare = -(-(slots + stations) // 8) * 8
    if factor is None:
        out_shape = jax.ShapeDtypeStruct((block + 1, rows, LANES), jnp.float32)
    else:
        out_shape = jax.ShapeDtypeStruct((parts, block, samples), jnp.float32)
    operands = [order, groups, templates, series]
    spaces = [pltpu.SMEM, pltpu.SMEM, pltpu.VMEM, pltpu.VMEM]
    if before is not None:
        operands.append(before)
        spaces.append(pltpu.VMEM)

    def body(*refs):
        refs = list(refs)
        if before is None:
            refs.insert(4, None)
        detect_kernel(padded, factor, *refs)

    return pl.pallas_call(
        body,
        out_shape=out_shape,
        in_specs=[pl.BlockSpec(memory_space=space) for space in spaces],
        out_specs=pl.BlockSpec(memory_space=pltpu.VMEM),
        scratch_shapes=[
            pltpu.SMEM((n_all * SLOTS,), jnp.int32),
            pltpu.SMEM((n_all * SLOTS,), jnp.int32),
            pltpu.SMEM((n_all,), jnp.int32),
            pltpu.VMEM((slots * 3 * L // LANES, LANES), jnp.float32),
            pltpu.VMEM((spare, 3 * SPAN), jnp.float32),
            pltpu.VMEM((spare, LANES), jnp.float32),
            pltpu.VMEM((3 * LANES, LANES), jnp.bfloat16),
            pltpu.VMEM((3, 2, padded + 8, LANES), jnp.float32),
            pltpu.VMEM((padded, LANES), jnp.float32),
            pltpu.VMEM((2, 2, rows, LANES), jnp.float32),
            pltpu.VMEM((2, 2 * rows, 3 * SPAN), jnp.bfloat16),
            pltpu.VMEM((2, SLOTS * HALF, 3 * SPAN), jnp.bfloat16),
            pltpu.VMEM((2, rows, SLOTS * HALF), jnp.float32),
            pltpu.VMEM((block + 1, rows, LANES), jnp.float32),
            pltpu.VMEM((rows, block, LANES), jnp.float32),
        ],
        compiler_params=pltpu.CompilerParams(vmem_limit_bytes=32 * 1024 * 1024),
        cost_estimate=pl.CostEstimate(
            flops=16 * series.shape[0] * stations * 2 * rows * 3 * SPAN * SLOTS * HALF,
            bytes_accessed=templates.size * 2 + 4 * block * rows * LANES,
            transcendentals=0,
        ),
    )(*operands)


def copies_to(value, axis, groups=None):
    count = len(groups[0]) if groups else lax.axis_size(axis)
    spread = jnp.broadcast_to(value[None], (count,) + value.shape)
    return lax.all_to_all(spread, axis, 0, 0, axis_index_groups=groups, tiled=True)


def on_device(record, templates, template_groups):
    channels, stations, samples = record.shape
    n_tm, n_sta = lax.axis_size("tm"), lax.axis_size("sta")
    m, s = lax.axis_index("tm"), lax.axis_index("sta")
    n_a = n_sta
    n_b = n_tm // n_a
    near = [[a * n_b + b for b in range(n_b)] for a in range(n_a)]
    far = [[a * n_b + b for a in range(n_a)] for b in range(n_b)]
    spread = template_groups.shape[1]

    turn = [
        ((a * n_b + b) * n_sta + t, (t * n_b + b) * n_sta + a)
        for a in range(n_a)
        for b in range(n_b)
        for t in range(n_sta)
    ]
    own = lax.ppermute(templates.reshape(-1, LANES), ("tm", "sta"), turn)
    first = (s * n_b + lax.rem(m, n_b)) * n_a
    groups = lax.dynamic_slice_in_dim(template_groups, first, n_a, 0)

    lines = channels * stations
    steps = samples // LANES
    around = copies_to(record.reshape(lines * steps, LANES), "tm", near)
    around, own = lax.optimization_barrier((around, own))
    front = around[0].reshape(lines, steps, LANES)[:, : L // LANES]
    tail = lax.ppermute(front, "tm", [(i + n_b, i) for i in range(n_tm - n_b)])
    block = copies_to(own, "tm", far)
    main = around.reshape(n_b, lines, steps, LANES)
    main = main.transpose(1, 0, 2, 3).reshape(lines, n_b * steps, LANES)
    rest = jnp.zeros((lines, 8 - L // LANES, LANES), record.dtype)
    padded = n_b * steps + 8
    mine = jnp.concatenate([main, tail, rest], axis=1).reshape(-1, LANES)

    cores = 2
    n_y = n_sta // cores
    y, core = s // cores, lax.rem(s, cores)
    pieces = [mine]
    for k in range(1, n_y):
        pairs = [(t, (t + k * cores) % n_sta) for t in range(n_sta)]
        pieces.append(lax.ppermute(mine, "sta", pairs))
    swap = [(t, t ^ 1) for t in range(n_sta)]
    pieces = jnp.stack(pieces)
    others = lax.ppermute(pieces, "sta", swap)
    rows_of_y = lax.rem(y - jnp.arange(n_y, dtype=jnp.int32) + n_y, n_y) * cores
    factor = math.sqrt(channels * L / (spread * stations))
    total = detect(rows_of_y + core, groups, block, pieces, None, n_sta, padded, n_b, None)
    total = detect(rows_of_y + 1 - core, groups, block, others, total, n_sta, padded, n_b, factor)

    found = lax.all_to_all(total, "tm", 0, 0, axis_index_groups=near, tiled=True)
    return found.reshape(n_b * n_a, samples)


def solution(mesh):
    return jax.shard_map(
        on_device,
        mesh=mesh,
        in_specs=(P(None, "sta", "tm"), P(("tm", "sta"), None, None, None), P()),
        out_specs=P("sta", "tm"),
        check_vma=False,
    )
```

```python
import math

import jax
import jax.numpy as jnp
from jax import lax
from jax.experimental import pallas as pl
from jax.experimental.pallas import tpu as pltpu
from jax.sharding import PartitionSpec as P

L = 512
LANES = 128
HALF = 64
SPAN = L + LANES
SLOTS = 4
epsilon = 1e-06


def detect_kernel(
    padded,
    factor,
    order_ref,
    groups_ref,
    templates_ref,
    series_ref,
    before_ref,
    out_ref,
    source,
    home,
    count,
    wide,
    waves,
    norms,
    band,
    shifts,
    energy,
    scales,
    windows,
    toeplitz,
    share,
    total,
    turned,
):
    block, spread = groups_ref.shape
    n_group = series_ref.shape[0]
    rows = total.shape[1]
    parts = 3 * L // LANES
    slots = wide.shape[0] // parts
    stations = slots // (block * spread)
    lane = lax.broadcasted_iota(jnp.int32, (1, LANES), 1)
    low = lane < HALF

    def clear(n, carry):
        source[n] = block * spread
        home[n] = block
        return carry

    lax.fori_loop(0, source.shape[0], clear, 0)
    for n in range(count.shape[0]):
        count[n] = 0
    for r in range(block):
        for i in range(spread):
            named = groups_ref[r, i]
            slot = named * SLOTS + count[named]
            source[slot] = r * spread + i
            home[slot] = r
            count[named] = count[named] + 1
    spare = waves.shape[0] - slots
    for r in range(block):
        each = slots // block * parts
        wide[r * each : (r + 1) * each, :] = templates_ref[r, -each:, :].astype(jnp.float32)
    for c in range(3):
        for v in range(L // LANES):
            at = c * SPAN + v * LANES
            waves[0:slots, at : at + LANES] = wide[pl.ds(c * L // LANES + v, slots, parts), :]
        waves[0:slots, c * SPAN + L : (c + 1) * SPAN] = jnp.zeros((slots, LANES), jnp.float32)
    waves[slots:, :] = jnp.zeros((spare, 3 * SPAN), jnp.float32)
    squares = jnp.sum(jnp.square(waves[0:slots, :]), axis=1, keepdims=True)
    norms[0:slots, :] = jnp.broadcast_to(lax.rsqrt(squares + epsilon), (slots, LANES))
    norms[slots:, :] = jnp.zeros((spare, LANES), jnp.float32)
    r = lax.broadcasted_iota(jnp.int32, (LANES, LANES), 0)
    l = lax.broadcasted_iota(jnp.int32, (LANES, LANES), 1)
    band[0:LANES, :] = jnp.where(r >= l, 1.0, 0.0).astype(jnp.bfloat16)
    band[LANES : 2 * LANES, :] = jnp.ones((LANES, LANES), jnp.bfloat16)
    band[2 * LANES :, :] = jnp.where(r < l, 1.0, 0.0).astype(jnp.bfloat16)
    shifts[:, :, padded:, :] = jnp.zeros((3, 2, 8, LANES), jnp.float32)
    if before_ref is None:
        total[...] = jnp.zeros_like(total)
    else:
        total[...] = before_ref[...]

    def prepare(group, station, buffer):
        squares = jnp.zeros((padded, LANES), jnp.float32)
        for c in range(3):
            at = (c * stations + station) * padded
            plain = series_ref[group, at : at + padded, :].astype(jnp.float32)
            squares = squares + plain * plain
            shifts[c, 0, 0:padded, :] = plain
            after = shifts[c, 0, 1 : padded + 1, :]
            shifts[c, 1, 0:padded, :] = pltpu.roll(jnp.where(low, after, plain), HALF, 1)
        energy[...] = squares
        middle = energy[1 : rows + 1, :] + energy[2 : rows + 2, :] + energy[3 : rows + 3, :]
        pieces = jnp.concatenate([energy[0:rows, :], middle, energy[4 : rows + 4, :]], axis=1)
        coarse = pieces.astype(jnp.bfloat16)
        fine = (pieces - coarse.astype(jnp.float32)).astype(jnp.bfloat16)
        window_energy = jnp.dot(coarse, band[...], preferred_element_type=jnp.float32)
        window_energy += jnp.dot(fine, band[...], preferred_element_type=jnp.float32)
        scale = lax.rsqrt(window_energy + epsilon)
        other = pltpu.roll(scale, HALF, 1)
        scales[buffer, 0] = jnp.where(low, scale, other)
        scales[buffer, 1] = jnp.where(low, other, scale)
        for j in range(SLOTS):
            row = source[order_ref[group] * SLOTS + j] * stations + station
            for c in range(3):
                wave = waves[pl.ds(row, 1), c * SPAN : (c + 1) * SPAN]
                moved = pltpu.roll(
                    jnp.broadcast_to(wave, (HALF, SPAN)), 0, 1, stride=1, stride_axis=0
                )
                toeplitz[buffer, j * HALF : (j + 1) * HALF, c * SPAN : (c + 1) * SPAN] = (
                    moved.astype(jnp.bfloat16)
                )
        for c in range(3):
            for e in range(2):
                for v in range(SPAN // LANES):
                    at = c * SPAN + v * LANES
                    windows[buffer, e * rows : (e + 1) * rows, at : at + LANES] = shifts[
                        c, e, v : v + rows, :
                    ].astype(jnp.bfloat16)

    def combine(group, station, buffer):
        product = lax.dot_general(
            windows[buffer],
            toeplitz[buffer],
            (((1,), (1,)), ((), ())),
            preferred_element_type=jnp.float32,
        )
        weight = []
        for j in range(SLOTS):
            row = source[order_ref[group] * SLOTS + j] * stations + station
            weight.append(norms[pl.ds(row, 1), :])
        for p in range(SLOTS // 2):
            both = jnp.where(low, weight[2 * p], weight[2 * p + 1])
            at = p * LANES
            for e in range(2):
                term = product[e * rows : (e + 1) * rows, at : at + LANES]
                term = term * (scales[buffer, e] * both)
                if station:
                    term = term + share[e, :, at : at + LANES]
                share[e, :, at : at + LANES] = term

    def group_term(group, carry):
        later = lax.min(group + 1, n_group - 1)
        for station in range(stations):
            if station < stations - 1:
                prepare(group, station + 1, (station + 1) % 2)
            else:
                prepare(later, 0, (station + 1) % 2)
            combine(group, station, station % 2)
        for j in range(SLOTS):
            at = (j // 2) * LANES
            first = share[0, :, at : at + LANES]
            second = share[1, :, at : at + LANES]
            if j % 2 == 0:
                whole = jnp.where(low, first, pltpu.roll(second, HALF, 1))
            else:
                whole = jnp.where(low, pltpu.roll(first, HALF, 1), second)
            r = home[order_ref[group] * SLOTS + j]
            total[r] = total[r] + whole
        return carry

    prepare(0, 0, 0)
    lax.fori_loop(0, n_group, group_term, 0)
    if factor is None:
        out_ref[...] = total[...]
        return
    for r in range(block):
        turned[:, r, :] = total[r] * factor
    n_out, _, samples = out_ref.shape
    for w in range(n_out):
        for i in range(samples // LANES):
            out_ref[w, :, i * LANES : (i + 1) * LANES] = turned[w * (samples // LANES) + i]


def detect(order, groups, templates, series, before, n_all, padded, parts, factor):
    block, spread = groups.shape
    stations = 4
    slots = block * spread * stations
    rows = padded - 8
    samples = rows * LANES // parts
    spare = -(-(slots + stations) // 8) * 8
    if factor is None:
        out_shape = jax.ShapeDtypeStruct((block + 1, rows, LANES), jnp.float32)
    else:
        out_shape = jax.ShapeDtypeStruct((parts, block, samples), jnp.float32)
    operands = [order, groups, templates, series]
    spaces = [pltpu.SMEM, pltpu.SMEM, pltpu.VMEM, pltpu.VMEM]
    if before is not None:
        operands.append(before)
        spaces.append(pltpu.VMEM)

    def body(*refs):
        refs = list(refs)
        if before is None:
            refs.insert(4, None)
        detect_kernel(padded, factor, *refs)

    return pl.pallas_call(
        body,
        out_shape=out_shape,
        in_specs=[pl.BlockSpec(memory_space=space) for space in spaces],
        out_specs=pl.BlockSpec(memory_space=pltpu.VMEM),
        scratch_shapes=[
            pltpu.SMEM((n_all * SLOTS,), jnp.int32),
            pltpu.SMEM((n_all * SLOTS,), jnp.int32),
            pltpu.SMEM((n_all,), jnp.int32),
            pltpu.VMEM((slots * 3 * L // LANES, LANES), jnp.float32),
            pltpu.VMEM((spare, 3 * SPAN), jnp.float32),
            pltpu.VMEM((spare, LANES), jnp.float32),
            pltpu.VMEM((3 * LANES, LANES), jnp.bfloat16),
            pltpu.VMEM((3, 2, padded + 8, LANES), jnp.float32),
            pltpu.VMEM((padded, LANES), jnp.float32),
            pltpu.VMEM((2, 2, rows, LANES), jnp.float32),
            pltpu.VMEM((2, 2 * rows, 3 * SPAN), jnp.bfloat16),
            pltpu.VMEM((2, SLOTS * HALF, 3 * SPAN), jnp.bfloat16),
            pltpu.VMEM((2, rows, SLOTS * HALF), jnp.float32),
            pltpu.VMEM((block + 1, rows, LANES), jnp.float32),
            pltpu.VMEM((rows, block, LANES), jnp.float32),
        ],
        compiler_params=pltpu.CompilerParams(vmem_limit_bytes=32 * 1024 * 1024),
        cost_estimate=pl.CostEstimate(
            flops=16 * series.shape[0] * stations * 2 * rows * 3 * SPAN * SLOTS * HALF,
            bytes_accessed=templates.size * 2 + 4 * block * rows * LANES,
            transcendentals=0,
        ),
    )(*operands)


def copies_to(value, axis, groups=None):
    count = len(groups[0]) if groups else lax.axis_size(axis)
    spread = jnp.broadcast_to(value[None], (count,) + value.shape)
    return lax.all_to_all(spread, axis, 0, 0, axis_index_groups=groups, tiled=True)


def on_device(record, templates, template_groups):
    channels, stations, samples = record.shape
    n_tm, n_sta = lax.axis_size("tm"), lax.axis_size("sta")
    m, s = lax.axis_index("tm"), lax.axis_index("sta")
    n_a = n_sta
    n_b = n_tm // n_a
    near = [[a * n_b + b for b in range(n_b)] for a in range(n_a)]
    far = [[a * n_b + b for a in range(n_a)] for b in range(n_b)]
    spread = template_groups.shape[1]

    turn = [
        ((a * n_b + b) * n_sta + t, (t * n_b + b) * n_sta + a)
        for a in range(n_a)
        for b in range(n_b)
        for t in range(n_sta)
    ]
    own = lax.ppermute(templates.reshape(-1, LANES), ("tm", "sta"), turn)
    first = (s * n_b + lax.rem(m, n_b)) * n_a
    groups = lax.dynamic_slice_in_dim(template_groups, first, n_a, 0)

    lines = channels * stations
    steps = samples // LANES
    around = copies_to(record.reshape(lines * steps, LANES), "tm", near)
    front = around[0].reshape(lines, steps, LANES)[:, : L // LANES]
    tail = lax.ppermute(front, "tm", [(i + n_b, i) for i in range(n_tm - n_b)])
    tail, own = lax.optimization_barrier((tail, own))
    block = copies_to(own, "tm", far)
    main = around.reshape(n_b, lines, steps, LANES)
    main = main.transpose(1, 0, 2, 3).reshape(lines, n_b * steps, LANES)
    rest = jnp.zeros((lines, 8 - L // LANES, LANES), record.dtype)
    padded = n_b * steps + 8
    mine = jnp.concatenate([main, tail, rest], axis=1).reshape(-1, LANES)

    cores = 2
    n_y = n_sta // cores
    y, core = s // cores, lax.rem(s, cores)
    pieces = [mine]
    for k in range(1, n_y):
        pairs = [(t, (t + k * cores) % n_sta) for t in range(n_sta)]
        pieces.append(lax.ppermute(mine, "sta", pairs))
    swap = [(t, t ^ 1) for t in range(n_sta)]
    pieces = jnp.stack(pieces)
    others = lax.ppermute(pieces, "sta", swap)
    rows_of_y = lax.rem(y - jnp.arange(n_y, dtype=jnp.int32) + n_y, n_y) * cores
    factor = math.sqrt(channels * L / (spread * stations))
    total = detect(rows_of_y + core, groups, block, pieces, None, n_sta, padded, n_b, None)
    total = detect(rows_of_y + 1 - core, groups, block, others, total, n_sta, padded, n_b, factor)

    found = lax.all_to_all(total, "tm", 0, 0, axis_index_groups=near, tiled=True)
    return found.reshape(n_b * n_a, samples)


def solution(mesh):
    return jax.shard_map(
        on_device,
        mesh=mesh,
        in_specs=(P(None, "sta", "tm"), P(("tm", "sta"), None, None, None), P()),
        out_specs=P("sta", "tm"),
        check_vma=False,
    )
```

```python
import math

import jax
import jax.numpy as jnp
from jax import lax
from jax.experimental import pallas as pl
from jax.experimental.pallas import tpu as pltpu
from jax.sharding import PartitionSpec as P

L = 512
LANES = 128
HALF = 64
SPAN = L + LANES
SLOTS = 4
epsilon = 1e-06


def detect_kernel(
    padded,
    factor,
    order_ref,
    groups_ref,
    templates_ref,
    series_ref,
    before_ref,
    out_ref,
    source,
    home,
    count,
    wide,
    waves,
    norms,
    band,
    shifts,
    energy,
    scales,
    windows,
    toeplitz,
    share,
    total,
    turned,
):
    block, spread = groups_ref.shape
    n_group = series_ref.shape[0]
    rows = total.shape[1]
    parts = 3 * L // LANES
    slots = wide.shape[0] // parts
    stations = slots // (block * spread)
    lane = lax.broadcasted_iota(jnp.int32, (1, LANES), 1)
    low = lane < HALF

    def clear(n, carry):
        source[n] = block * spread
        home[n] = block
        return carry

    lax.fori_loop(0, source.shape[0], clear, 0)
    for n in range(count.shape[0]):
        count[n] = 0
    for r in range(block):
        for i in range(spread):
            named = groups_ref[r, i]
            slot = named * SLOTS + count[named]
            source[slot] = r * spread + i
            home[slot] = r
            count[named] = count[named] + 1
    spare = waves.shape[0] - slots
    for r in range(block):
        each = slots // block * parts
        wide[r * each : (r + 1) * each, :] = templates_ref[r, -each:, :].astype(jnp.float32)
    for c in range(3):
        for v in range(L // LANES):
            at = c * SPAN + v * LANES
            waves[0:slots, at : at + LANES] = wide[pl.ds(c * L // LANES + v, slots, parts), :]
        waves[0:slots, c * SPAN + L : (c + 1) * SPAN] = jnp.zeros((slots, LANES), jnp.float32)
    waves[slots:, :] = jnp.zeros((spare, 3 * SPAN), jnp.float32)
    squares = jnp.sum(jnp.square(waves[0:slots, :]), axis=1, keepdims=True)
    norms[0:slots, :] = jnp.broadcast_to(lax.rsqrt(squares + epsilon), (slots, LANES))
    norms[slots:, :] = jnp.zeros((spare, LANES), jnp.float32)
    r = lax.broadcasted_iota(jnp.int32, (LANES, LANES), 0)
    l = lax.broadcasted_iota(jnp.int32, (LANES, LANES), 1)
    band[0:LANES, :] = jnp.where(r >= l, 1.0, 0.0).astype(jnp.bfloat16)
    band[LANES : 2 * LANES, :] = jnp.ones((LANES, LANES), jnp.bfloat16)
    band[2 * LANES :, :] = jnp.where(r < l, 1.0, 0.0).astype(jnp.bfloat16)
    shifts[:, :, padded:, :] = jnp.zeros((3, 2, 8, LANES), jnp.float32)
    if before_ref is None:
        total[...] = jnp.zeros_like(total)
    else:
        total[...] = before_ref[...]

    def prepare(group, station, buffer):
        squares = jnp.zeros((padded, LANES), jnp.float32)
        for c in range(3):
            at = (c * stations + station) * padded
            plain = series_ref[group, at : at + padded, :].astype(jnp.float32)
            squares = squares + plain * plain
            shifts[c, 0, 0:padded, :] = plain
            after = shifts[c, 0, 1 : padded + 1, :]
            shifts[c, 1, 0:padded, :] = pltpu.roll(jnp.where(low, after, plain), HALF, 1)
        energy[...] = squares
        middle = energy[1 : rows + 1, :] + energy[2 : rows + 2, :] + energy[3 : rows + 3, :]
        pieces = jnp.concatenate([energy[0:rows, :], middle, energy[4 : rows + 4, :]], axis=1)
        coarse = pieces.astype(jnp.bfloat16)
        fine = (pieces - coarse.astype(jnp.float32)).astype(jnp.bfloat16)
        window_energy = jnp.dot(coarse, band[...], preferred_element_type=jnp.float32)
        window_energy += jnp.dot(fine, band[...], preferred_element_type=jnp.float32)
        scale = lax.rsqrt(window_energy + epsilon)
        other = pltpu.roll(scale, HALF, 1)
        scales[buffer, 0] = jnp.where(low, scale, other)
        scales[buffer, 1] = jnp.where(low, other, scale)
        for j in range(SLOTS):
            row = source[order_ref[group] * SLOTS + j] * stations + station
            for c in range(3):
                wave = waves[pl.ds(row, 1), c * SPAN : (c + 1) * SPAN]
                moved = pltpu.roll(
                    jnp.broadcast_to(wave, (HALF, SPAN)), 0, 1, stride=1, stride_axis=0
                )
                toeplitz[buffer, j * HALF : (j + 1) * HALF, c * SPAN : (c + 1) * SPAN] = (
                    moved.astype(jnp.bfloat16)
                )
        for c in range(3):
            for e in range(2):
                for v in range(SPAN // LANES):
                    at = c * SPAN + v * LANES
                    windows[buffer, e * rows : (e + 1) * rows, at : at + LANES] = shifts[
                        c, e, v : v + rows, :
                    ].astype(jnp.bfloat16)

    def combine(group, station, buffer):
        product = lax.dot_general(
            windows[buffer],
            toeplitz[buffer],
            (((1,), (1,)), ((), ())),
            preferred_element_type=jnp.float32,
        )
        weight = []
        for j in range(SLOTS):
            row = source[order_ref[group] * SLOTS + j] * stations + station
            weight.append(norms[pl.ds(row, 1), :])
        for p in range(SLOTS // 2):
            both = jnp.where(low, weight[2 * p], weight[2 * p + 1])
            at = p * LANES
            for e in range(2):
                term = product[e * rows : (e + 1) * rows, at : at + LANES]
                term = term * (scales[buffer, e] * both)
                if station:
                    term = term + share[e, :, at : at + LANES]
                share[e, :, at : at + LANES] = term

    def group_term(group, carry):
        later = lax.min(group + 1, n_group - 1)
        for station in range(stations):
            if station < stations - 1:
                prepare(group, station + 1, (station + 1) % 2)
            else:
                prepare(later, 0, (station + 1) % 2)
            combine(group, station, station % 2)
        for j in range(SLOTS):
            at = (j // 2) * LANES
            first = share[0, :, at : at + LANES]
            second = share[1, :, at : at + LANES]
            if j % 2 == 0:
                whole = jnp.where(low, first, pltpu.roll(second, HALF, 1))
            else:
                whole = jnp.where(low, pltpu.roll(first, HALF, 1), second)
            r = home[order_ref[group] * SLOTS + j]
            total[r] = total[r] + whole
        return carry

    prepare(0, 0, 0)
    lax.fori_loop(0, n_group, group_term, 0)
    if factor is None:
        out_ref[...] = total[...]
        return
    for r in range(block):
        turned[:, r, :] = total[r] * factor
    n_out, _, samples = out_ref.shape
    for w in range(n_out):
        for i in range(samples // LANES):
            out_ref[w, :, i * LANES : (i + 1) * LANES] = turned[w * (samples // LANES) + i]


def detect(order, groups, templates, series, before, n_all, padded, parts, factor):
    block, spread = groups.shape
    stations = 4
    slots = block * spread * stations
    rows = padded - 8
    samples = rows * LANES // parts
    spare = -(-(slots + stations) // 8) * 8
    if factor is None:
        out_shape = jax.ShapeDtypeStruct((block + 1, rows, LANES), jnp.float32)
    else:
        out_shape = jax.ShapeDtypeStruct((parts, block, samples), jnp.float32)
    operands = [order, groups, templates, series]
    spaces = [pltpu.SMEM, pltpu.SMEM, pltpu.VMEM, pltpu.VMEM]
    if before is not None:
        operands.append(before)
        spaces.append(pltpu.VMEM)

    def body(*refs):
        refs = list(refs)
        if before is None:
            refs.insert(4, None)
        detect_kernel(padded, factor, *refs)

    return pl.pallas_call(
        body,
        out_shape=out_shape,
        in_specs=[pl.BlockSpec(memory_space=space) for space in spaces],
        out_specs=pl.BlockSpec(memory_space=pltpu.VMEM),
        scratch_shapes=[
            pltpu.SMEM((n_all * SLOTS,), jnp.int32),
            pltpu.SMEM((n_all * SLOTS,), jnp.int32),
            pltpu.SMEM((n_all,), jnp.int32),
            pltpu.VMEM((slots * 3 * L // LANES, LANES), jnp.float32),
            pltpu.VMEM((spare, 3 * SPAN), jnp.float32),
            pltpu.VMEM((spare, LANES), jnp.float32),
            pltpu.VMEM((3 * LANES, LANES), jnp.bfloat16),
            pltpu.VMEM((3, 2, padded + 8, LANES), jnp.float32),
            pltpu.VMEM((padded, LANES), jnp.float32),
            pltpu.VMEM((2, 2, rows, LANES), jnp.float32),
            pltpu.VMEM((2, 2 * rows, 3 * SPAN), jnp.bfloat16),
            pltpu.VMEM((2, SLOTS * HALF, 3 * SPAN), jnp.bfloat16),
            pltpu.VMEM((2, rows, SLOTS * HALF), jnp.float32),
            pltpu.VMEM((block + 1, rows, LANES), jnp.float32),
            pltpu.VMEM((rows, block, LANES), jnp.float32),
        ],
        compiler_params=pltpu.CompilerParams(vmem_limit_bytes=32 * 1024 * 1024),
        cost_estimate=pl.CostEstimate(
            flops=16 * series.shape[0] * stations * 2 * rows * 3 * SPAN * SLOTS * HALF,
            bytes_accessed=templates.size * 2 + 4 * block * rows * LANES,
            transcendentals=0,
        ),
    )(*operands)


def copies_to(value, axis, groups=None):
    count = len(groups[0]) if groups else lax.axis_size(axis)
    spread = jnp.broadcast_to(value[None], (count,) + value.shape)
    return lax.all_to_all(spread, axis, 0, 0, axis_index_groups=groups, tiled=True)


def on_device(record, templates, template_groups):
    channels, stations, samples = record.shape
    n_tm, n_sta = lax.axis_size("tm"), lax.axis_size("sta")
    m, s = lax.axis_index("tm"), lax.axis_index("sta")
    n_a = n_sta
    n_b = n_tm // n_a
    near = [[a * n_b + b for b in range(n_b)] for a in range(n_a)]
    far = [[a * n_b + b for a in range(n_a)] for b in range(n_b)]
    spread = template_groups.shape[1]

    first = (s * n_b + lax.rem(m, n_b)) * n_a
    groups = lax.dynamic_slice_in_dim(template_groups, first, n_a, 0)

    lines = channels * stations
    steps = samples // LANES
    around = copies_to(record.reshape(lines * steps, LANES), "tm", near)
    around, own = lax.optimization_barrier((around, templates.reshape(-1, LANES)))
    block = copies_to(own, "tm", far)
    block = lax.all_to_all(block, "sta", 0, 0, tiled=True)
    front = around[0].reshape(lines, steps, LANES)[:, : L // LANES]
    tail = lax.ppermute(front, "tm", [(i + n_b, i) for i in range(n_tm - n_b)])
    main = around.reshape(n_b, lines, steps, LANES)
    main = main.transpose(1, 0, 2, 3).reshape(lines, n_b * steps, LANES)
    rest = jnp.zeros((lines, 8 - L // LANES, LANES), record.dtype)
    padded = n_b * steps + 8
    mine = jnp.concatenate([main, tail, rest], axis=1).reshape(-1, LANES)

    cores = 2
    n_y = n_sta // cores
    y, core = s // cores, lax.rem(s, cores)
    pieces = [mine]
    for k in range(1, n_y):
        pairs = [(t, (t + k * cores) % n_sta) for t in range(n_sta)]
        pieces.append(lax.ppermute(mine, "sta", pairs))
    swap = [(t, t ^ 1) for t in range(n_sta)]
    pieces = jnp.stack(pieces)
    others = lax.ppermute(pieces, "sta", swap)
    rows_of_y = lax.rem(y - jnp.arange(n_y, dtype=jnp.int32) + n_y, n_y) * cores
    factor = math.sqrt(channels * L / (spread * stations))
    total = detect(rows_of_y + core, groups, block, pieces, None, n_sta, padded, n_b, None)
    total = detect(rows_of_y + 1 - core, groups, block, others, total, n_sta, padded, n_b, factor)

    found = lax.all_to_all(total, "tm", 0, 0, axis_index_groups=near, tiled=True)
    return found.reshape(n_b * n_a, samples)


def solution(mesh):
    return jax.shard_map(
        on_device,
        mesh=mesh,
        in_specs=(P(None, "sta", "tm"), P(("tm", "sta"), None, None, None), P()),
        out_specs=P("sta", "tm"),
        check_vma=False,
    )
```

```python
import math

import jax
import jax.numpy as jnp
from jax import lax
from jax.experimental import pallas as pl
from jax.experimental.pallas import tpu as pltpu
from jax.sharding import PartitionSpec as P

L = 512
LANES = 128
HALF = 64
SPAN = L + LANES
SLOTS = 4
epsilon = 1e-06


def detect_kernel(
    each,
    factor,
    order_ref,
    groups_ref,
    templates_ref,
    series_ref,
    before_ref,
    out_ref,
    source,
    home,
    count,
    wide,
    tails,
    waves,
    norms,
    band,
    shifts,
    energy,
    scales,
    windows,
    toeplitz,
    share,
    total,
    turned,
):
    block, spread = groups_ref.shape
    n_group = series_ref.shape[0]
    rows = total.shape[1]
    padded = rows + 8
    ahead = tails.shape[0] // templates_ref.shape[0]
    tail = L // LANES
    parts = 3 * L // LANES
    slots = wide.shape[0] // parts
    stations = slots // (block * spread)
    lane = lax.broadcasted_iota(jnp.int32, (1, LANES), 1)
    low = lane < HALF

    def clear(n, carry):
        source[n] = block * spread
        home[n] = block
        return carry

    lax.fori_loop(0, source.shape[0], clear, 0)
    for n in range(count.shape[0]):
        count[n] = 0
    for r in range(block):
        for i in range(spread):
            named = groups_ref[r, i]
            slot = named * SLOTS + count[named]
            source[slot] = r * spread + i
            home[slot] = r
            count[named] = count[named] + 1
    spare = waves.shape[0] - slots
    for r in range(block):
        wide[r * each : (r + 1) * each, :] = templates_ref[r, 0:each, :].astype(jnp.float32)
    for n in range(templates_ref.shape[0]):
        tails[n * ahead : (n + 1) * ahead, :] = templates_ref[n, each:, :].astype(jnp.float32)
    for c in range(3):
        for v in range(L // LANES):
            at = c * SPAN + v * LANES
            waves[0:slots, at : at + LANES] = wide[pl.ds(c * L // LANES + v, slots, parts), :]
        waves[0:slots, c * SPAN + L : (c + 1) * SPAN] = jnp.zeros((slots, LANES), jnp.float32)
    waves[slots:, :] = jnp.zeros((spare, 3 * SPAN), jnp.float32)
    squares = jnp.sum(jnp.square(waves[0:slots, :]), axis=1, keepdims=True)
    norms[0:slots, :] = jnp.broadcast_to(lax.rsqrt(squares + epsilon), (slots, LANES))
    norms[slots:, :] = jnp.zeros((spare, LANES), jnp.float32)
    r = lax.broadcasted_iota(jnp.int32, (LANES, LANES), 0)
    l = lax.broadcasted_iota(jnp.int32, (LANES, LANES), 1)
    band[0:LANES, :] = jnp.where(r >= l, 1.0, 0.0).astype(jnp.bfloat16)
    band[LANES : 2 * LANES, :] = jnp.ones((LANES, LANES), jnp.bfloat16)
    band[2 * LANES :, :] = jnp.where(r < l, 1.0, 0.0).astype(jnp.bfloat16)
    shifts[:, :, rows:, :] = jnp.zeros((3, 2, 16, LANES), jnp.float32)
    if before_ref is None:
        total[...] = jnp.zeros_like(total)
    else:
        total[...] = before_ref[...]

    def prepare(group, station, buffer):
        squares = jnp.zeros((padded, LANES), jnp.float32)
        for c in range(3):
            line = c * stations + station
            main = series_ref[group, line * rows : (line + 1) * rows, :]
            shifts[c, 0, 0:rows, :] = main.astype(jnp.float32)
            at = order_ref[group] * ahead + line * tail
            shifts[c, 0, rows : rows + tail, :] = tails[pl.ds(at, tail), :]
            plain = shifts[c, 0, 0:padded, :]
            squares = squares + plain * plain
            after = shifts[c, 0, 1 : padded + 1, :]
            shifts[c, 1, 0:padded, :] = pltpu.roll(jnp.where(low, after, plain), HALF, 1)
        energy[...] = squares
        middle = energy[1 : rows + 1, :] + energy[2 : rows + 2, :] + energy[3 : rows + 3, :]
        pieces = jnp.concatenate([energy[0:rows, :], middle, energy[4 : rows + 4, :]], axis=1)
        coarse = pieces.astype(jnp.bfloat16)
        fine = (pieces - coarse.astype(jnp.float32)).astype(jnp.bfloat16)
        window_energy = jnp.dot(coarse, band[...], preferred_element_type=jnp.float32)
        window_energy += jnp.dot(fine, band[...], preferred_element_type=jnp.float32)
        scale = lax.rsqrt(window_energy + epsilon)
        other = pltpu.roll(scale, HALF, 1)
        scales[buffer, 0] = jnp.where(low, scale, other)
        scales[buffer, 1] = jnp.where(low, other, scale)
        for j in range(SLOTS):
            row = source[order_ref[group] * SLOTS + j] * stations + station
            for c in range(3):
                wave = waves[pl.ds(row, 1), c * SPAN : (c + 1) * SPAN]
                moved = pltpu.roll(
                    jnp.broadcast_to(wave, (HALF, SPAN)), 0, 1, stride=1, stride_axis=0
                )
                toeplitz[buffer, j * HALF : (j + 1) * HALF, c * SPAN : (c + 1) * SPAN] = (
                    moved.astype(jnp.bfloat16)
                )
        for c in range(3):
            for e in range(2):
                for v in range(SPAN // LANES):
                    at = c * SPAN + v * LANES
                    windows[buffer, e * rows : (e + 1) * rows, at : at + LANES] = shifts[
                        c, e, v : v + rows, :
                    ].astype(jnp.bfloat16)

    def combine(group, station, buffer):
        product = lax.dot_general(
            windows[buffer],
            toeplitz[buffer],
            (((1,), (1,)), ((), ())),
            preferred_element_type=jnp.float32,
        )
        weight = []
        for j in range(SLOTS):
            row = source[order_ref[group] * SLOTS + j] * stations + station
            weight.append(norms[pl.ds(row, 1), :])
        for p in range(SLOTS // 2):
            both = jnp.where(low, weight[2 * p], weight[2 * p + 1])
            at = p * LANES
            for e in range(2):
                term = product[e * rows : (e + 1) * rows, at : at + LANES]
                term = term * (scales[buffer, e] * both)
                if station:
                    term = term + share[e, :, at : at + LANES]
                share[e, :, at : at + LANES] = term

    def group_term(group, carry):
        later = lax.min(group + 1, n_group - 1)
        for station in range(stations):
            if station < stations - 1:
                prepare(group, station + 1, (station + 1) % 2)
            else:
                prepare(later, 0, (station + 1) % 2)
            combine(group, station, station % 2)
        for j in range(SLOTS):
            at = (j // 2) * LANES
            first = share[0, :, at : at + LANES]
            second = share[1, :, at : at + LANES]
            if j % 2 == 0:
                whole = jnp.where(low, first, pltpu.roll(second, HALF, 1))
            else:
                whole = jnp.where(low, pltpu.roll(first, HALF, 1), second)
            r = home[order_ref[group] * SLOTS + j]
            total[r] = total[r] + whole
        return carry

    prepare(0, 0, 0)
    lax.fori_loop(0, n_group, group_term, 0)
    if factor is None:
        out_ref[...] = total[...]
        return
    for r in range(block):
        turned[:, r, :] = total[r] * factor
    n_out, _, samples = out_ref.shape
    for w in range(n_out):
        for i in range(samples // LANES):
            out_ref[w, :, i * LANES : (i + 1) * LANES] = turned[w * (samples // LANES) + i]


def detect(order, groups, templates, series, before, each, parts, factor):
    n_all = templates.shape[0]
    block, spread = groups.shape
    stations = 4
    slots = block * spread * stations
    rows = series.shape[1] // (3 * stations)
    padded = rows + 8
    samples = rows * LANES // parts
    spare = -(-(slots + stations) // 8) * 8
    if factor is None:
        out_shape = jax.ShapeDtypeStruct((block + 1, rows, LANES), jnp.float32)
    else:
        out_shape = jax.ShapeDtypeStruct((parts, block, samples), jnp.float32)
    operands = [order, groups, templates, series]
    spaces = [pltpu.SMEM, pltpu.SMEM, pltpu.VMEM, pltpu.VMEM]
    if before is not None:
        operands.append(before)
        spaces.append(pltpu.VMEM)

    def body(*refs):
        refs = list(refs)
        if before is None:
            refs.insert(4, None)
        detect_kernel(each, factor, *refs)

    return pl.pallas_call(
        body,
        out_shape=out_shape,
        in_specs=[pl.BlockSpec(memory_space=space) for space in spaces],
        out_specs=pl.BlockSpec(memory_space=pltpu.VMEM),
        scratch_shapes=[
            pltpu.SMEM((n_all * SLOTS,), jnp.int32),
            pltpu.SMEM((n_all * SLOTS,), jnp.int32),
            pltpu.SMEM((n_all,), jnp.int32),
            pltpu.VMEM((slots * 3 * L // LANES, LANES), jnp.float32),
            pltpu.VMEM((n_all * (templates.shape[1] - each), LANES), jnp.float32),
            pltpu.VMEM((spare, 3 * SPAN), jnp.float32),
            pltpu.VMEM((spare, LANES), jnp.float32),
            pltpu.VMEM((3 * LANES, LANES), jnp.bfloat16),
            pltpu.VMEM((3, 2, padded + 8, LANES), jnp.float32),
            pltpu.VMEM((padded, LANES), jnp.float32),
            pltpu.VMEM((2, 2, rows, LANES), jnp.float32),
            pltpu.VMEM((2, 2 * rows, 3 * SPAN), jnp.bfloat16),
            pltpu.VMEM((2, SLOTS * HALF, 3 * SPAN), jnp.bfloat16),
            pltpu.VMEM((2, rows, SLOTS * HALF), jnp.float32),
            pltpu.VMEM((block + 1, rows, LANES), jnp.float32),
            pltpu.VMEM((rows, block, LANES), jnp.float32),
        ],
        compiler_params=pltpu.CompilerParams(vmem_limit_bytes=32 * 1024 * 1024),
        cost_estimate=pl.CostEstimate(
            flops=16 * series.shape[0] * stations * 2 * rows * 3 * SPAN * SLOTS * HALF,
            bytes_accessed=templates.size * 2 + 4 * block * rows * LANES,
            transcendentals=0,
        ),
    )(*operands)


def copies_to(value, axis, groups=None):
    count = len(groups[0]) if groups else lax.axis_size(axis)
    spread = jnp.broadcast_to(value[None], (count,) + value.shape)
    return lax.all_to_all(spread, axis, 0, 0, axis_index_groups=groups, tiled=True)


def on_device(record, templates, template_groups):
    channels, stations, samples = record.shape
    n_tm, n_sta = lax.axis_size("tm"), lax.axis_size("sta")
    m, s = lax.axis_index("tm"), lax.axis_index("sta")
    n_a = n_sta
    n_b = n_tm // n_a
    near = [[a * n_b + b for b in range(n_b)] for a in range(n_a)]
    far = [[a * n_b + b for a in range(n_a)] for b in range(n_b)]
    spread = template_groups.shape[1]

    first = (s * n_b + lax.rem(m, n_b)) * n_a
    groups = lax.dynamic_slice_in_dim(template_groups, first, n_a, 0)

    lines = channels * stations
    steps = samples // LANES
    around = copies_to(record.reshape(lines * steps, LANES), "tm", near)
    around, own = lax.optimization_barrier((around, templates.reshape(-1, LANES)))
    front = around[0].reshape(lines, steps, LANES)[:, : L // LANES]
    tail = lax.ppermute(front, "tm", [(i + n_b, i) for i in range(n_tm - n_b)])
    tail = jnp.broadcast_to(tail.reshape(1, -1, LANES), (n_sta, lines * L // LANES, LANES))
    block = copies_to(own, "tm", far)
    block = lax.all_to_all(jnp.concatenate([block, tail], axis=1), "sta", 0, 0, tiled=True)
    main = around.reshape(n_b, lines, steps, LANES)
    mine = main.transpose(1, 0, 2, 3).reshape(-1, LANES)

    cores = 2
    n_y = n_sta // cores
    y, core = s // cores, lax.rem(s, cores)
    pieces = [mine]
    for k in range(1, n_y):
        pairs = [(t, (t + k * cores) % n_sta) for t in range(n_sta)]
        pieces.append(lax.ppermute(mine, "sta", pairs))
    swap = [(t, t ^ 1) for t in range(n_sta)]
    pieces = jnp.stack(pieces)
    others = lax.ppermute(pieces, "sta", swap)
    rows_of_y = lax.rem(y - jnp.arange(n_y, dtype=jnp.int32) + n_y, n_y) * cores
    factor = math.sqrt(channels * L / (spread * stations))
    total = detect(rows_of_y + core, groups, block, pieces, None, own.shape[0], n_b, None)
    other = rows_of_y + 1 - core
    total = detect(other, groups, block, others, total, own.shape[0], n_b, factor)

    found = lax.all_to_all(total, "tm", 0, 0, axis_index_groups=near, tiled=True)
    return found.reshape(n_b * n_a, samples)


def solution(mesh):
    return jax.shard_map(
        on_device,
        mesh=mesh,
        in_specs=(P(None, "sta", "tm"), P(("tm", "sta"), None, None, None), P()),
        out_specs=P("sta", "tm"),
        check_vma=False,
    )
```

```python
import math

import jax
import jax.numpy as jnp
from jax import lax
from jax.experimental import pallas as pl
from jax.experimental.pallas import tpu as pltpu
from jax.sharding import PartitionSpec as P

L = 512
LANES = 128
HALF = 64
STEP = L + HALF
WIDTH = 3 * STEP + HALF
SLOTS = 4
epsilon = 1e-06


def detect_kernel(
    each,
    factor,
    order_ref,
    groups_ref,
    templates_ref,
    series_ref,
    before_ref,
    out_ref,
    source,
    home,
    count,
    wide,
    tails,
    waves,
    norms,
    band,
    shifts,
    energy,
    scales,
    windows,
    toeplitz,
    share,
    total,
    turned,
):
    block, spread = groups_ref.shape
    n_group = series_ref.shape[0]
    rows = total.shape[1]
    padded = rows + 8
    ahead = tails.shape[0] // templates_ref.shape[0]
    tail = L // LANES
    parts = 3 * L // LANES
    slots = wide.shape[0] // parts
    stations = slots // (block * spread)
    lane = lax.broadcasted_iota(jnp.int32, (1, LANES), 1)
    low = lane < HALF

    def clear(n, carry):
        source[n] = block * spread
        home[n] = block
        return carry

    lax.fori_loop(0, source.shape[0], clear, 0)
    for n in range(count.shape[0]):
        count[n] = 0
    for r in range(block):
        for i in range(spread):
            named = groups_ref[r, i]
            slot = named * SLOTS + count[named]
            source[slot] = r * spread + i
            home[slot] = r
            count[named] = count[named] + 1
    spare = waves.shape[0] - slots
    for r in range(block):
        wide[r * each : (r + 1) * each, :] = templates_ref[r, 0:each, :].astype(jnp.float32)
    for n in range(templates_ref.shape[0]):
        tails[n * ahead : (n + 1) * ahead, :] = templates_ref[n, each:, :].astype(jnp.float32)
    waves[...] = jnp.zeros_like(waves)
    for c in range(3):
        for v in range(L // LANES):
            at = c * STEP + v * LANES
            waves[0:slots, at : at + LANES] = wide[pl.ds(c * L // LANES + v, slots, parts), :]
    squares = jnp.sum(jnp.square(waves[0:slots, :]), axis=1, keepdims=True)
    norms[0:slots, :] = jnp.broadcast_to(lax.rsqrt(squares + epsilon), (slots, LANES))
    norms[slots:, :] = jnp.zeros((spare, LANES), jnp.float32)
    r = lax.broadcasted_iota(jnp.int32, (LANES, LANES), 0)
    l = lax.broadcasted_iota(jnp.int32, (LANES, LANES), 1)
    band[0:LANES, :] = jnp.where(r >= l, 1.0, 0.0).astype(jnp.bfloat16)
    band[LANES : 2 * LANES, :] = jnp.ones((LANES, LANES), jnp.bfloat16)
    band[2 * LANES :, :] = jnp.where(r < l, 1.0, 0.0).astype(jnp.bfloat16)
    shifts[:, :, rows:, :] = jnp.zeros((3, 2, 16, LANES), jnp.float32)
    if before_ref is None:
        total[...] = jnp.zeros_like(total)
    else:
        total[...] = before_ref[...]

    def prepare(group, station, buffer):
        squares = jnp.zeros((padded, LANES), jnp.float32)
        for c in range(3):
            line = c * stations + station
            main = series_ref[group, line * rows : (line + 1) * rows, :]
            shifts[c, 0, 0:rows, :] = main.astype(jnp.float32)
            at = order_ref[group] * ahead + line * tail
            shifts[c, 0, rows : rows + tail, :] = tails[pl.ds(at, tail), :]
            plain = shifts[c, 0, 0:padded, :]
            squares = squares + plain * plain
            after = shifts[c, 0, 1 : padded + 1, :]
            shifts[c, 1, 0:padded, :] = pltpu.roll(jnp.where(low, after, plain), HALF, 1)
        energy[...] = squares
        middle = energy[1 : rows + 1, :] + energy[2 : rows + 2, :] + energy[3 : rows + 3, :]
        pieces = jnp.concatenate([energy[0:rows, :], middle, energy[4 : rows + 4, :]], axis=1)
        coarse = pieces.astype(jnp.bfloat16)
        fine = (pieces - coarse.astype(jnp.float32)).astype(jnp.bfloat16)
        window_energy = jnp.dot(coarse, band[...], preferred_element_type=jnp.float32)
        window_energy += jnp.dot(fine, band[...], preferred_element_type=jnp.float32)
        scale = lax.rsqrt(window_energy + epsilon)
        other = pltpu.roll(scale, HALF, 1)
        scales[buffer, 0] = jnp.where(low, scale, other)
        scales[buffer, 1] = jnp.where(low, other, scale)
        for j in range(SLOTS):
            row = source[order_ref[group] * SLOTS + j] * stations + station
            wave = jnp.broadcast_to(waves[pl.ds(row, 1), :], (HALF, WIDTH))
            moved = pltpu.roll(wave, 0, 1, stride=1, stride_axis=0)
            toeplitz[buffer, j * HALF : (j + 1) * HALF, :] = moved.astype(jnp.bfloat16)
        for e in range(2):
            tiles = [shifts[0, e, v : v + rows, :] for v in range(tail)]
            if e:
                start = shifts[1, 0, 0:rows, :]
            else:
                start = pltpu.roll(shifts[1, 0, 0:rows, :], HALF, 1)
            tiles.append(jnp.where(low, shifts[0, e, tail : tail + rows, :], start))
            tiles += [shifts[1, 1 - e, v + e : v + e + rows, :] for v in range(tail)]
            tiles += [shifts[2, e, v : v + rows, :] for v in range(tail + 1)]
            for n, tile in enumerate(tiles):
                at = n * LANES
                windows[buffer, e * rows : (e + 1) * rows, at : at + LANES] = tile.astype(
                    jnp.bfloat16
                )

    def combine(group, station, buffer):
        weight = []
        for j in range(SLOTS):
            row = source[order_ref[group] * SLOTS + j] * stations + station
            weight.append(norms[pl.ds(row, 1), :])
        for p in range(SLOTS // 2):
            both = jnp.where(low, weight[2 * p], weight[2 * p + 1])
            at = p * LANES
            product = lax.dot_general(
                windows[buffer],
                toeplitz[buffer, at : at + LANES, :],
                (((1,), (1,)), ((), ())),
                preferred_element_type=jnp.float32,
            )
            for e in range(2):
                term = product[e * rows : (e + 1) * rows, :] * (scales[buffer, e] * both)
                if station:
                    term = term + share[e, :, at : at + LANES]
                share[e, :, at : at + LANES] = term

    def group_term(group, carry):
        later = lax.min(group + 1, n_group - 1)
        for station in range(stations):
            combine(group, station, station % 2)
            if station < stations - 1:
                prepare(group, station + 1, (station + 1) % 2)
            else:
                prepare(later, 0, (station + 1) % 2)
        for j in range(SLOTS):
            at = (j // 2) * LANES
            first = share[0, :, at : at + LANES]
            second = share[1, :, at : at + LANES]
            if j % 2 == 0:
                whole = jnp.where(low, first, pltpu.roll(second, HALF, 1))
            else:
                whole = jnp.where(low, pltpu.roll(first, HALF, 1), second)
            r = home[order_ref[group] * SLOTS + j]
            total[r] = total[r] + whole
        return carry

    prepare(0, 0, 0)
    lax.fori_loop(0, n_group, group_term, 0)
    if factor is None:
        out_ref[...] = total[...]
        return
    for r in range(block):
        turned[:, r, :] = total[r] * factor
    n_out, _, samples = out_ref.shape
    for w in range(n_out):
        for i in range(samples // LANES):
            out_ref[w, :, i * LANES : (i + 1) * LANES] = turned[w * (samples // LANES) + i]


def detect(order, groups, templates, series, before, each, parts, factor):
    n_all = templates.shape[0]
    block, spread = groups.shape
    stations = 4
    slots = block * spread * stations
    rows = series.shape[1] // (3 * stations)
    padded = rows + 8
    samples = rows * LANES // parts
    spare = -(-(slots + stations) // 8) * 8
    if factor is None:
        out_shape = jax.ShapeDtypeStruct((block + 1, rows, LANES), jnp.float32)
    else:
        out_shape = jax.ShapeDtypeStruct((parts, block, samples), jnp.float32)
    operands = [order, groups, templates, series]
    spaces = [pltpu.SMEM, pltpu.SMEM, pltpu.VMEM, pltpu.VMEM]
    if before is not None:
        operands.append(before)
        spaces.append(pltpu.VMEM)

    def body(*refs):
        refs = list(refs)
        if before is None:
            refs.insert(4, None)
        detect_kernel(each, factor, *refs)

    return pl.pallas_call(
        body,
        out_shape=out_shape,
        in_specs=[pl.BlockSpec(memory_space=space) for space in spaces],
        out_specs=pl.BlockSpec(memory_space=pltpu.VMEM),
        scratch_shapes=[
            pltpu.SMEM((n_all * SLOTS,), jnp.int32),
            pltpu.SMEM((n_all * SLOTS,), jnp.int32),
            pltpu.SMEM((n_all,), jnp.int32),
            pltpu.VMEM((slots * 3 * L // LANES, LANES), jnp.float32),
            pltpu.VMEM((n_all * (templates.shape[1] - each), LANES), jnp.float32),
            pltpu.VMEM((spare, WIDTH), jnp.float32),
            pltpu.VMEM((spare, LANES), jnp.float32),
            pltpu.VMEM((3 * LANES, LANES), jnp.bfloat16),
            pltpu.VMEM((3, 2, padded + 8, LANES), jnp.float32),
            pltpu.VMEM((padded, LANES), jnp.float32),
            pltpu.VMEM((2, 2, rows, LANES), jnp.float32),
            pltpu.VMEM((2, 2 * rows, WIDTH), jnp.bfloat16),
            pltpu.VMEM((2, SLOTS * HALF, WIDTH), jnp.bfloat16),
            pltpu.VMEM((2, rows, SLOTS * HALF), jnp.float32),
            pltpu.VMEM((block + 1, rows, LANES), jnp.float32),
            pltpu.VMEM((rows, block, LANES), jnp.float32),
        ],
        compiler_params=pltpu.CompilerParams(vmem_limit_bytes=32 * 1024 * 1024),
        cost_estimate=pl.CostEstimate(
            flops=16 * series.shape[0] * stations * 2 * rows * WIDTH * SLOTS * HALF,
            bytes_accessed=templates.size * 2 + 4 * block * rows * LANES,
            transcendentals=0,
        ),
    )(*operands)


def copies_to(value, axis, groups=None):
    count = len(groups[0]) if groups else lax.axis_size(axis)
    spread = jnp.broadcast_to(value[None], (count,) + value.shape)
    return lax.all_to_all(spread, axis, 0, 0, axis_index_groups=groups, tiled=True)


def on_device(record, templates, template_groups):
    channels, stations, samples = record.shape
    n_tm, n_sta = lax.axis_size("tm"), lax.axis_size("sta")
    m, s = lax.axis_index("tm"), lax.axis_index("sta")
    n_a = n_sta
    n_b = n_tm // n_a
    near = [[a * n_b + b for b in range(n_b)] for a in range(n_a)]
    far = [[a * n_b + b for a in range(n_a)] for b in range(n_b)]
    spread = template_groups.shape[1]

    first = (s * n_b + lax.rem(m, n_b)) * n_a
    groups = lax.dynamic_slice_in_dim(template_groups, first, n_a, 0)

    lines = channels * stations
    steps = samples // LANES
    around = copies_to(record.reshape(lines * steps, LANES), "tm", near)
    around, own = lax.optimization_barrier((around, templates.reshape(-1, LANES)))
    front = around[0].reshape(lines, steps, LANES)[:, : L // LANES]
    tail = lax.ppermute(front, "tm", [(i + n_b, i) for i in range(n_tm - n_b)])
    tail = jnp.broadcast_to(tail.reshape(1, -1, LANES), (n_sta, lines * L // LANES, LANES))
    block = copies_to(own, "tm", far)
    block = lax.all_to_all(jnp.concatenate([block, tail], axis=1), "sta", 0, 0, tiled=True)
    main = around.reshape(n_b, lines, steps, LANES)
    mine = main.transpose(1, 0, 2, 3).reshape(-1, LANES)

    cores = 2
    n_y = n_sta // cores
    y, core = s // cores, lax.rem(s, cores)
    pieces = [mine]
    for k in range(1, n_y):
        pairs = [(t, (t + k * cores) % n_sta) for t in range(n_sta)]
        pieces.append(lax.ppermute(mine, "sta", pairs))
    swap = [(t, t ^ 1) for t in range(n_sta)]
    pieces = jnp.stack(pieces)
    others = lax.ppermute(pieces, "sta", swap)
    rows_of_y = lax.rem(y - jnp.arange(n_y, dtype=jnp.int32) + n_y, n_y) * cores
    factor = math.sqrt(channels * L / (spread * stations))
    total = detect(rows_of_y + core, groups, block, pieces, None, own.shape[0], n_b, None)
    other = rows_of_y + 1 - core
    total = detect(other, groups, block, others, total, own.shape[0], n_b, factor)

    found = lax.all_to_all(total, "tm", 0, 0, axis_index_groups=near, tiled=True)
    return found.reshape(n_b * n_a, samples)


def solution(mesh):
    return jax.shard_map(
        on_device,
        mesh=mesh,
        in_specs=(P(None, "sta", "tm"), P(("tm", "sta"), None, None, None), P()),
        out_specs=P("sta", "tm"),
        check_vma=False,
    )
```

```python
import math

import jax
import jax.numpy as jnp
from jax import lax
from jax.experimental import pallas as pl
from jax.experimental.pallas import tpu as pltpu
from jax.sharding import PartitionSpec as P

L = 512
LANES = 128
HALF = 64
STEP = L + HALF
WIDTH = 3 * STEP + HALF
SLOTS = 4
epsilon = 1e-06


def detect_kernel(
    each,
    factor,
    order_ref,
    groups_ref,
    templates_ref,
    series_ref,
    before_ref,
    out_ref,
    source,
    home,
    count,
    wide,
    tails,
    waves,
    norms,
    band,
    shifts,
    energy,
    scales,
    windows,
    toeplitz,
    share,
    total,
    turned,
):
    block, spread = groups_ref.shape
    n_group = series_ref.shape[0]
    rows = total.shape[1]
    padded = rows + 8
    ahead = tails.shape[0] // templates_ref.shape[0]
    tail = L // LANES
    parts = 3 * L // LANES
    slots = wide.shape[0] // parts
    stations = slots // (block * spread)
    lane = lax.broadcasted_iota(jnp.int32, (1, LANES), 1)
    low = lane < HALF

    def clear(n, carry):
        source[n] = block * spread
        home[n] = block
        return carry

    lax.fori_loop(0, source.shape[0], clear, 0)
    for n in range(count.shape[0]):
        count[n] = 0
    for r in range(block):
        for i in range(spread):
            named = groups_ref[r, i]
            slot = named * SLOTS + count[named]
            source[slot] = r * spread + i
            home[slot] = r
            count[named] = count[named] + 1
    spare = waves.shape[0] - slots
    for r in range(block):
        wide[r * each : (r + 1) * each, :] = templates_ref[r, 0:each, :].astype(jnp.float32)
    for n in range(templates_ref.shape[0]):
        tails[n * ahead : (n + 1) * ahead, :] = templates_ref[n, each:, :].astype(jnp.float32)
    waves[...] = jnp.zeros_like(waves)
    for c in range(3):
        for v in range(L // LANES):
            at = c * STEP + v * LANES
            waves[0:slots, at : at + LANES] = wide[pl.ds(c * L // LANES + v, slots, parts), :]
    squares = jnp.sum(jnp.square(waves[0:slots, :]), axis=1, keepdims=True)
    norms[0:slots, :] = jnp.broadcast_to(lax.rsqrt(squares + epsilon), (slots, LANES))
    norms[slots:, :] = jnp.zeros((spare, LANES), jnp.float32)
    r = lax.broadcasted_iota(jnp.int32, (LANES, LANES), 0)
    l = lax.broadcasted_iota(jnp.int32, (LANES, LANES), 1)
    band[0:LANES, :] = jnp.where(r >= l, 1.0, 0.0).astype(jnp.bfloat16)
    band[LANES : 2 * LANES, :] = jnp.ones((LANES, LANES), jnp.bfloat16)
    band[2 * LANES :, :] = jnp.where(r < l, 1.0, 0.0).astype(jnp.bfloat16)
    shifts[:, :, rows:, :] = jnp.zeros((3, 2, 16, LANES), jnp.float32)
    if before_ref is None:
        total[...] = jnp.zeros_like(total)
    else:
        total[...] = before_ref[...]

    def prepare(group, station, buffer):
        squares = jnp.zeros((padded, LANES), jnp.float32)
        for c in range(3):
            line = c * stations + station
            main = series_ref[group, line * rows : (line + 1) * rows, :]
            shifts[c, 0, 0:rows, :] = main.astype(jnp.float32)
            at = order_ref[group] * ahead + line * tail
            shifts[c, 0, rows : rows + tail, :] = tails[pl.ds(at, tail), :]
            plain = shifts[c, 0, 0:padded, :]
            squares = squares + plain * plain
            after = shifts[c, 0, 1 : padded + 1, :]
            shifts[c, 1, 0:padded, :] = pltpu.roll(jnp.where(low, after, plain), HALF, 1)
        energy[...] = squares
        middle = energy[1 : rows + 1, :] + energy[2 : rows + 2, :] + energy[3 : rows + 3, :]
        pieces = jnp.concatenate([energy[0:rows, :], middle, energy[4 : rows + 4, :]], axis=1)
        coarse = pieces.astype(jnp.bfloat16)
        fine = (pieces - coarse.astype(jnp.float32)).astype(jnp.bfloat16)
        window_energy = jnp.dot(coarse, band[...], preferred_element_type=jnp.float32)
        window_energy += jnp.dot(fine, band[...], preferred_element_type=jnp.float32)
        scale = lax.rsqrt(window_energy + epsilon)
        other = pltpu.roll(scale, HALF, 1)
        scales[buffer, 0] = jnp.where(low, scale, other)
        scales[buffer, 1] = jnp.where(low, other, scale)
        for j in range(SLOTS):
            row = source[order_ref[group] * SLOTS + j] * stations + station
            wave = jnp.broadcast_to(waves[pl.ds(row, 1), :], (HALF, WIDTH))
            moved = pltpu.roll(wave, 0, 1, stride=1, stride_axis=0)
            toeplitz[buffer, j * HALF : (j + 1) * HALF, :] = moved.astype(jnp.bfloat16)
        for e in range(2):
            tiles = [shifts[0, e, v : v + rows, :] for v in range(tail)]
            if e:
                start = shifts[1, 0, 0:rows, :]
            else:
                start = pltpu.roll(shifts[1, 0, 0:rows, :], HALF, 1)
            tiles.append(jnp.where(low, shifts[0, e, tail : tail + rows, :], start))
            tiles += [shifts[1, 1 - e, v + e : v + e + rows, :] for v in range(tail)]
            tiles += [shifts[2, e, v : v + rows, :] for v in range(tail + 1)]
            for n, tile in enumerate(tiles):
                at = n * LANES
                windows[buffer, e * rows : (e + 1) * rows, at : at + LANES] = tile.astype(
                    jnp.bfloat16
                )

    def combine(group, station, buffer):
        weight = []
        for j in range(SLOTS):
            row = source[order_ref[group] * SLOTS + j] * stations + station
            weight.append(norms[pl.ds(row, 1), :])
        for p in range(SLOTS // 2):
            both = jnp.where(low, weight[2 * p], weight[2 * p + 1])
            at = p * LANES
            product = lax.dot_general(
                windows[buffer],
                toeplitz[buffer, at : at + LANES, :],
                (((1,), (1,)), ((), ())),
                preferred_element_type=jnp.float32,
            )
            for e in range(2):
                term = product[e * rows : (e + 1) * rows, :] * (scales[buffer, e] * both)
                if station:
                    term = term + share[e, :, at : at + LANES]
                share[e, :, at : at + LANES] = term

    def group_term(group, carry):
        later = lax.min(group + 1, n_group - 1)
        for station in range(stations):
            combine(group, station, station % 2)
            if station < stations - 1:
                prepare(group, station + 1, (station + 1) % 2)
            else:
                prepare(later, 0, (station + 1) % 2)
        for j in range(SLOTS):
            at = (j // 2) * LANES
            first = share[0, :, at : at + LANES]
            second = share[1, :, at : at + LANES]
            if j % 2 == 0:
                whole = jnp.where(low, first, pltpu.roll(second, HALF, 1))
            else:
                whole = jnp.where(low, pltpu.roll(first, HALF, 1), second)
            r = home[order_ref[group] * SLOTS + j]
            total[r] = total[r] + whole
        return carry

    prepare(0, 0, 0)
    lax.fori_loop(0, n_group, group_term, 0)
    if factor is None:
        out_ref[...] = total[...]
        return
    for r in range(block):
        turned[:, r, :] = total[r] * factor
    n_out, _, samples = out_ref.shape
    for w in range(n_out):
        for i in range(samples // LANES):
            out_ref[w, :, i * LANES : (i + 1) * LANES] = turned[w * (samples // LANES) + i]


def detect(order, groups, templates, series, before, each, parts, factor):
    n_all = templates.shape[0]
    block, spread = groups.shape
    stations = 4
    slots = block * spread * stations
    rows = series.shape[1] // (3 * stations)
    padded = rows + 8
    samples = rows * LANES // parts
    spare = -(-(slots + stations) // 8) * 8
    if factor is None:
        out_shape = jax.ShapeDtypeStruct((block + 1, rows, LANES), jnp.float32)
    else:
        out_shape = jax.ShapeDtypeStruct((parts, block, samples), jnp.float32)
    operands = [order, groups, templates, series]
    spaces = [pltpu.SMEM, pltpu.SMEM, pltpu.VMEM, pltpu.VMEM]
    if before is not None:
        operands.append(before)
        spaces.append(pltpu.VMEM)

    def body(*refs):
        refs = list(refs)
        if before is None:
            refs.insert(4, None)
        detect_kernel(each, factor, *refs)

    return pl.pallas_call(
        body,
        out_shape=out_shape,
        in_specs=[pl.BlockSpec(memory_space=space) for space in spaces],
        out_specs=pl.BlockSpec(memory_space=pltpu.VMEM),
        scratch_shapes=[
            pltpu.SMEM((n_all * SLOTS,), jnp.int32),
            pltpu.SMEM((n_all * SLOTS,), jnp.int32),
            pltpu.SMEM((n_all,), jnp.int32),
            pltpu.VMEM((slots * 3 * L // LANES, LANES), jnp.float32),
            pltpu.VMEM((n_all * (templates.shape[1] - each), LANES), jnp.float32),
            pltpu.VMEM((spare, WIDTH), jnp.float32),
            pltpu.VMEM((spare, LANES), jnp.float32),
            pltpu.VMEM((3 * LANES, LANES), jnp.bfloat16),
            pltpu.VMEM((3, 2, padded + 8, LANES), jnp.float32),
            pltpu.VMEM((padded, LANES), jnp.float32),
            pltpu.VMEM((2, 2, rows, LANES), jnp.float32),
            pltpu.VMEM((2, 2 * rows, WIDTH), jnp.bfloat16),
            pltpu.VMEM((2, SLOTS * HALF, WIDTH), jnp.bfloat16),
            pltpu.VMEM((2, rows, SLOTS * HALF), jnp.float32),
            pltpu.VMEM((block + 1, rows, LANES), jnp.float32),
            pltpu.VMEM((rows, block, LANES), jnp.float32),
        ],
        compiler_params=pltpu.CompilerParams(vmem_limit_bytes=32 * 1024 * 1024),
        cost_estimate=pl.CostEstimate(
            flops=16 * series.shape[0] * stations * 2 * rows * WIDTH * SLOTS * HALF,
            bytes_accessed=templates.size * 2 + 4 * block * rows * LANES,
            transcendentals=0,
        ),
    )(*operands)


def copies_to(value, axis, groups=None):
    count = len(groups[0]) if groups else lax.axis_size(axis)
    spread = jnp.broadcast_to(value[None], (count,) + value.shape)
    return lax.all_to_all(spread, axis, 0, 0, axis_index_groups=groups, tiled=True)


def on_device(record, templates, template_groups):
    channels, stations, samples = record.shape
    n_tm, n_sta = lax.axis_size("tm"), lax.axis_size("sta")
    m, s = lax.axis_index("tm"), lax.axis_index("sta")
    n_a = n_sta
    n_b = n_tm // n_a
    near = [[a * n_b + b for b in range(n_b)] for a in range(n_a)]
    far = [[a * n_b + b for a in range(n_a)] for b in range(n_b)]
    spread = template_groups.shape[1]

    first = (s * n_b + lax.rem(m, n_b)) * n_a
    groups = lax.dynamic_slice_in_dim(template_groups, first, n_a, 0)

    lines = channels * stations
    steps = samples // LANES
    half = n_b // 2
    four = [[i + j for j in range(half)] for i in range(0, n_tm, half)]
    same = lax.all_gather(record.reshape(lines * steps, LANES), "tm", axis_index_groups=four)
    other = lax.ppermute(same, "tm", [(i, i ^ half) for i in range(n_tm)])
    upper = lax.rem(m // half, 2) == 1
    around = jnp.concatenate([jnp.where(upper, other, same), jnp.where(upper, same, other)])
    own = templates.reshape(-1, LANES)
    front = around[0].reshape(lines, steps, LANES)[:, : L // LANES]
    tail = lax.ppermute(front, "tm", [(i + n_b, i) for i in range(n_tm - n_b)])
    tail = jnp.broadcast_to(tail.reshape(1, -1, LANES), (n_sta, lines * L // LANES, LANES))
    block = copies_to(own, "tm", far)
    block = lax.all_to_all(jnp.concatenate([block, tail], axis=1), "sta", 0, 0, tiled=True)
    main = around.reshape(n_b, lines, steps, LANES)
    mine = main.transpose(1, 0, 2, 3).reshape(-1, LANES)

    cores = 2
    n_y = n_sta // cores
    y, core = s // cores, lax.rem(s, cores)
    pieces = [mine]
    for k in range(1, n_y):
        pairs = [(t, (t + k * cores) % n_sta) for t in range(n_sta)]
        pieces.append(lax.ppermute(mine, "sta", pairs))
    swap = [(t, t ^ 1) for t in range(n_sta)]
    pieces = jnp.stack(pieces)
    others = lax.ppermute(pieces, "sta", swap)
    rows_of_y = lax.rem(y - jnp.arange(n_y, dtype=jnp.int32) + n_y, n_y) * cores
    factor = math.sqrt(channels * L / (spread * stations))
    total = detect(rows_of_y + core, groups, block, pieces, None, own.shape[0], n_b, None)
    other = rows_of_y + 1 - core
    total = detect(other, groups, block, others, total, own.shape[0], n_b, factor)

    found = lax.all_to_all(total, "tm", 0, 0, axis_index_groups=near, tiled=True)
    return found.reshape(n_b * n_a, samples)


def solution(mesh):
    return jax.shard_map(
        on_device,
        mesh=mesh,
        in_specs=(P(None, "sta", "tm"), P(("tm", "sta"), None, None, None), P()),
        out_specs=P("sta", "tm"),
        check_vma=False,
    )
```

```python
import math

import jax
import jax.numpy as jnp
from jax import lax
from jax.experimental import pallas as pl
from jax.experimental.pallas import tpu as pltpu
from jax.sharding import PartitionSpec as P

L = 512
LANES = 128
HALF = 64
STEP = L + HALF
WIDTH = 3 * STEP + HALF
SLOTS = 4
epsilon = 1e-06


def detect_kernel(
    factor,
    order_ref,
    groups_ref,
    templates_ref,
    series_ref,
    before_ref,
    out_ref,
    source,
    home,
    count,
    wide,
    tails,
    waves,
    norms,
    band,
    shifts,
    energy,
    scales,
    windows,
    toeplitz,
    share,
    total,
    turned,
):
    block, spread = groups_ref.shape
    n_group = series_ref.shape[0]
    rows = total.shape[1]
    padded = rows + 8
    ahead = tails.shape[0] // n_group
    tail = L // LANES
    parts = 3 * L // LANES
    slots = wide.shape[0] // parts
    stations = slots // (block * spread)
    lane = lax.broadcasted_iota(jnp.int32, (1, LANES), 1)
    low = lane < HALF

    def clear(n, carry):
        source[n] = block * spread
        home[n] = block
        return carry

    lax.fori_loop(0, source.shape[0], clear, 0)
    for n in range(count.shape[0]):
        count[n] = 0
    for r in range(block):
        for i in range(spread):
            named = groups_ref[r, i]
            slot = named * SLOTS + count[named]
            source[slot] = r * spread + i
            home[slot] = r
            count[named] = count[named] + 1
    spare = waves.shape[0] - slots
    each = slots // block * parts
    for r in range(block):
        wide[r * each : (r + 1) * each, :] = templates_ref[r].astype(jnp.float32)
    for n in range(n_group):
        tails[n * ahead : (n + 1) * ahead, :] = series_ref[n, -ahead:, :].astype(jnp.float32)
    waves[...] = jnp.zeros_like(waves)
    for c in range(3):
        for v in range(L // LANES):
            at = c * STEP + v * LANES
            waves[0:slots, at : at + LANES] = wide[pl.ds(c * L // LANES + v, slots, parts), :]
    squares = jnp.sum(jnp.square(waves[0:slots, :]), axis=1, keepdims=True)
    norms[0:slots, :] = jnp.broadcast_to(lax.rsqrt(squares + epsilon), (slots, LANES))
    norms[slots:, :] = jnp.zeros((spare, LANES), jnp.float32)
    r = lax.broadcasted_iota(jnp.int32, (LANES, LANES), 0)
    l = lax.broadcasted_iota(jnp.int32, (LANES, LANES), 1)
    band[0:LANES, :] = jnp.where(r >= l, 1.0, 0.0).astype(jnp.bfloat16)
    band[LANES : 2 * LANES, :] = jnp.ones((LANES, LANES), jnp.bfloat16)
    band[2 * LANES :, :] = jnp.where(r < l, 1.0, 0.0).astype(jnp.bfloat16)
    shifts[:, :, rows:, :] = jnp.zeros((3, 2, 16, LANES), jnp.float32)
    if before_ref is None:
        total[...] = jnp.zeros_like(total)
    else:
        total[...] = before_ref[...]

    def prepare(group, station, buffer):
        squares = jnp.zeros((padded, LANES), jnp.float32)
        for c in range(3):
            line = c * stations + station
            main = series_ref[group, line * rows : (line + 1) * rows, :]
            shifts[c, 0, 0:rows, :] = main.astype(jnp.float32)
            at = group * ahead + line * tail
            shifts[c, 0, rows : rows + tail, :] = tails[pl.ds(at, tail), :]
            plain = shifts[c, 0, 0:padded, :]
            squares = squares + plain * plain
            after = shifts[c, 0, 1 : padded + 1, :]
            shifts[c, 1, 0:padded, :] = pltpu.roll(jnp.where(low, after, plain), HALF, 1)
        energy[...] = squares
        middle = energy[1 : rows + 1, :] + energy[2 : rows + 2, :] + energy[3 : rows + 3, :]
        pieces = jnp.concatenate([energy[0:rows, :], middle, energy[4 : rows + 4, :]], axis=1)
        coarse = pieces.astype(jnp.bfloat16)
        fine = (pieces - coarse.astype(jnp.float32)).astype(jnp.bfloat16)
        window_energy = jnp.dot(coarse, band[...], preferred_element_type=jnp.float32)
        window_energy += jnp.dot(fine, band[...], preferred_element_type=jnp.float32)
        scale = lax.rsqrt(window_energy + epsilon)
        other = pltpu.roll(scale, HALF, 1)
        scales[buffer, 0] = jnp.where(low, scale, other)
        scales[buffer, 1] = jnp.where(low, other, scale)
        for j in range(SLOTS):
            row = source[order_ref[group] * SLOTS + j] * stations + station
            wave = jnp.broadcast_to(waves[pl.ds(row, 1), :], (HALF, WIDTH))
            moved = pltpu.roll(wave, 0, 1, stride=1, stride_axis=0)
            toeplitz[buffer, j * HALF : (j + 1) * HALF, :] = moved.astype(jnp.bfloat16)
        for e in range(2):
            tiles = [shifts[0, e, v : v + rows, :] for v in range(tail)]
            if e:
                start = shifts[1, 0, 0:rows, :]
            else:
                start = pltpu.roll(shifts[1, 0, 0:rows, :], HALF, 1)
            tiles.append(jnp.where(low, shifts[0, e, tail : tail + rows, :], start))
            tiles += [shifts[1, 1 - e, v + e : v + e + rows, :] for v in range(tail)]
            tiles += [shifts[2, e, v : v + rows, :] for v in range(tail + 1)]
            for n, tile in enumerate(tiles):
                at = n * LANES
                windows[buffer, e * rows : (e + 1) * rows, at : at + LANES] = tile.astype(
                    jnp.bfloat16
                )

    def combine(group, station, buffer):
        weight = []
        for j in range(SLOTS):
            row = source[order_ref[group] * SLOTS + j] * stations + station
            weight.append(norms[pl.ds(row, 1), :])
        for p in range(SLOTS // 2):
            both = jnp.where(low, weight[2 * p], weight[2 * p + 1])
            at = p * LANES
            product = lax.dot_general(
                windows[buffer],
                toeplitz[buffer, at : at + LANES, :],
                (((1,), (1,)), ((), ())),
                preferred_element_type=jnp.float32,
            )
            for e in range(2):
                term = product[e * rows : (e + 1) * rows, :] * (scales[buffer, e] * both)
                if station:
                    term = term + share[e, :, at : at + LANES]
                share[e, :, at : at + LANES] = term

    def group_term(group, carry):
        later = lax.min(group + 1, n_group - 1)
        for station in range(stations):
            combine(group, station, station % 2)
            if station < stations - 1:
                prepare(group, station + 1, (station + 1) % 2)
            else:
                prepare(later, 0, (station + 1) % 2)
        for j in range(SLOTS):
            at = (j // 2) * LANES
            first = share[0, :, at : at + LANES]
            second = share[1, :, at : at + LANES]
            if j % 2 == 0:
                whole = jnp.where(low, first, pltpu.roll(second, HALF, 1))
            else:
                whole = jnp.where(low, pltpu.roll(first, HALF, 1), second)
            r = home[order_ref[group] * SLOTS + j]
            total[r] = total[r] + whole
        return carry

    prepare(0, 0, 0)
    lax.fori_loop(0, n_group, group_term, 0)
    if factor is None:
        out_ref[...] = total[...]
        return
    for r in range(block):
        turned[:, r, :] = total[r] * factor
    n_out, _, samples = out_ref.shape
    for w in range(n_out):
        for i in range(samples // LANES):
            out_ref[w, :, i * LANES : (i + 1) * LANES] = turned[w * (samples // LANES) + i]


def detect(order, groups, templates, series, before, parts, factor):
    n_all = templates.shape[0]
    block, spread = groups.shape
    stations = 4
    slots = block * spread * stations
    ahead = 3 * stations * L // LANES
    rows = (series.shape[1] - ahead) // (3 * stations)
    padded = rows + 8
    samples = rows * LANES // parts
    spare = -(-(slots + stations) // 8) * 8
    if factor is None:
        out_shape = jax.ShapeDtypeStruct((block + 1, rows, LANES), jnp.float32)
    else:
        out_shape = jax.ShapeDtypeStruct((parts, block, samples), jnp.float32)
    operands = [order, groups, templates, series]
    spaces = [pltpu.SMEM, pltpu.SMEM, pltpu.VMEM, pltpu.VMEM]
    if before is not None:
        operands.append(before)
        spaces.append(pltpu.VMEM)

    def body(*refs):
        refs = list(refs)
        if before is None:
            refs.insert(4, None)
        detect_kernel(factor, *refs)

    return pl.pallas_call(
        body,
        out_shape=out_shape,
        in_specs=[pl.BlockSpec(memory_space=space) for space in spaces],
        out_specs=pl.BlockSpec(memory_space=pltpu.VMEM),
        scratch_shapes=[
            pltpu.SMEM((n_all * SLOTS,), jnp.int32),
            pltpu.SMEM((n_all * SLOTS,), jnp.int32),
            pltpu.SMEM((n_all,), jnp.int32),
            pltpu.VMEM((slots * 3 * L // LANES, LANES), jnp.float32),
            pltpu.VMEM((series.shape[0] * ahead, LANES), jnp.float32),
            pltpu.VMEM((spare, WIDTH), jnp.float32),
            pltpu.VMEM((spare, LANES), jnp.float32),
            pltpu.VMEM((3 * LANES, LANES), jnp.bfloat16),
            pltpu.VMEM((3, 2, padded + 8, LANES), jnp.float32),
            pltpu.VMEM((padded, LANES), jnp.float32),
            pltpu.VMEM((2, 2, rows, LANES), jnp.float32),
            pltpu.VMEM((2, 2 * rows, WIDTH), jnp.bfloat16),
            pltpu.VMEM((2, SLOTS * HALF, WIDTH), jnp.bfloat16),
            pltpu.VMEM((2, rows, SLOTS * HALF), jnp.float32),
            pltpu.VMEM((block + 1, rows, LANES), jnp.float32),
            pltpu.VMEM((rows, block, LANES), jnp.float32),
        ],
        compiler_params=pltpu.CompilerParams(vmem_limit_bytes=32 * 1024 * 1024),
        cost_estimate=pl.CostEstimate(
            flops=16 * series.shape[0] * stations * 2 * rows * WIDTH * SLOTS * HALF,
            bytes_accessed=templates.size * 2 + 4 * block * rows * LANES,
            transcendentals=0,
        ),
    )(*operands)


def copies_to(value, axis, groups=None):
    count = len(groups[0]) if groups else lax.axis_size(axis)
    spread = jnp.broadcast_to(value[None], (count,) + value.shape)
    return lax.all_to_all(spread, axis, 0, 0, axis_index_groups=groups, tiled=True)


def on_device(record, templates, template_groups):
    channels, stations, samples = record.shape
    n_tm, n_sta = lax.axis_size("tm"), lax.axis_size("sta")
    m, s = lax.axis_index("tm"), lax.axis_index("sta")
    n_a = n_sta
    n_b = n_tm // n_a
    near = [[a * n_b + b for b in range(n_b)] for a in range(n_a)]
    far = [[a * n_b + b for a in range(n_a)] for b in range(n_b)]
    spread = template_groups.shape[1]

    first = (s * n_b + lax.rem(m, n_b)) * n_a
    groups = lax.dynamic_slice_in_dim(template_groups, first, n_a, 0)

    lines = channels * stations
    steps = samples // LANES
    half = n_b // 2
    four = [[i + j for j in range(half)] for i in range(0, n_tm, half)]
    same = lax.all_gather(record.reshape(lines * steps, LANES), "tm", axis_index_groups=four)
    other = lax.ppermute(same, "tm", [(i, i ^ half) for i in range(n_tm)])
    upper = lax.rem(m // half, 2) == 1
    around = jnp.concatenate([jnp.where(upper, other, same), jnp.where(upper, same, other)])
    own = templates.reshape(-1, LANES)
    front = around[0].reshape(lines, steps, LANES)[:, : L // LANES]
    tail = lax.ppermute(front, "tm", [(i + n_b, i) for i in range(n_tm - n_b)])
    block = copies_to(own, "tm", far)
    block = lax.all_to_all(block, "sta", 0, 0, tiled=True)
    tail, block = lax.optimization_barrier((tail, block))
    main = around.reshape(n_b, lines, steps, LANES)
    main = main.transpose(1, 0, 2, 3).reshape(-1, LANES)
    mine = jnp.concatenate([main, tail.reshape(-1, LANES)])

    cores = 2
    n_y = n_sta // cores
    y, core = s // cores, lax.rem(s, cores)
    pieces = [mine]
    for k in range(1, n_y):
        pairs = [(t, (t + k * cores) % n_sta) for t in range(n_sta)]
        pieces.append(lax.ppermute(mine, "sta", pairs))
    swap = [(t, t ^ 1) for t in range(n_sta)]
    pieces = jnp.stack(pieces)
    others = lax.ppermute(pieces, "sta", swap)
    rows_of_y = lax.rem(y - jnp.arange(n_y, dtype=jnp.int32) + n_y, n_y) * cores
    factor = math.sqrt(channels * L / (spread * stations))
    total = detect(rows_of_y + core, groups, block, pieces, None, n_b, None)
    other = rows_of_y + 1 - core
    total = detect(other, groups, block, others, total, n_b, factor)

    found = lax.all_to_all(total, "tm", 0, 0, axis_index_groups=near, tiled=True)
    return found.reshape(n_b * n_a, samples)


def solution(mesh):
    return jax.shard_map(
        on_device,
        mesh=mesh,
        in_specs=(P(None, "sta", "tm"), P(("tm", "sta"), None, None, None), P()),
        out_specs=P("sta", "tm"),
        check_vma=False,
    )
```

```python
import math

import jax
import jax.numpy as jnp
from jax import lax
from jax.experimental import pallas as pl
from jax.experimental.pallas import tpu as pltpu
from jax.sharding import PartitionSpec as P

L = 512
LANES = 128
HALF = 64
STEP = L + HALF
WIDTH = 3 * STEP + HALF
SLOTS = 4
epsilon = 1e-06


def detect_kernel(
    factor,
    order_ref,
    groups_ref,
    templates_ref,
    series_ref,
    before_ref,
    out_ref,
    source,
    home,
    count,
    wide,
    tails,
    waves,
    norms,
    band,
    shifts,
    energy,
    scales,
    windows,
    toeplitz,
    share,
    total,
    turned,
):
    block, spread = groups_ref.shape
    n_group = series_ref.shape[0]
    rows = total.shape[1]
    padded = rows + 8
    ahead = tails.shape[0] // n_group
    tail = L // LANES
    parts = 3 * L // LANES
    slots = wide.shape[0] // parts
    stations = slots // (block * spread)
    lane = lax.broadcasted_iota(jnp.int32, (1, LANES), 1)
    low = lane < HALF

    def clear(n, carry):
        source[n] = block * spread
        home[n] = block
        return carry

    lax.fori_loop(0, source.shape[0], clear, 0)
    for n in range(count.shape[0]):
        count[n] = 0
    for r in range(block):
        for i in range(spread):
            named = groups_ref[r, i]
            slot = named * SLOTS + count[named]
            source[slot] = r * spread + i
            home[slot] = r
            count[named] = count[named] + 1
    spare = waves.shape[0] - slots
    each = slots // block * parts
    for r in range(block):
        wide[r * each : (r + 1) * each, :] = templates_ref[r].astype(jnp.float32)
    for n in range(n_group):
        tails[n * ahead : (n + 1) * ahead, :] = series_ref[n, -ahead:, :].astype(jnp.float32)
    waves[...] = jnp.zeros_like(waves)
    for c in range(3):
        for v in range(L // LANES):
            at = c * STEP + v * LANES
            waves[0:slots, at : at + LANES] = wide[pl.ds(c * L // LANES + v, slots, parts), :]
    squares = jnp.sum(jnp.square(waves[0:slots, :]), axis=1, keepdims=True)
    norms[0:slots, :] = jnp.broadcast_to(lax.rsqrt(squares + epsilon), (slots, LANES))
    norms[slots:, :] = jnp.zeros((spare, LANES), jnp.float32)
    r = lax.broadcasted_iota(jnp.int32, (LANES, LANES), 0)
    l = lax.broadcasted_iota(jnp.int32, (LANES, LANES), 1)
    band[0:LANES, :] = jnp.where(r >= l, 1.0, 0.0).astype(jnp.bfloat16)
    band[LANES : 2 * LANES, :] = jnp.ones((LANES, LANES), jnp.bfloat16)
    band[2 * LANES :, :] = jnp.where(r < l, 1.0, 0.0).astype(jnp.bfloat16)
    shifts[:, :, rows:, :] = jnp.zeros((3, 2, 16, LANES), jnp.float32)
    if before_ref is None:
        total[...] = jnp.zeros_like(total)
    else:
        total[...] = before_ref[...]

    def prepare(group, station, buffer):
        squares = jnp.zeros((padded, LANES), jnp.float32)
        for c in range(3):
            line = c * stations + station
            main = series_ref[group, line * rows : (line + 1) * rows, :]
            shifts[c, 0, 0:rows, :] = main.astype(jnp.float32)
            at = group * ahead + line * tail
            shifts[c, 0, rows : rows + tail, :] = tails[pl.ds(at, tail), :]
            plain = shifts[c, 0, 0:padded, :]
            squares = squares + plain * plain
            after = shifts[c, 0, 1 : padded + 1, :]
            shifts[c, 1, 0:padded, :] = pltpu.roll(jnp.where(low, after, plain), HALF, 1)
        energy[...] = squares
        middle = energy[1 : rows + 1, :] + energy[2 : rows + 2, :] + energy[3 : rows + 3, :]
        pieces = jnp.concatenate([energy[0:rows, :], middle, energy[4 : rows + 4, :]], axis=1)
        coarse = pieces.astype(jnp.bfloat16)
        fine = (pieces - coarse.astype(jnp.float32)).astype(jnp.bfloat16)
        window_energy = jnp.dot(coarse, band[...], preferred_element_type=jnp.float32)
        window_energy += jnp.dot(fine, band[...], preferred_element_type=jnp.float32)
        scale = lax.rsqrt(window_energy + epsilon)
        other = pltpu.roll(scale, HALF, 1)
        scales[buffer, 0] = jnp.where(low, scale, other)
        scales[buffer, 1] = jnp.where(low, other, scale)
        for j in range(SLOTS):
            row = source[order_ref[group] * SLOTS + j] * stations + station
            wave = jnp.broadcast_to(waves[pl.ds(row, 1), :], (HALF, WIDTH))
            moved = pltpu.roll(wave, 0, 1, stride=1, stride_axis=0)
            toeplitz[buffer, j * HALF : (j + 1) * HALF, :] = moved.astype(jnp.bfloat16)
        for e in range(2):
            tiles = [shifts[0, e, v : v + rows, :] for v in range(tail)]
            if e:
                start = shifts[1, 0, 0:rows, :]
            else:
                start = pltpu.roll(shifts[1, 0, 0:rows, :], HALF, 1)
            tiles.append(jnp.where(low, shifts[0, e, tail : tail + rows, :], start))
            tiles += [shifts[1, 1 - e, v + e : v + e + rows, :] for v in range(tail)]
            tiles += [shifts[2, e, v : v + rows, :] for v in range(tail + 1)]
            for n, tile in enumerate(tiles):
                at = n * LANES
                windows[buffer, e * rows : (e + 1) * rows, at : at + LANES] = tile.astype(
                    jnp.bfloat16
                )

    def combine(group, station, buffer):
        weight = []
        for j in range(SLOTS):
            row = source[order_ref[group] * SLOTS + j] * stations + station
            weight.append(norms[pl.ds(row, 1), :])
        for p in range(SLOTS // 2):
            both = jnp.where(low, weight[2 * p], weight[2 * p + 1])
            at = p * LANES
            product = lax.dot_general(
                windows[buffer],
                toeplitz[buffer, at : at + LANES, :],
                (((1,), (1,)), ((), ())),
                preferred_element_type=jnp.float32,
            )
            for e in range(2):
                term = product[e * rows : (e + 1) * rows, :] * (scales[buffer, e] * both)
                if station:
                    term = term + share[e, :, at : at + LANES]
                share[e, :, at : at + LANES] = term

    def group_term(group, carry):
        later = lax.min(group + 1, n_group - 1)
        for station in range(stations):
            combine(group, station, station % 2)
            if station < stations - 1:
                prepare(group, station + 1, (station + 1) % 2)
            else:
                prepare(later, 0, (station + 1) % 2)
        for j in range(SLOTS):
            at = (j // 2) * LANES
            first = share[0, :, at : at + LANES]
            second = share[1, :, at : at + LANES]
            if j % 2 == 0:
                whole = jnp.where(low, first, pltpu.roll(second, HALF, 1))
            else:
                whole = jnp.where(low, pltpu.roll(first, HALF, 1), second)
            r = home[order_ref[group] * SLOTS + j]
            total[r] = total[r] + whole
        return carry

    prepare(0, 0, 0)
    lax.fori_loop(0, n_group, group_term, 0)
    if factor is None:
        out_ref[...] = total[...]
        return
    for r in range(block):
        turned[:, r, :] = total[r] * factor
    n_out, _, samples = out_ref.shape
    for w in range(n_out):
        for i in range(samples // LANES):
            out_ref[w, :, i * LANES : (i + 1) * LANES] = turned[w * (samples // LANES) + i]


def detect(order, groups, templates, series, before, parts, factor):
    n_all = templates.shape[0]
    block, spread = groups.shape
    stations = 4
    slots = block * spread * stations
    ahead = 3 * stations * L // LANES
    rows = (series.shape[1] - ahead) // (3 * stations)
    padded = rows + 8
    samples = rows * LANES // parts
    spare = -(-(slots + stations) // 8) * 8
    if factor is None:
        out_shape = jax.ShapeDtypeStruct((block + 1, rows, LANES), jnp.float32)
    else:
        out_shape = jax.ShapeDtypeStruct((parts, block, samples), jnp.float32)
    operands = [order, groups, templates, series]
    spaces = [pltpu.SMEM, pltpu.SMEM, pltpu.VMEM, pltpu.VMEM]
    if before is not None:
        operands.append(before)
        spaces.append(pltpu.VMEM)

    def body(*refs):
        refs = list(refs)
        if before is None:
            refs.insert(4, None)
        detect_kernel(factor, *refs)

    return pl.pallas_call(
        body,
        out_shape=out_shape,
        in_specs=[pl.BlockSpec(memory_space=space) for space in spaces],
        out_specs=pl.BlockSpec(memory_space=pltpu.VMEM),
        scratch_shapes=[
            pltpu.SMEM((n_all * SLOTS,), jnp.int32),
            pltpu.SMEM((n_all * SLOTS,), jnp.int32),
            pltpu.SMEM((n_all,), jnp.int32),
            pltpu.VMEM((slots * 3 * L // LANES, LANES), jnp.float32),
            pltpu.VMEM((series.shape[0] * ahead, LANES), jnp.float32),
            pltpu.VMEM((spare, WIDTH), jnp.float32),
            pltpu.VMEM((spare, LANES), jnp.float32),
            pltpu.VMEM((3 * LANES, LANES), jnp.bfloat16),
            pltpu.VMEM((3, 2, padded + 8, LANES), jnp.float32),
            pltpu.VMEM((padded, LANES), jnp.float32),
            pltpu.VMEM((2, 2, rows, LANES), jnp.float32),
            pltpu.VMEM((2, 2 * rows, WIDTH), jnp.bfloat16),
            pltpu.VMEM((2, SLOTS * HALF, WIDTH), jnp.bfloat16),
            pltpu.VMEM((2, rows, SLOTS * HALF), jnp.float32),
            pltpu.VMEM((block + 1, rows, LANES), jnp.float32),
            pltpu.VMEM((rows, block, LANES), jnp.float32),
        ],
        compiler_params=pltpu.CompilerParams(vmem_limit_bytes=32 * 1024 * 1024),
        cost_estimate=pl.CostEstimate(
            flops=16 * series.shape[0] * stations * 2 * rows * WIDTH * SLOTS * HALF,
            bytes_accessed=templates.size * 2 + 4 * block * rows * LANES,
            transcendentals=0,
        ),
    )(*operands)


def copies_to(value, axis, groups=None):
    count = len(groups[0]) if groups else lax.axis_size(axis)
    spread = jnp.broadcast_to(value[None], (count,) + value.shape)
    return lax.all_to_all(spread, axis, 0, 0, axis_index_groups=groups, tiled=True)


def on_device(record, templates, template_groups):
    channels, stations, samples = record.shape
    n_tm, n_sta = lax.axis_size("tm"), lax.axis_size("sta")
    m, s = lax.axis_index("tm"), lax.axis_index("sta")
    n_a = n_sta
    n_b = n_tm // n_a
    near = [[a * n_b + b for b in range(n_b)] for a in range(n_a)]
    far = [[a * n_b + b for a in range(n_a)] for b in range(n_b)]
    spread = template_groups.shape[1]

    first = (s * n_b + lax.rem(m, n_b)) * n_a
    groups = lax.dynamic_slice_in_dim(template_groups, first, n_a, 0)

    lines = channels * stations
    steps = samples // LANES
    half = n_b // 2
    four = [[i + j for j in range(half)] for i in range(0, n_tm, half)]
    head = lax.ppermute(record[:, :, :L], "tm", [(i + half, i) for i in range(n_tm - half)])
    piece = [record.reshape(lines * steps, LANES), head.reshape(-1, LANES)]
    four_pieces = lax.all_gather(jnp.concatenate(piece), "tm", axis_index_groups=four)
    same = four_pieces[:, : lines * steps].reshape(-1, LANES)
    next_head = four_pieces[0, lines * steps :]
    sent = jnp.concatenate([same, next_head])
    other = lax.ppermute(sent, "tm", [(i, i ^ half) for i in range(n_tm)])
    other, other_head = other[: same.shape[0]], other[same.shape[0] :]
    upper = lax.rem(m // half, 2) == 1
    around = jnp.concatenate([jnp.where(upper, other, same), jnp.where(upper, same, other)])
    tail = jnp.where(upper, next_head, other_head)
    own = templates.reshape(-1, LANES)
    block = copies_to(own, "tm", far)
    block = lax.all_to_all(block, "sta", 0, 0, tiled=True)
    main = around.reshape(n_b, lines, steps, LANES)
    main = main.transpose(1, 0, 2, 3).reshape(-1, LANES)
    mine = jnp.concatenate([main, tail])

    cores = 2
    n_y = n_sta // cores
    y, core = s // cores, lax.rem(s, cores)
    pieces = [mine]
    for k in range(1, n_y):
        pairs = [(t, (t + k * cores) % n_sta) for t in range(n_sta)]
        pieces.append(lax.ppermute(mine, "sta", pairs))
    swap = [(t, t ^ 1) for t in range(n_sta)]
    pieces = jnp.stack(pieces)
    others = lax.ppermute(pieces, "sta", swap)
    rows_of_y = lax.rem(y - jnp.arange(n_y, dtype=jnp.int32) + n_y, n_y) * cores
    factor = math.sqrt(channels * L / (spread * stations))
    total = detect(rows_of_y + core, groups, block, pieces, None, n_b, None)
    other = rows_of_y + 1 - core
    total = detect(other, groups, block, others, total, n_b, factor)

    found = lax.all_to_all(total, "tm", 0, 0, axis_index_groups=near, tiled=True)
    return found.reshape(n_b * n_a, samples)


def solution(mesh):
    return jax.shard_map(
        on_device,
        mesh=mesh,
        in_specs=(P(None, "sta", "tm"), P(("tm", "sta"), None, None, None), P()),
        out_specs=P("sta", "tm"),
        check_vma=False,
    )
```

```python
import math

import jax
import jax.numpy as jnp
from jax import lax
from jax.experimental import pallas as pl
from jax.experimental.pallas import tpu as pltpu
from jax.sharding import PartitionSpec as P

L = 512
LANES = 128
HALF = 64
STEP = L + HALF
WIDTH = 3 * STEP + HALF
SLOTS = 4
epsilon = 1e-06


def detect_kernel(
    factor,
    order_ref,
    groups_ref,
    templates_ref,
    series_ref,
    before_ref,
    out_ref,
    source,
    home,
    count,
    tails,
    waves,
    norms,
    band,
    shifts,
    energy,
    scales,
    windows,
    toeplitz,
    share,
    total,
    turned,
):
    block, spread = groups_ref.shape
    n_group = series_ref.shape[0]
    rows = total.shape[1]
    padded = rows + 8
    ahead = tails.shape[0] // n_group
    tail = L // LANES
    stations = templates_ref.shape[2]
    slots = block * spread * stations
    lane = lax.broadcasted_iota(jnp.int32, (1, LANES), 1)
    low = lane < HALF

    def clear(n, carry):
        source[n] = block * spread
        home[n] = block
        return carry

    lax.fori_loop(0, source.shape[0], clear, 0)
    for n in range(count.shape[0]):
        count[n] = 0
    for r in range(block):
        for i in range(spread):
            named = groups_ref[r, i]
            slot = named * SLOTS + count[named]
            source[slot] = r * spread + i
            home[slot] = r
            count[named] = count[named] + 1
    spare = waves.shape[0] - slots
    for n in range(n_group):
        tails[n * ahead : (n + 1) * ahead, :] = series_ref[n, -ahead:, :].astype(jnp.float32)
    waves[...] = jnp.zeros_like(waves)
    for n in range(block * spread):
        for c in range(3):
            part = templates_ref[n // spread, n % spread, :, c * L : (c + 1) * L]
            at = c * STEP
            waves[n * stations : (n + 1) * stations, at : at + L] = part.astype(jnp.float32)
    squares = jnp.sum(jnp.square(waves[0:slots, :]), axis=1, keepdims=True)
    norms[0:slots, :] = jnp.broadcast_to(lax.rsqrt(squares + epsilon), (slots, LANES))
    norms[slots:, :] = jnp.zeros((spare, LANES), jnp.float32)
    r = lax.broadcasted_iota(jnp.int32, (LANES, LANES), 0)
    l = lax.broadcasted_iota(jnp.int32, (LANES, LANES), 1)
    band[0:LANES, :] = jnp.where(r >= l, 1.0, 0.0).astype(jnp.bfloat16)
    band[LANES : 2 * LANES, :] = jnp.ones((LANES, LANES), jnp.bfloat16)
    band[2 * LANES :, :] = jnp.where(r < l, 1.0, 0.0).astype(jnp.bfloat16)
    shifts[:, :, rows:, :] = jnp.zeros((3, 2, 16, LANES), jnp.float32)
    if before_ref is None:
        total[...] = jnp.zeros_like(total)
    else:
        total[...] = before_ref[...]

    def prepare(group, station, buffer):
        squares = jnp.zeros((padded, LANES), jnp.float32)
        for c in range(3):
            line = c * stations + station
            main = series_ref[group, line * rows : (line + 1) * rows, :]
            shifts[c, 0, 0:rows, :] = main.astype(jnp.float32)
            at = group * ahead + line * tail
            shifts[c, 0, rows : rows + tail, :] = tails[pl.ds(at, tail), :]
            plain = shifts[c, 0, 0:padded, :]
            squares = squares + plain * plain
            after = shifts[c, 0, 1 : padded + 1, :]
            shifts[c, 1, 0:padded, :] = pltpu.roll(jnp.where(low, after, plain), HALF, 1)
        energy[...] = squares
        middle = energy[1 : rows + 1, :] + energy[2 : rows + 2, :] + energy[3 : rows + 3, :]
        pieces = jnp.concatenate([energy[0:rows, :], middle, energy[4 : rows + 4, :]], axis=1)
        coarse = pieces.astype(jnp.bfloat16)
        fine = (pieces - coarse.astype(jnp.float32)).astype(jnp.bfloat16)
        window_energy = jnp.dot(coarse, band[...], preferred_element_type=jnp.float32)
        window_energy += jnp.dot(fine, band[...], preferred_element_type=jnp.float32)
        scale = lax.rsqrt(window_energy + epsilon)
        other = pltpu.roll(scale, HALF, 1)
        scales[buffer, 0] = jnp.where(low, scale, other)
        scales[buffer, 1] = jnp.where(low, other, scale)
        for j in range(SLOTS):
            row = source[order_ref[group] * SLOTS + j] * stations + station
            wave = jnp.broadcast_to(waves[pl.ds(row, 1), :], (HALF, WIDTH))
            moved = pltpu.roll(wave, 0, 1, stride=1, stride_axis=0)
            toeplitz[buffer, j * HALF : (j + 1) * HALF, :] = moved.astype(jnp.bfloat16)
        for e in range(2):
            tiles = [shifts[0, e, v : v + rows, :] for v in range(tail)]
            if e:
                start = shifts[1, 0, 0:rows, :]
            else:
                start = pltpu.roll(shifts[1, 0, 0:rows, :], HALF, 1)
            tiles.append(jnp.where(low, shifts[0, e, tail : tail + rows, :], start))
            tiles += [shifts[1, 1 - e, v + e : v + e + rows, :] for v in range(tail)]
            tiles += [shifts[2, e, v : v + rows, :] for v in range(tail + 1)]
            for n, tile in enumerate(tiles):
                at = n * LANES
                windows[buffer, e * rows : (e + 1) * rows, at : at + LANES] = tile.astype(
                    jnp.bfloat16
                )

    def combine(group, station, buffer):
        weight = []
        for j in range(SLOTS):
            row = source[order_ref[group] * SLOTS + j] * stations + station
            weight.append(norms[pl.ds(row, 1), :])
        for p in range(SLOTS // 2):
            both = jnp.where(low, weight[2 * p], weight[2 * p + 1])
            at = p * LANES
            product = lax.dot_general(
                windows[buffer],
                toeplitz[buffer, at : at + LANES, :],
                (((1,), (1,)), ((), ())),
                preferred_element_type=jnp.float32,
            )
            for e in range(2):
                term = product[e * rows : (e + 1) * rows, :] * (scales[buffer, e] * both)
                if station:
                    term = term + share[e, :, at : at + LANES]
                share[e, :, at : at + LANES] = term

    def group_term(group, carry):
        later = lax.min(group + 1, n_group - 1)
        for station in range(stations):
            combine(group, station, station % 2)
            if station < stations - 1:
                prepare(group, station + 1, (station + 1) % 2)
            else:
                prepare(later, 0, (station + 1) % 2)
        for j in range(SLOTS):
            at = (j // 2) * LANES
            first = share[0, :, at : at + LANES]
            second = share[1, :, at : at + LANES]
            if j % 2 == 0:
                whole = jnp.where(low, first, pltpu.roll(second, HALF, 1))
            else:
                whole = jnp.where(low, pltpu.roll(first, HALF, 1), second)
            r = home[order_ref[group] * SLOTS + j]
            total[r] = total[r] + whole
        return carry

    prepare(0, 0, 0)
    lax.fori_loop(0, n_group, group_term, 0)
    if factor is None:
        out_ref[...] = total[...]
        return
    for r in range(block):
        turned[:, r, :] = total[r] * factor
    n_out, _, samples = out_ref.shape
    for w in range(n_out):
        for i in range(samples // LANES):
            out_ref[w, :, i * LANES : (i + 1) * LANES] = turned[w * (samples // LANES) + i]


def detect(order, groups, templates, series, before, parts, factor):
    n_all = templates.shape[0]
    block, spread = groups.shape
    stations = 4
    slots = block * spread * stations
    ahead = 3 * stations * L // LANES
    rows = (series.shape[1] - ahead) // (3 * stations)
    padded = rows + 8
    samples = rows * LANES // parts
    spare = -(-(slots + stations) // 8) * 8
    if factor is None:
        out_shape = jax.ShapeDtypeStruct((block + 1, rows, LANES), jnp.float32)
    else:
        out_shape = jax.ShapeDtypeStruct((parts, block, samples), jnp.float32)
    operands = [order, groups, templates, series]
    spaces = [pltpu.SMEM, pltpu.SMEM, pltpu.VMEM, pltpu.VMEM]
    if before is not None:
        operands.append(before)
        spaces.append(pltpu.VMEM)

    def body(*refs):
        refs = list(refs)
        if before is None:
            refs.insert(4, None)
        detect_kernel(factor, *refs)

    return pl.pallas_call(
        body,
        out_shape=out_shape,
        in_specs=[pl.BlockSpec(memory_space=space) for space in spaces],
        out_specs=pl.BlockSpec(memory_space=pltpu.VMEM),
        scratch_shapes=[
            pltpu.SMEM((n_all * SLOTS,), jnp.int32),
            pltpu.SMEM((n_all * SLOTS,), jnp.int32),
            pltpu.SMEM((n_all,), jnp.int32),
            pltpu.VMEM((series.shape[0] * ahead, LANES), jnp.float32),
            pltpu.VMEM((spare, WIDTH), jnp.float32),
            pltpu.VMEM((spare, LANES), jnp.float32),
            pltpu.VMEM((3 * LANES, LANES), jnp.bfloat16),
            pltpu.VMEM((3, 2, padded + 8, LANES), jnp.float32),
            pltpu.VMEM((padded, LANES), jnp.float32),
            pltpu.VMEM((2, 2, rows, LANES), jnp.float32),
            pltpu.VMEM((2, 2 * rows, WIDTH), jnp.bfloat16),
            pltpu.VMEM((2, SLOTS * HALF, WIDTH), jnp.bfloat16),
            pltpu.VMEM((2, rows, SLOTS * HALF), jnp.float32),
            pltpu.VMEM((block + 1, rows, LANES), jnp.float32),
            pltpu.VMEM((rows, block, LANES), jnp.float32),
        ],
        compiler_params=pltpu.CompilerParams(vmem_limit_bytes=32 * 1024 * 1024),
        cost_estimate=pl.CostEstimate(
            flops=16 * series.shape[0] * stations * 2 * rows * WIDTH * SLOTS * HALF,
            bytes_accessed=templates.size * 2 + 4 * block * rows * LANES,
            transcendentals=0,
        ),
    )(*operands)


def copies_to(value, axis, groups=None):
    count = len(groups[0]) if groups else lax.axis_size(axis)
    spread = jnp.broadcast_to(value[None], (count,) + value.shape)
    return lax.all_to_all(spread, axis, 0, 0, axis_index_groups=groups, tiled=True)


def on_device(record, templates, template_groups):
    channels, stations, samples = record.shape
    n_tm, n_sta = lax.axis_size("tm"), lax.axis_size("sta")
    m, s = lax.axis_index("tm"), lax.axis_index("sta")
    n_a = n_sta
    n_b = n_tm // n_a
    near = [[a * n_b + b for b in range(n_b)] for a in range(n_a)]
    far = [[a * n_b + b for a in range(n_a)] for b in range(n_b)]
    spread = template_groups.shape[1]

    first = (s * n_b + lax.rem(m, n_b)) * n_a
    groups = lax.dynamic_slice_in_dim(template_groups, first, n_a, 0)

    lines = channels * stations
    steps = samples // LANES
    half = n_b // 2
    four = [[i + j for j in range(half)] for i in range(0, n_tm, half)]
    head = lax.ppermute(record, "tm", [(i + half, i) for i in range(n_tm - half)])
    piece = [record.reshape(lines * steps, LANES), head[:, :, :L].reshape(-1, LANES)]
    four_pieces = lax.all_gather(jnp.concatenate(piece), "tm", axis_index_groups=four)
    same = four_pieces[:, : lines * steps].reshape(-1, LANES)
    next_head = four_pieces[0, lines * steps :]
    sent = jnp.concatenate([same, next_head])
    other = lax.ppermute(sent, "tm", [(i, i ^ half) for i in range(n_tm)])
    other, other_head = other[: same.shape[0]], other[same.shape[0] :]
    upper = lax.rem(m // half, 2) == 1
    around = jnp.concatenate([jnp.where(upper, other, same), jnp.where(upper, same, other)])
    tail = jnp.where(upper, next_head, other_head)
    own = templates[0]
    block = copies_to(own, "tm", far)
    block = lax.all_to_all(block, "sta", 0, 0, tiled=True)
    main = around.reshape(n_b, lines, steps, LANES)
    main = main.transpose(1, 0, 2, 3).reshape(-1, LANES)
    mine = jnp.concatenate([main, tail])

    cores = 2
    n_y = n_sta // cores
    y, core = s // cores, lax.rem(s, cores)
    pieces = [mine]
    for k in range(1, n_y):
        pairs = [(t, (t + k * cores) % n_sta) for t in range(n_sta)]
        pieces.append(lax.ppermute(mine, "sta", pairs))
    swap = [(t, t ^ 1) for t in range(n_sta)]
    pieces = jnp.stack(pieces)
    others = lax.ppermute(pieces, "sta", swap)
    rows_of_y = lax.rem(y - jnp.arange(n_y, dtype=jnp.int32) + n_y, n_y) * cores
    factor = math.sqrt(channels * L / (spread * stations))
    total = detect(rows_of_y + core, groups, block, pieces, None, n_b, None)
    other = rows_of_y + 1 - core
    total = detect(other, groups, block, others, total, n_b, factor)

    found = lax.all_to_all(total, "tm", 0, 0, axis_index_groups=near, tiled=True)
    return found.reshape(n_b * n_a, samples)


def solution(mesh):
    return jax.shard_map(
        on_device,
        mesh=mesh,
        in_specs=(P(None, "sta", "tm"), P(("tm", "sta"), None, None, None), P()),
        out_specs=P("sta", "tm"),
        check_vma=False,
    )
```

```python
import math

import jax
import jax.numpy as jnp
from jax import lax
from jax.experimental import pallas as pl
from jax.experimental.pallas import tpu as pltpu
from jax.sharding import PartitionSpec as P

L = 512
LANES = 128
HALF = 64
STEP = L + HALF
WIDTH = 3 * STEP + HALF
SLOTS = 4
epsilon = 1e-06


def detect_kernel(
    each,
    factor,
    order_ref,
    groups_ref,
    templates_ref,
    series_ref,
    before_ref,
    out_ref,
    source,
    home,
    count,
    wide,
    tails,
    waves,
    norms,
    band,
    shifts,
    energy,
    scales,
    windows,
    toeplitz,
    share,
    total,
    turned,
):
    block, spread = groups_ref.shape
    n_group = series_ref.shape[0]
    rows = total.shape[1]
    padded = rows + 8
    ahead = tails.shape[0] // templates_ref.shape[0]
    tail = L // LANES
    parts = 3 * L // LANES
    slots = wide.shape[0] // parts
    stations = slots // (block * spread)
    lane = lax.broadcasted_iota(jnp.int32, (1, LANES), 1)
    low = lane < HALF

    def clear(n, carry):
        source[n] = block * spread
        home[n] = block
        return carry

    lax.fori_loop(0, source.shape[0], clear, 0)
    for n in range(count.shape[0]):
        count[n] = 0
    for r in range(block):
        for i in range(spread):
            named = groups_ref[r, i]
            slot = named * SLOTS + count[named]
            source[slot] = r * spread + i
            home[slot] = r
            count[named] = count[named] + 1
    spare = waves.shape[0] - slots
    for r in range(block):
        wide[r * each : (r + 1) * each, :] = templates_ref[r, 0:each, :].astype(jnp.float32)
    for n in range(templates_ref.shape[0]):
        tails[n * ahead : (n + 1) * ahead, :] = templates_ref[n, each:, :].astype(jnp.float32)
    waves[...] = jnp.zeros_like(waves)
    for c in range(3):
        for v in range(L // LANES):
            at = c * STEP + v * LANES
            waves[0:slots, at : at + LANES] = wide[pl.ds(c * L // LANES + v, slots, parts), :]
    squares = jnp.sum(jnp.square(waves[0:slots, :]), axis=1, keepdims=True)
    norms[0:slots, :] = jnp.broadcast_to(lax.rsqrt(squares + epsilon), (slots, LANES))
    norms[slots:, :] = jnp.zeros((spare, LANES), jnp.float32)
    r = lax.broadcasted_iota(jnp.int32, (LANES, LANES), 0)
    l = lax.broadcasted_iota(jnp.int32, (LANES, LANES), 1)
    band[0:LANES, :] = jnp.where(r >= l, 1.0, 0.0).astype(jnp.bfloat16)
    band[LANES : 2 * LANES, :] = jnp.ones((LANES, LANES), jnp.bfloat16)
    band[2 * LANES :, :] = jnp.where(r < l, 1.0, 0.0).astype(jnp.bfloat16)
    shifts[:, :, rows:, :] = jnp.zeros((3, 2, 16, LANES), jnp.float32)
    if before_ref is None:
        total[...] = jnp.zeros_like(total)
    else:
        total[...] = before_ref[...]

    def prepare(group, station, buffer):
        squares = jnp.zeros((padded, LANES), jnp.float32)
        for c in range(3):
            line = c * stations + station
            main = series_ref[group, line * rows : (line + 1) * rows, :]
            shifts[c, 0, 0:rows, :] = main.astype(jnp.float32)
            at = order_ref[group] * ahead + line * tail
            shifts[c, 0, rows : rows + tail, :] = tails[pl.ds(at, tail), :]
            plain = shifts[c, 0, 0:padded, :]
            squares = squares + plain * plain
            after = shifts[c, 0, 1 : padded + 1, :]
            shifts[c, 1, 0:padded, :] = pltpu.roll(jnp.where(low, after, plain), HALF, 1)
        energy[...] = squares
        middle = energy[1 : rows + 1, :] + energy[2 : rows + 2, :] + energy[3 : rows + 3, :]
        pieces = jnp.concatenate([energy[0:rows, :], middle, energy[4 : rows + 4, :]], axis=1)
        coarse = pieces.astype(jnp.bfloat16)
        fine = (pieces - coarse.astype(jnp.float32)).astype(jnp.bfloat16)
        window_energy = jnp.dot(coarse, band[...], preferred_element_type=jnp.float32)
        window_energy += jnp.dot(fine, band[...], preferred_element_type=jnp.float32)
        scale = lax.rsqrt(window_energy + epsilon)
        other = pltpu.roll(scale, HALF, 1)
        scales[buffer, 0] = jnp.where(low, scale, other)
        scales[buffer, 1] = jnp.where(low, other, scale)
        for j in range(SLOTS):
            row = source[order_ref[group] * SLOTS + j] * stations + station
            wave = jnp.broadcast_to(waves[pl.ds(row, 1), :], (HALF, WIDTH))
            moved = pltpu.roll(wave, 0, 1, stride=1, stride_axis=0)
            toeplitz[buffer, j * HALF : (j + 1) * HALF, :] = moved.astype(jnp.bfloat16)
        for e in range(2):
            tiles = [shifts[0, e, v : v + rows, :] for v in range(tail)]
            if e:
                start = shifts[1, 0, 0:rows, :]
            else:
                start = pltpu.roll(shifts[1, 0, 0:rows, :], HALF, 1)
            tiles.append(jnp.where(low, shifts[0, e, tail : tail + rows, :], start))
            tiles += [shifts[1, 1 - e, v + e : v + e + rows, :] for v in range(tail)]
            tiles += [shifts[2, e, v : v + rows, :] for v in range(tail + 1)]
            for n, tile in enumerate(tiles):
                at = n * LANES
                windows[buffer, e * rows : (e + 1) * rows, at : at + LANES] = tile.astype(
                    jnp.bfloat16
                )

    def combine(group, station, buffer):
        weight = []
        for j in range(SLOTS):
            row = source[order_ref[group] * SLOTS + j] * stations + station
            weight.append(norms[pl.ds(row, 1), :])
        for p in range(SLOTS // 2):
            both = jnp.where(low, weight[2 * p], weight[2 * p + 1])
            at = p * LANES
            product = lax.dot_general(
                windows[buffer],
                toeplitz[buffer, at : at + LANES, :],
                (((1,), (1,)), ((), ())),
                preferred_element_type=jnp.float32,
            )
            for e in range(2):
                term = product[e * rows : (e + 1) * rows, :] * (scales[buffer, e] * both)
                if station:
                    term = term + share[e, :, at : at + LANES]
                share[e, :, at : at + LANES] = term

    def group_term(group, carry):
        later = lax.min(group + 1, n_group - 1)
        for station in range(stations):
            combine(group, station, station % 2)
            if station < stations - 1:
                prepare(group, station + 1, (station + 1) % 2)
            else:
                prepare(later, 0, (station + 1) % 2)
        for j in range(SLOTS):
            at = (j // 2) * LANES
            first = share[0, :, at : at + LANES]
            second = share[1, :, at : at + LANES]
            if j % 2 == 0:
                whole = jnp.where(low, first, pltpu.roll(second, HALF, 1))
            else:
                whole = jnp.where(low, pltpu.roll(first, HALF, 1), second)
            r = home[order_ref[group] * SLOTS + j]
            total[r] = total[r] + whole
        return carry

    prepare(0, 0, 0)
    lax.fori_loop(0, n_group, group_term, 0)
    if factor is None:
        out_ref[...] = total[...]
        return
    for r in range(block):
        turned[:, r, :] = total[r] * factor
    n_out, _, samples = out_ref.shape
    for w in range(n_out):
        for i in range(samples // LANES):
            out_ref[w, :, i * LANES : (i + 1) * LANES] = turned[w * (samples // LANES) + i]


def detect(order, groups, templates, series, before, each, parts, factor):
    n_all = templates.shape[0]
    block, spread = groups.shape
    stations = 4
    slots = block * spread * stations
    rows = series.shape[1] // (3 * stations)
    padded = rows + 8
    samples = rows * LANES // parts
    spare = -(-(slots + stations) // 8) * 8
    if factor is None:
        out_shape = jax.ShapeDtypeStruct((block + 1, rows, LANES), jnp.float32)
    else:
        out_shape = jax.ShapeDtypeStruct((parts, block, samples), jnp.float32)
    operands = [order, groups, templates, series]
    spaces = [pltpu.SMEM, pltpu.SMEM, pltpu.VMEM, pltpu.VMEM]
    if before is not None:
        operands.append(before)
        spaces.append(pltpu.VMEM)

    def body(*refs):
        refs = list(refs)
        if before is None:
            refs.insert(4, None)
        detect_kernel(each, factor, *refs)

    return pl.pallas_call(
        body,
        out_shape=out_shape,
        in_specs=[pl.BlockSpec(memory_space=space) for space in spaces],
        out_specs=pl.BlockSpec(memory_space=pltpu.VMEM),
        scratch_shapes=[
            pltpu.SMEM((n_all * SLOTS,), jnp.int32),
            pltpu.SMEM((n_all * SLOTS,), jnp.int32),
            pltpu.SMEM((n_all,), jnp.int32),
            pltpu.VMEM((slots * 3 * L // LANES, LANES), jnp.float32),
            pltpu.VMEM((n_all * (templates.shape[1] - each), LANES), jnp.float32),
            pltpu.VMEM((spare, WIDTH), jnp.float32),
            pltpu.VMEM((spare, LANES), jnp.float32),
            pltpu.VMEM((3 * LANES, LANES), jnp.bfloat16),
            pltpu.VMEM((3, 2, padded + 8, LANES), jnp.float32),
            pltpu.VMEM((padded, LANES), jnp.float32),
            pltpu.VMEM((2, 2, rows, LANES), jnp.float32),
            pltpu.VMEM((2, 2 * rows, WIDTH), jnp.bfloat16),
            pltpu.VMEM((2, SLOTS * HALF, WIDTH), jnp.bfloat16),
            pltpu.VMEM((2, rows, SLOTS * HALF), jnp.float32),
            pltpu.VMEM((block + 1, rows, LANES), jnp.float32),
            pltpu.VMEM((rows, block, LANES), jnp.float32),
        ],
        compiler_params=pltpu.CompilerParams(vmem_limit_bytes=32 * 1024 * 1024),
        cost_estimate=pl.CostEstimate(
            flops=16 * series.shape[0] * stations * 2 * rows * WIDTH * SLOTS * HALF,
            bytes_accessed=templates.size * 2 + 4 * block * rows * LANES,
            transcendentals=0,
        ),
    )(*operands)


def copies_to(value, axis, groups=None):
    count = len(groups[0]) if groups else lax.axis_size(axis)
    spread = jnp.broadcast_to(value[None], (count,) + value.shape)
    return lax.all_to_all(spread, axis, 0, 0, axis_index_groups=groups, tiled=True)


def on_device(record, templates, template_groups):
    channels, stations, samples = record.shape
    n_tm, n_sta = lax.axis_size("tm"), lax.axis_size("sta")
    m, s = lax.axis_index("tm"), lax.axis_index("sta")
    n_a = n_sta
    n_b = n_tm // n_a
    near = [[a * n_b + b for b in range(n_b)] for a in range(n_a)]
    far = [[a * n_b + b for a in range(n_a)] for b in range(n_b)]
    spread = template_groups.shape[1]

    first = (s * n_b + lax.rem(m, n_b)) * n_a
    groups = lax.dynamic_slice_in_dim(template_groups, first, n_a, 0)

    lines = channels * stations
    steps = samples // LANES
    half = n_b // 2
    four = [[i + j for j in range(half)] for i in range(0, n_tm, half)]
    same = lax.all_gather(record.reshape(lines * steps, LANES), "tm", axis_index_groups=four)
    other = lax.ppermute(same, "tm", [(i, i ^ half) for i in range(n_tm)])
    upper = lax.rem(m // half, 2) == 1
    around = jnp.concatenate([jnp.where(upper, other, same), jnp.where(upper, same, other)])
    own = templates.reshape(-1, LANES)
    front = around[0].reshape(lines, steps, LANES)[:, : L // LANES]
    tail = lax.ppermute(front, "tm", [(i + n_b, i) for i in range(n_tm - n_b)])
    tail = jnp.broadcast_to(tail.reshape(1, -1, LANES), (n_sta, lines * L // LANES, LANES))
    block = copies_to(own, "tm", far)
    block = lax.all_to_all(jnp.concatenate([block, tail], axis=1), "sta", 0, 0, tiled=True)
    main = around.reshape(n_b, lines, steps, LANES)
    mine = main.transpose(1, 0, 2, 3).reshape(-1, LANES)

    cores = 2
    n_y = n_sta // cores
    y, core = s // cores, lax.rem(s, cores)
    pieces = [mine]
    turns = [0, 1, 3, 2]
    for k in turns[1:]:
        pairs = [(t, (t + k * cores) % n_sta) for t in range(n_sta)]
        pieces.append(lax.ppermute(mine, "sta", pairs))
    swap = [(t, t ^ 1) for t in range(n_sta)]
    pieces = jnp.stack(pieces)
    others = lax.ppermute(pieces, "sta", swap)
    rows_of_y = lax.rem(y - jnp.array(turns, jnp.int32) + n_y, n_y) * cores
    factor = math.sqrt(channels * L / (spread * stations))
    total = detect(rows_of_y + core, groups, block, pieces, None, own.shape[0], n_b, None)
    other = rows_of_y + 1 - core
    total = detect(other, groups, block, others, total, own.shape[0], n_b, factor)

    found = lax.all_to_all(total, "tm", 0, 0, axis_index_groups=near, tiled=True)
    return found.reshape(n_b * n_a, samples)


def solution(mesh):
    return jax.shard_map(
        on_device,
        mesh=mesh,
        in_specs=(P(None, "sta", "tm"), P(("tm", "sta"), None, None, None), P()),
        out_specs=P("sta", "tm"),
        check_vma=False,
    )
```
